128 devices in a mesh: rep: 16 (over y, z_hi, core), shard: 8 (over x, z_lo).
Axes of the slice: x: 4, y: 4, z: 4 (z_hi: 2, z_lo: 2; z = z_hi * 2 + z_lo), core: 2. Of those that a mesh axis runs over, the one named last changes fastest.
Arguments:
- tokens: bfloat16 [16384, 2048], P(('rep', 'shard')), may hold values from -6 to 6
- out_cotangent: bfloat16 [16384, 2048], P(('rep', 'shard')), may hold values from -6 to 6
- attend_weight: bfloat16 [2048, 6144], P('shard'), may hold values from -0.125 to 0.125
- attend_bias: bfloat16 [6144], P('shard'), may hold values from -3 to 3
- dense_weight: bfloat16 [2048, 2048], P('shard'), may hold values from -0.75 to 0.75
- dense_bias: bfloat16 [2048], P('shard'), may hold values from -3 to 3
- expand_weight: bfloat16 [2048, 8192], P('shard'), may hold values from -0.125 to 0.125
- expand_bias: bfloat16 [8192], P('shard'), may hold values from -3 to 3
- shrink_weight: bfloat16 [8192, 2048], P('shard'), may hold values from -0.0625 to 0.0625
- shrink_bias: bfloat16 [2048], P('shard'), may hold values from -3 to 3
- attend_gain: bfloat16 [2048], P('shard'), may hold values from 0.25 to 1.75
- attend_shift: bfloat16 [2048], P('shard'), may hold values from -3 to 3
- feed_gain: bfloat16 [2048], P('shard'), may hold values from 0.25 to 1.75
- feed_shift: bfloat16 [2048], P('shard'), may hold values from -3 to 3
- lengths: int32 [16, 4], P('rep'), may hold values from 85 to 512, as said below
- slot_source: int32 [16, 1024], P('rep'), may hold values from 0 to 1023, as said below
Outputs:
- layer_out: bfloat16 [16384, 2048], P(('rep', 'shard'))
- tokens_gradient: float32 [16384, 2048], P(('rep', 'shard'))
- attend_weight_gradient: float32 [2048, 6144], P('shard')
- attend_bias_gradient: float32 [6144], P('shard')
- dense_weight_gradient: float32 [2048, 2048], P('shard')
- dense_bias_gradient: float32 [2048], P('shard')
- expand_weight_gradient: float32 [2048, 8192], P('shard')
- expand_bias_gradient: float32 [8192], P('shard')
- shrink_weight_gradient: float32 [8192, 2048], P('shard')
- shrink_bias_gradient: float32 [2048], P('shard')
- attend_gain_gradient: float32 [2048], P('shard')
- attend_shift_gradient: float32 [2048], P('shard')
- feed_gain_gradient: float32 [2048], P('shard')
- feed_shift_gradient: float32 [2048], P('shard')
The draws below stay inside these ranges and needn't reach their ends.
Inputs may be any that keep to these rules, and one draw needn't show every extreme that they name: `lengths`: each row sums to 1024; the first sequence of every group has 512 tokens. `slot_source`: each row is a permutation of the group's packed indices; each row's slots are spread over the group's devices, 128 to a device.
All inputs are finite; a program needn't handle non-finite values.
Results may differ from the reference program's by a relative error of at most 0.024.
Values may be sent and summed in bfloat16 or wider, within the bound.
A program may use at most 448 MiB of HBM per device.

```python
import jax
import jax.numpy as jnp
from jax import lax

D = 2048
H = 8
HD = 256
FF = 8192
ROT = 64
TOK_DEV = 128
GROUPS = 16
GROUP_TOK = 1024
TOKENS = 16384
MAXLEN = 512
NSEQ = 4


def draw_lengths(key, part):
    key = jax.random.fold_in(key, 1)
    others = NSEQ - 1
    spare = GROUP_TOK - MAXLEN
    even_share = spare // others
    leftover = spare - even_share * others
    paired = others // 2
    reach = even_share // 2
    delta_key, order_key = jax.random.split(key)
    deltas = jax.random.randint(delta_key, (GROUPS, paired), -reach, reach + 1)
    deltas = deltas.at[0, 0].set(-reach)
    spread = jnp.zeros((GROUPS, others), jnp.int32)
    spread = spread.at[:, 0:2 * paired:2].add(deltas)
    spread = spread.at[:, 1:2 * paired:2].add(-deltas)
    parts_all = even_share + spread
    parts_all = parts_all.at[:, 0].add(leftover)
    shuffle_keys = jax.random.split(order_key, GROUPS)
    orders = jax.vmap(lambda one_key: jax.random.permutation(one_key, others))(shuffle_keys)
    parts_all = jnp.take_along_axis(parts_all, orders, axis=1)
    first = jnp.full((GROUPS, 1), MAXLEN, jnp.int32)
    return jnp.concatenate([first, parts_all], axis=1).astype(jnp.int32)


def draw_slot_source(key, part):
    key = jax.random.fold_in(key, 2)
    shard_count = GROUP_TOK // TOK_DEV

    def one_group(group_key):
        head_key, tail_key, mix_key = jax.random.split(group_key, 3)
        leading = jax.random.permutation(head_key, shard_count)
        remains = jax.random.permutation(tail_key, GROUP_TOK - shard_count) + shard_count
        table = jnp.concatenate([leading[:, None], remains.reshape(shard_count, TOK_DEV - 1)], axis=1)
        mixes = jax.vmap(lambda row_key: jax.random.permutation(row_key, TOK_DEV))(jax.random.split(mix_key, shard_count))
        return jnp.take_along_axis(table, mixes, axis=1).reshape(GROUP_TOK)
    return jax.vmap(one_group)(jax.random.split(key, GROUPS)).astype(jnp.int32)


def block_scale(own_key, extent, cuts, smallest, top_value):
    level, own = 1.0, jax.random.fold_in(own_key, 6)
    for position, blocks in cuts:
        draws = jnp.exp(jax.random.uniform(jax.random.fold_in(own, position), (blocks,), jnp.float32, smallest / len(cuts), top_value / len(cuts)))
        level = level * jnp.repeat(draws, extent[position] // blocks).reshape([-1 if axis == position else 1 for axis in range(len(extent))])
    return level


def normal_values(rng, shape, deviation, bound, shards=(), kind=jnp.bfloat16):
    result = deviation * jax.random.normal(rng, shape, jnp.float32)
    if shards:
        result = result * block_scale(rng, shape, shards, -0.22, 0.18)
    return jnp.clip(result, -bound, bound).astype(kind)


def setup_inputs(seed: int = 0) -> dict:
    key_list = jax.random.split(jax.random.key(seed), 17)
    tokens = normal_values(key_list[0], (TOKENS, D), 1.0, 6.0, ((0, 128),))
    out_cotangent = normal_values(key_list[1], (TOKENS, D), 1.0, 6.0, ((0, 128),))
    attend_weight = normal_values(key_list[2], (D, 3 * D), D ** -0.5, 0.125, ((0, 8),))
    attend_bias = normal_values(key_list[3], (3 * D,), 0.5, 3.0, ((0, 8),))
    dense_weight = normal_values(key_list[4], (D, D), (D // 32) ** -0.5, 0.75, ((0, 8),))
    dense_bias = normal_values(key_list[5], (D,), 0.3, 3.0, ((0, 8),))
    expand_weight = normal_values(key_list[6], (D, FF), D ** -0.5, 0.125, ((0, 8),))
    expand_bias = normal_values(key_list[7], (FF,), 0.5, 3.0, ((0, 8),))
    shrink_weight = normal_values(key_list[8], (FF, D), FF ** -0.5, 0.0625, ((0, 8),))
    shrink_bias = normal_values(key_list[9], (D,), 0.3, 3.0, ((0, 8),))
    attend_gain = jnp.clip(1.0 + 0.15 * jax.random.normal(key_list[10], (D,), jnp.float32), 0.25, 1.75).astype(jnp.bfloat16)
    attend_shift = normal_values(key_list[11], (D,), 0.3, 3.0, ((0, 8),))
    feed_gain = jnp.clip(1.0 + 0.15 * jax.random.normal(key_list[12], (D,), jnp.float32), 0.25, 1.75).astype(jnp.bfloat16)
    feed_shift = normal_values(key_list[13], (D,), 0.3, 3.0, ((0, 8),))
    lengths = draw_lengths(jax.random.fold_in(key_list[16], 71), 0)
    slot_source = draw_slot_source(jax.random.fold_in(key_list[16], 71), 0)
    return {"tokens": tokens, "out_cotangent": out_cotangent, "attend_weight": attend_weight, "attend_bias": attend_bias, "dense_weight": dense_weight, "dense_bias": dense_bias, "expand_weight": expand_weight, "expand_bias": expand_bias, "shrink_weight": shrink_weight, "shrink_bias": shrink_bias, "attend_gain": attend_gain, "attend_shift": attend_shift, "feed_gain": feed_gain, "feed_shift": feed_shift, "lengths": lengths, "slot_source": slot_source}


EPSILON = 1e-05
NEG_FILL = -1e+30
HIGHEST = lax.Precision.HIGHEST

@jax.custom_vjp
def low(v):
    return lax.optimization_barrier(v.astype(jnp.bfloat16)).astype(jnp.float32)

@jax.custom_vjp
def low_back(v):
    return v

def low_keep(v):
    return (low(v), None)

def low_pass(kept, grad):
    return (grad,)

def back_keep(v):
    return (v, None)

def back_low(kept, grad):
    return (low(grad),)
low.defvjp(low_keep, low_pass)
low_back.defvjp(back_keep, back_low)

def layer_norm(values, gain, shift):
    center = values - lax.optimization_barrier(jnp.mean(values, axis=-1, keepdims=True))
    spread = lax.optimization_barrier(jnp.mean(center * center, axis=-1, keepdims=True))
    return center * lax.rsqrt(spread + EPSILON) * gain + shift

def stream_info(length_row, source_row):
    starts = jnp.cumsum(length_row) - length_row
    after = source_row[:, None] >= starts[None, :]
    seq_ids = lax.optimization_barrier(jnp.sum(after.astype(jnp.int32), axis=1)) - 1
    begins = lax.optimization_barrier(jnp.max(jnp.where(after, starts[None, :], 0), axis=1))
    return (seq_ids, source_row - begins)

def rotary_tables(positions):
    half_dims = ROT // 2
    rates = 10000.0 ** (-(jnp.arange(half_dims, dtype=jnp.float32) * 2.0 / ROT))
    angles = positions.astype(jnp.float32)[:, None] * rates[None, :]
    angles = jnp.concatenate([angles, angles], axis=1)
    return (jnp.cos(angles), jnp.sin(angles))

def rotate(values, cosine_table, sine_table):
    half_dims = ROT // 2
    leading = values[..., :ROT]
    turned = jnp.concatenate([-leading[..., half_dims:], leading[..., :half_dims]], axis=-1)
    leading = leading * cosine_table[:, None, :] + turned * sine_table[:, None, :]
    return jnp.concatenate([leading, values[..., ROT:]], axis=-1)

def group_layer(params, pieces):
    attend_weight, attend_bias, dense_weight, dense_bias, expand_weight, expand_bias, shrink_weight, shrink_bias, attend_gain, attend_shift, feed_gain, feed_shift = params
    inputs, seq_ids, positions = pieces
    row_count = inputs.shape[0]
    model_width = inputs.shape[1]
    attend_in = low(layer_norm(inputs, attend_gain, attend_shift))
    feed_in = low(layer_norm(inputs, feed_gain, feed_shift))
    triple = low_back(jnp.dot(attend_in, attend_weight, precision=HIGHEST) + attend_bias)
    cosine_table, sine_table = rotary_tables(positions)
    heads_shape = (row_count, H, HD)
    queries = low(rotate(triple[:, :model_width].reshape(heads_shape), cosine_table, sine_table) * HD ** (-0.5))
    key_heads = low(rotate(triple[:, model_width:2 * model_width].reshape(heads_shape), cosine_table, sine_table))
    value_heads = low(triple[:, 2 * model_width:].reshape(heads_shape))
    scores = low_back(jnp.einsum('qhd,khd->hqk', queries, key_heads, precision=HIGHEST))
    visible = (seq_ids[:, None] == seq_ids[None, :]) & (positions[None, :] <= positions[:, None])
    scores = jnp.where(visible[None], scores, NEG_FILL)
    soft_weights = jax.nn.softmax(scores, axis=-1)
    attended = jnp.einsum('hqk,khd->qhd', low(soft_weights), value_heads, precision=HIGHEST)
    attended = low(low_back(attended.reshape(row_count, model_width)))
    attend_out = jnp.dot(attended, dense_weight, precision=HIGHEST) + dense_bias
    expand_pre = low_back(jnp.dot(feed_in, expand_weight, precision=HIGHEST) + expand_bias)
    activated = low(jax.nn.gelu(expand_pre, approximate=False))
    feed_out = jnp.dot(activated, shrink_weight, precision=HIGHEST) + shrink_bias
    return inputs + attend_out + feed_out

def reference(tokens, out_cotangent, attend_weight, attend_bias, dense_weight, dense_bias, expand_weight, expand_bias, shrink_weight, shrink_bias, attend_gain, attend_shift, feed_gain, feed_shift, lengths, slot_source):
    group_count = lengths.shape[0]
    seq_ids, positions = jax.vmap(stream_info)(lengths, slot_source)
    checked = jax.checkpoint(group_layer)

    def forward(inputs, p_attend_weight, p_attend_bias, p_dense_weight, p_dense_bias, p_expand_weight, p_expand_bias, p_shrink_weight, p_shrink_bias, p_attend_gain, p_attend_shift, p_feed_gain, p_feed_shift):
        params = (p_attend_weight, p_attend_bias, p_dense_weight, p_dense_bias, p_expand_weight, p_expand_bias, p_shrink_weight, p_shrink_bias, p_attend_gain, p_attend_shift, p_feed_gain, p_feed_shift)
        mapped = lax.map(lambda pieces: checked(params, pieces), (inputs.reshape(group_count, GROUP_TOK, D), seq_ids, positions))
        return mapped.reshape(group_count * GROUP_TOK, D)
    floats = (tokens.astype(jnp.float32), attend_weight.astype(jnp.float32), attend_bias.astype(jnp.float32), dense_weight.astype(jnp.float32), dense_bias.astype(jnp.float32), expand_weight.astype(jnp.float32), expand_bias.astype(jnp.float32), shrink_weight.astype(jnp.float32), shrink_bias.astype(jnp.float32), attend_gain.astype(jnp.float32), attend_shift.astype(jnp.float32), feed_gain.astype(jnp.float32), feed_shift.astype(jnp.float32))
    layer_out, pullback = jax.vjp(forward, *floats)
    grads = pullback(out_cotangent.astype(jnp.float32))
    return (layer_out.astype(jnp.bfloat16), grads[0], grads[1], grads[2], grads[3], grads[4], grads[5], grads[6], grads[7], grads[8], grads[9], grads[10], grads[11], grads[12])
```

```python
import jax
import jax.numpy as jnp
from jax import lax
from jax.experimental import pallas as pl
from jax.experimental.pallas import tpu as pltpu
from jax.sharding import PartitionSpec as P

D = 2048
HD = 256
ROT = 64
FF_DEV = 1024
ROWS = 128
GROUP = 1024
EPSILON = 1e-05
NEG_FILL = -1e30
MESH = pl.DeviceIdType.MESH
BF = jnp.bfloat16
F32 = jnp.float32
NN = (((1,), (0,)), ((), ()))
NT = (((1,), (1,)), ((), ()))
TN = (((0,), (0,)), ((), ()))
INV_ROOT = HD ** (-0.5)


def dot(a, b, dims):
    return lax.dot_general(a, b, dims, preferred_element_type=F32)


def span(lo, hi, size, body):
    def step(i, carry):
        body(i, pl.ds(pl.multiple_of(i * size, size), size))
        return carry

    lax.fori_loop(lo, hi, step, 0)


def rows_at(start, count):
    return pl.ds(pl.multiple_of(start, 16), count)


def tiles(total, size, body):
    span(0, total // size, size, body)


def turn(values, cosine, sine):
    first = values[:, :128]
    lane = lax.broadcasted_iota(jnp.int32, first.shape, 1)
    swapped = jnp.where(lane < ROT // 2, pltpu.roll(first, 128 - ROT // 2, 1), pltpu.roll(first, ROT // 2, 1))
    return jnp.concatenate([first * cosine + swapped * sine, values[:, 128:]], axis=1)


class Links:
    def __init__(self, send_sems, recv_sems):
        self.rep, self.shard = lax.axis_index("rep"), lax.axis_index("shard")
        rep, shard = self.rep, self.shard
        self.y, self.zh, self.c = rep // 4, lax.rem(rep // 2, 2), lax.rem(rep, 2)
        self.x, self.zl = shard // 2, lax.rem(shard, 2)
        self.sibling = (self.y * 4 + self.zh * 2 + (1 - self.c), shard)
        self.z_rep = (self.y * 4 + (1 - self.zh) * 2 + self.c, shard)
        self.y_plus, self.y_minus, self.y_far = self.at_y(1), self.at_y(3), self.at_y(2)
        self.x_plus, self.x_minus = self.at_x(1), self.at_x(3)
        self.z_shard = (rep, self.x * 2 + (1 - self.zl))
        self.send_sems, self.recv_sems, self.used, self.open = send_sems, recv_sems, 0, []

    def at_y(self, step):
        return (lax.rem(self.y + step, 4) * 4 + self.zh * 2 + self.c, self.shard)

    def at_x(self, step):
        return (self.rep, lax.rem(self.x + step, 4) * 2 + self.zl)

    def peer(self, k):
        return lax.rem(self.shard + k, 8)

    def greet(self, devices):
        barrier = pltpu.get_barrier_semaphore()
        for device in devices:
            pl.semaphore_signal(barrier, inc=1, device_id=device, device_id_type=MESH)
        pl.semaphore_wait(barrier, len(devices))

    def send(self, src, dst, device):
        slot = self.used
        self.used += 1
        copy = pltpu.make_async_remote_copy(
            src_ref=src, dst_ref=dst, send_sem=self.send_sems.at[slot],
            recv_sem=self.recv_sems.at[slot], device_id=device, device_id_type=MESH,
        )
        copy.start()
        self.open.append(copy)
        return slot

    def move(self, src, dst):
        slot = self.used
        self.used += 1
        copy = pltpu.make_async_copy(src, dst, self.recv_sems.at[slot])
        copy.start()
        return slot

    def arrive(self, ref, slot):
        pltpu.make_async_copy(ref, ref, self.recv_sems.at[slot]).wait()

    def close(self):
        for copy in self.open:
            copy.wait_send()


def add_into(target, *others):
    count, total, width = target.shape
    size = 16
    while total % (2 * size) == 0 and 2 * size * width <= 65536:
        size *= 2

    def body(i, carry):
        rows = rows_at(lax.rem(i, total // size) * size, size)
        j = lax.div(i, total // size)
        value = target[j, rows, :].astype(F32)
        for other in others:
            value = value + other[j, rows, :].astype(F32)
        target[j, rows, :] = value.astype(BF)
        return carry

    lax.fori_loop(0, count * (total // size), body, 0)


def ring_steps(links, strip, local, near, far, pos, plus, minus):
    ahead, behind, across = lax.rem(pos + 1, 4), lax.rem(pos + 3, 4), lax.rem(pos + 2, 4)
    a = links.send(strip(across, 0), far.at[0], minus)
    b = links.send(strip(across, 1), far.at[1], plus)
    c0 = links.send(strip(behind, 1), near.at[0, :, 1], minus)
    c1 = links.send(strip(ahead, 0), near.at[1, :, 0], plus)
    yield
    links.arrive(far.at[0], a)
    below, above = local(behind, 0), local(ahead, 1)
    add_into(below, far.at[0])
    d0 = links.send(below, near.at[0, :, 0], minus)
    links.arrive(far.at[1], b)
    add_into(above, far.at[1])
    d1 = links.send(above, near.at[1, :, 1], plus)
    yield
    links.arrive(near.at[0, :, 1], c0)
    links.arrive(near.at[1, :, 0], c1)
    links.arrive(near.at[0, :, 0], d0)
    links.arrive(near.at[1, :, 1], d1)
    for h in range(2):
        add_into(local(pos, h), near.at[0, :, h], near.at[1, :, h])


def swap_steps(links, local, pos, other, index, partner):
    a = links.send(local(pos, 1 - index), other, partner)
    yield
    links.arrive(other, a)
    add_into(local(pos, index), other)


def token_scatter_job(links, source, mine, out, near, far, other):
    x, zl = links.x, links.zl

    def strip(p, h):
        return source.at[:, rows_at((p * 2 + h) * ROWS, ROWS)]

    local = strip
    if mine is not None:
        ahead, behind = lax.rem(x + 1, 4), lax.rem(x + 3, 4)
        places = [(behind, 0), (ahead, 1), (x, 0), (x, 1)]
        slots = [links.move(strip(*place), mine.at[i]) for i, place in enumerate(places)]

        def local(p, h):
            if p is x:
                return mine.at[2 + h]
            return mine.at[h]

    ring = ring_steps(links, strip, local, near, far, x, links.x_plus, links.x_minus)
    next(ring)
    yield
    if mine is not None:
        for i, slot in enumerate(slots):
            links.arrive(mine.at[i], slot)
    yield from ring
    yield from swap_steps(links, local, x, other, zl, links.z_shard)
    links.arrive(out, links.move(local(x, zl), out))


def token_gather_job(links, own, out):
    mine = links.shard * ROWS
    z, xp, xm = links.z_shard, links.x_plus, links.x_minus

    def part(shard, first, count):
        return out.at[rows_at(shard * ROWS + first, count)]

    def forward(shard, first, count, device):
        return links.send(part(shard, first, count), part(shard, first, count), device)

    def near(step, flip):
        zl = 1 - links.zl if flip else links.zl
        return lax.rem(links.x + step, 4) * 2 + zl

    behind, ahead, across = near(3, False), near(1, False), near(2, False)
    behind_z, ahead_z, across_z, own_z = near(3, True), near(1, True), near(2, True), near(0, True)
    low, high = pl.ds(0, 64), pl.ds(64, 64)
    z_low = links.send(own.at[low], part(links.shard, 0, 64), z)
    p_low = links.send(own.at[low], part(links.shard, 0, 64), xp)
    m_low = links.send(own.at[low], part(links.shard, 0, 64), xm)
    p_high = links.send(own.at[high], part(links.shard, 64, 64), xp)
    m_high = links.send(own.at[high], part(links.shard, 64, 64), xm)
    z_high = links.send(own.at[high], part(links.shard, 64, 64), z)
    kept = links.move(own, out.at[rows_at(mine, ROWS)])
    yield
    links.arrive(part(own_z, 0, 64), z_low)
    p_z = forward(own_z, 0, 64, xp)
    m_z = forward(own_z, 0, 64, xm)
    links.arrive(part(behind, 0, 64), p_low)
    p_far0 = forward(behind, 0, 32, xp)
    links.arrive(part(ahead, 0, 64), m_low)
    m_far0 = forward(ahead, 32, 32, xm)
    yield
    links.arrive(part(behind, 64, 64), p_high)
    z_behind = forward(behind, 64, 64, z)
    p_far1 = forward(behind, 64, 32, xp)
    links.arrive(part(ahead, 64, 64), m_high)
    z_ahead = forward(ahead, 64, 64, z)
    m_far1 = forward(ahead, 96, 32, xm)
    yield
    links.arrive(part(behind_z, 0, 64), p_z)
    p_far2 = forward(behind_z, 0, 32, xp)
    links.arrive(part(ahead_z, 0, 64), m_z)
    m_far2 = forward(ahead_z, 32, 32, xm)
    links.arrive(part(across, 64, 32), p_far1)
    z_far0 = forward(across, 64, 32, z)
    links.arrive(part(across, 96, 32), m_far1)
    z_far1 = forward(across, 96, 32, z)
    yield
    links.arrive(out.at[rows_at(mine, ROWS)], kept)
    links.arrive(part(own_z, 64, 64), z_high)
    links.arrive(part(across, 0, 32), p_far0)
    links.arrive(part(across, 32, 32), m_far0)
    links.arrive(part(behind_z, 64, 64), z_behind)
    links.arrive(part(ahead_z, 64, 64), z_ahead)
    links.arrive(part(across_z, 0, 32), p_far2)
    links.arrive(part(across_z, 32, 32), m_far2)
    links.arrive(part(across_z, 64, 32), z_far0)
    links.arrive(part(across_z, 96, 32), z_far1)


def weight_job(links, weight, out, spans):
    piece = rows_at((links.y * 2 + links.c) * 32, 32)
    arrivals = []
    for k in range(8):
        target = links.peer(k)
        for to, first, stride, width in spans:
            cols = pl.ds(pl.multiple_of(first + target * stride, 256), width)
            src, dst = weight.at[piece, cols], out.at[links.shard, piece, pl.ds(to, width)]
            slot = links.send(src, dst, (links.rep, target)) if k else links.move(src, dst)
            arrivals.append((slot, to, width))
    yield
    for slot, to, width in arrivals:
        links.arrive(out.at[0, piece, pl.ds(to, width)], slot)

    def strip(step, first, count):
        return out.at[:, rows_at((lax.rem(links.y + step, 4) * 2 + links.c) * 32 + first, count)]

    def forward(step, first, count, device):
        return links.send(strip(step, first, count), strip(step, first, count), device)

    plus = forward(0, 0, 32, links.y_plus)
    minus = forward(0, 0, 32, links.y_minus)
    given = [(forward(0, 0, 32, links.sibling), 32)]
    yield
    links.arrive(strip(3, 0, 32), plus)
    far0 = forward(3, 0, 16, links.y_plus)
    given.append((forward(3, 0, 32, links.sibling), 32))
    links.arrive(strip(1, 0, 32), minus)
    far1 = forward(1, 16, 16, links.y_minus)
    given.append((forward(1, 0, 32, links.sibling), 32))
    yield
    links.arrive(strip(2, 0, 16), far0)
    given.append((forward(2, 0, 16, links.sibling), 16))
    links.arrive(strip(2, 16, 16), far1)
    given.append((forward(2, 16, 16, links.sibling), 16))
    yield
    for slot, count in given:
        links.arrive(strip(0, 0, count), slot)


def grad_job(links, grad, out, cols, m, got, near, far, other):
    c, y, zh, shard = links.c, links.y, links.zh, links.shard
    count = grad.shape[0]

    def row(cc, yy, hh):
        return (cc * 8 + yy * 2 + hh) * m

    theirs = [lax.rem(y + step, 4) for step in (2, 1, 3, 0)]
    slots = [
        links.send(grad.at[:, rows_at(row(1 - c, p, 0), 2 * m)], got.at[:, rows_at(p * 2 * m, 2 * m)], links.sibling)
        for p in theirs
    ]
    yield
    for p, slot in zip(theirs, slots):
        links.arrive(got.at[:, rows_at(p * 2 * m, 2 * m)], slot)

    add_into(grad.at[:, rows_at(c * 8 * m, 8 * m)], got)
    def held(p, h):
        return grad.at[:, rows_at(row(c, p, h), m)]

    yield from ring_steps(links, held, held, near, far, y, links.y_plus, links.y_minus)
    yield from swap_steps(links, held, y, other, zh, links.z_rep)
    piece = held(y, zh)

    def strip(yy, hh, n):
        return out.at[rows_at(row(c, yy, hh), n)]

    def forward(yy, hh, n, device):
        return links.send(strip(yy, hh, n), strip(yy, hh, n), device)

    mine = strip(y, zh, m)
    if count == 1:
        links.arrive(mine, links.move(piece.at[0], mine))
    else:
        waits = []
        for k in range(8):
            target = links.peer(k)
            for first, start, stride, width in cols:
                there = pl.ds(pl.multiple_of(start + shard * stride, 256), width)
                src = grad.at[target, rows_at(row(c, y, zh), m), pl.ds(first, width)]
                dst = out.at[rows_at(row(c, y, zh), m), there]
                slot = links.send(src, dst, (links.rep, target)) if k else links.move(src, dst)
                waits.append((slot, dst))
        yield
        for slot, dst in waits:
            links.arrive(dst, slot)
    a = forward(y, zh, m, links.z_rep)
    yield
    links.arrive(mine, a)
    e0 = forward(y, 0, 2 * m, links.y_plus)
    e1 = forward(y, 0, 2 * m, links.y_minus)
    given = [(forward(y, 0, 2 * m, links.sibling), 2 * m)]
    yield
    behind, ahead, across = lax.rem(y + 3, 4), lax.rem(y + 1, 4), lax.rem(y + 2, 4)
    links.arrive(strip(behind, 0, 2 * m), e0)
    f0 = forward(behind, 0, m, links.y_plus)
    given.append((forward(behind, 0, 2 * m, links.sibling), 2 * m))
    links.arrive(strip(ahead, 0, 2 * m), e1)
    f1 = forward(ahead, 1, m, links.y_minus)
    given.append((forward(ahead, 0, 2 * m, links.sibling), 2 * m))
    yield
    links.arrive(mine, f0)
    given.append((forward(across, 0, m, links.sibling), m))
    links.arrive(mine, f1)
    given.append((forward(across, 1, m, links.sibling), m))
    yield
    for slot, n in given:
        links.arrive(strip(y, 0, n), slot)


def vector_job(links, source, out, parts, acc, slots_y, other):
    a = links.move(source.at[links.shard], parts.at[links.shard])
    waits = [
        links.send(source.at[links.peer(k)], parts.at[links.shard], (links.rep, links.peer(k)))
        for k in range(1, 8)
    ]
    yield
    links.arrive(parts.at[0], a)
    for slot in waits:
        links.arrive(parts.at[0], slot)
    value = parts[0]
    for s in range(1, 8):
        value = value + parts[s]
    acc[0] = value
    a = links.send(acc.at[0], other.at[0], links.sibling)
    yield
    links.arrive(other.at[0], a)
    acc[1] = acc[0] + other[0]
    a = links.send(acc.at[1], other.at[1], links.z_rep)
    yield
    links.arrive(other.at[1], a)
    acc[2] = acc[1] + other[1]
    slots_y[links.y] = acc[2]
    there = slots_y.at[links.y]
    waits = [links.send(acc.at[2], there, d) for d in (links.y_plus, links.y_minus, links.y_far)]
    yield
    for slot in waits:
        links.arrive(there, slot)
    out[...] = (slots_y[0] + slots_y[1]) + (slots_y[2] + slots_y[3])


def step(*jobs):
    for job in jobs:
        next(job, None)


def run_jobs(*jobs):
    jobs = list(jobs)
    while jobs:
        jobs = [job for job in jobs if next(job, True) is None]


N_SEMS = 320
BACKWARD_ORDER = (
    "*S0", "S0", "*S1", "S1", "out", "S0", "*sl1", "S1", "*sl2", "S0", "*ag", "*D", "D", "S1",
    "*E0", "E0", "S0", "S1", "D", "out", "*at1", "D", "S0", "E0", "*at2", "S1", "D", "*key", "*A0",
    "A0", "out", "E0", "*A1", "A1", "D", "A0", "*A2", "A2", "A1", "*in1", "A2", "E0", "A0", "*in2",
    "A1", "out", "A2", "*in3", "S0", "A1", "A0", "E0", "*in4", "in", "S1", "A1", "A2", "*v", "vec",
    "A0", "E0", "A2", "S0", "S1", "S0", "D", "S0", "in", "S1", "E0", "S1", "D", "A1", "E0", "vec",
    "A0", "A2", "D", "D", "vec", "A1", "A2", "E0", "vec", "E0", "in", "A1", "A0", "vec", "A1", "A2",
    "A1", "A0", "A2", "A2", "A0", "A0", "in",
)
FORWARD_ORDER = (
    "E", "V", "X", "A", "*t1", "*t2", "E", "X", "X", "E", "A", "E", "E", "X", "C", "A", "V", "X", "*n1", "*n2",
    "A", "C", "*e1", "C", "A", "*e2", "*p", "*a1", "C", "*a2", "*o1", "*o2", "C",
)


def follow(order, tasks, jobs):
    for name in order:
        if name[0] == "*":
            tasks[name[1:]]()
        else:
            next(jobs[name], None)
    run_jobs(*jobs.values())

ANY = pl.BlockSpec(memory_space=pl.ANY)
VMEM = pl.BlockSpec(memory_space=pltpu.VMEM)
SMEM = pl.BlockSpec(memory_space=pltpu.SMEM)


def sems(n):
    return [pltpu.SemaphoreType.DMA((n,)), pltpu.SemaphoreType.DMA((n,))]


def shape(*dims, kind=BF):
    return jax.ShapeDtypeStruct(dims, kind)


def small_job(links, small, out):
    slots = [links.send(small, out.at[links.shard], (links.rep, links.peer(k))) for k in range(1, 8)]
    slots.append(links.move(small, out.at[links.shard]))
    yield
    for slot in slots:
        links.arrive(out.at[0], slot)


def forward_kernel(
    tok, cot_own, we_own, wa_own, wd_in, ws_in, g_a, s_a, g_f, s_f, b_d, b_s, b_a, b_e, source, lengths,
    x_out, we_out, wa_out, cot_all, attend_out, feed_out, act_out, slope_out, q_out, k_out, v_out,
    prob_out, mixed_out, part_out, stats_out, vec_out, cosine, sine,
    send_sems, recv_sems, x, we3, wa3, wd, ws, attend_in, feed_in, act, slope, q, k, v, prob, mixed, part,
    small, small_all, src, begin,
):
    links = Links(send_sems, recv_sems)
    own = links.shard
    small[...] = jnp.zeros((16, 256), F32)
    row = 0
    for ref in (g_a, s_a, g_f, s_f, b_d, b_s, b_a, b_e):
        for first in range(0, ref.shape[0], 256):
            small[row : row + 1, :] = ref[pl.ds(first, 256)].astype(F32).reshape(1, 256)
            row += 1
    links.greet(
        [(links.rep, links.peer(p)) for p in range(1, 8)]
        + [links.sibling, links.y_plus, links.y_minus]
    )
    expand = weight_job(links, we_own, we3, [(0, 0, FF_DEV, FF_DEV)])
    attend = weight_job(links, wa_own, wa3, [(p * HD, p * D, HD, HD) for p in range(3)])
    gather_x = token_gather_job(links, tok, x)
    gather_cot = token_gather_job(links, cot_own, cot_all)
    vectors = small_job(links, small, small_all)
    loads = []
    saves = []
    kept = {}

    def save(*pairs):
        for a, b in pairs:
            saves.append((links.move(a, b), b))

    def table_task(h):
        def run():
            if h == 0:
                loads.extend([links.move(wd_in, wd), links.move(ws_in, ws)])
                src[...] = jnp.broadcast_to(source[...].astype(F32), (128, GROUP)).T

            def tile(i, rows):
                here = src[rows, :]
                first = jnp.zeros_like(here)
                start = jnp.int32(0)
                for j in range(3):
                    start = start + lengths[0, j]
                    edge = start.astype(F32)
                    first = jnp.where(here >= edge, edge, first)
                begin[rows, :] = first
                lane = lax.broadcasted_iota(jnp.int32, here.shape, 1)
                pair = lax.rem(lane, ROT // 2).astype(F32)
                angle = (here - first) * jnp.exp(pair * (-2.0 * 9.210340371976184 / ROT))
                cosine[rows, :] = jnp.where(lane < ROT, jnp.cos(angle), 1.0)
                turned = jnp.sin(angle)
                sine[rows, :] = jnp.where(lane < ROT // 2, -turned, jnp.where(lane < ROT, turned, 0.0))

            span(2 * h, 2 * h + 2, 256, tile)

        return run

    def norm_task(h):
        def run():
            if h == 0:
                save((x, x_out))
                for s in range(8):
                    vec_out[:, s * 256 : (s + 1) * 256] = small_all[s, 0:8, :]
                pieces = []
                for p in range(3):
                    block = p * 8 + own
                    pieces.append(small_all[lax.div(block, 3), pl.ds(6 + lax.rem(block, 3), 1), :])
                kept["attend"] = jnp.concatenate(pieces, axis=1)
                kept["expand"] = jnp.concatenate([small_all[own, 9 + p : 10 + p, :] for p in range(4)], axis=1)

            def tile(i, rows):
                values = x[rows, :].astype(F32)
                mean = jnp.mean(values, axis=1, keepdims=True)
                center = values - mean
                inv = lax.rsqrt(jnp.mean(center * center, axis=1, keepdims=True) + EPSILON)
                normed = center * inv
                attend_in[rows, :] = (normed * vec_out[0:1, :] + vec_out[1:2, :]).astype(BF)
                feed_in[rows, :] = (normed * vec_out[2:3, :] + vec_out[3:4, :]).astype(BF)
                lane = lax.broadcasted_iota(jnp.int32, (128, 128), 1)
                stats_out[rows, :] = jnp.where(lane == 0, mean, inv)

            span(4 * h, 4 * h + 4, 128, tile)
            if h == 1:
                save((attend_in, attend_out), (feed_in, feed_out))

        return run

    we, wa = we3.reshape(D, FF_DEV), wa3.reshape(D, 3 * HD)

    def expand_task(h):
        def run():
            if h == 0:
                save((we3, we_out))

            def tile(i, rows):
                pre = dot(feed_in[rows, :], we[...], NN) + kept["expand"]
                below = 0.5 * (1.0 + lax.erf(pre * (0.5 ** 0.5)))
                act[rows, :] = (pre * below).astype(BF)
                density = jnp.exp(-0.5 * pre * pre) * 0.3989422804014327
                slope[rows, :] = (below + pre * density).astype(BF)

            span(2 * h, 2 * h + 2, 256, tile)
            if h == 1:
                save((act, act_out), (slope, slope_out))

        return run

    def project_task():
        save((wa3, wa_out))

        def tile(i, rows):
            triple = dot(attend_in[rows, :], wa[...], NN) + kept["attend"]
            cos, sin = cosine[rows, :], sine[rows, :]
            q[rows, :] = (turn(triple[:, :HD], cos, sin) * INV_ROOT).astype(BF)
            k[rows, :] = turn(triple[:, HD : 2 * HD], cos, sin).astype(BF)
            v[rows, :] = triple[:, 2 * HD :].astype(BF)

        tiles(GROUP, 256, tile)
        save((q, q_out), (k, k_out), (v, v_out))

    def attention_task(h):
        def run():
            key_src = source[...].astype(F32)

            def tile(i, rows):
                scores = dot(q[rows, :], k[...], NT)
                visible = (key_src >= begin[rows, 0:1]) & (key_src <= src[rows, 0:1])
                scores = jnp.where(visible, scores, NEG_FILL)
                weights = jnp.exp(scores - jnp.max(scores, axis=1, keepdims=True))
                weights = (weights / jnp.sum(weights, axis=1, keepdims=True)).astype(BF)
                prob[rows, :] = weights
                mixed[rows, :] = dot(weights, v[...], NN).astype(BF)

            span(2 * h, 2 * h + 2, 256, tile)
            if h == 1:
                save((prob, prob_out), (mixed, mixed_out))

        return run

    def out_task(h):
        def run():
            if h == 0:
                links.arrive(wd, loads[0])
                links.arrive(ws, loads[1])

            def tile(i, rows):
                total = dot(act[rows, :], ws[...], NN) + dot(mixed[rows, :], wd[...], NN)
                part[rows, :] = total.astype(BF)

            span(2 * h, 2 * h + 2, 256, tile)
            if h == 1:
                save((part, part_out))

        return run

    tasks = {
        "t1": table_task(0), "t2": table_task(1), "n1": norm_task(0), "n2": norm_task(1),
        "e1": expand_task(0), "e2": expand_task(1), "p": project_task,
        "a1": attention_task(0), "a2": attention_task(1), "o1": out_task(0), "o2": out_task(1),
    }
    follow(FORWARD_ORDER, tasks, {"E": expand, "A": attend, "X": gather_x, "C": gather_cot, "V": vectors})
    for slot, ref in saves:
        links.arrive(ref, slot)
    links.close()


def forward(*args):
    big, wide, head = (GROUP, D), (GROUP, FF_DEV), (GROUP, HD)
    table = shape(GROUP, 128, kind=F32)
    return pl.pallas_call(
        forward_kernel,
        out_shape=(
            shape(*big), shape(8, 256, FF_DEV), shape(8, 256, 3 * HD), shape(*big),
            shape(*big), shape(*big), shape(*wide), shape(*wide),
            shape(*head), shape(*head), shape(*head), shape(GROUP, GROUP), shape(*head), shape(*big),
            table, shape(8, D, kind=F32), table, table,
        ),
        in_specs=[ANY] * 6 + [VMEM] * 9 + [SMEM],
        out_specs=[ANY] * 14 + [VMEM] * 4,
        scratch_shapes=sems(N_SEMS)
        + [
            pltpu.VMEM(dims, BF)
            for dims in (
                big, (8, 256, FF_DEV), (8, 256, 3 * HD), (HD, D), (FF_DEV, D), big, big, wide, wide,
                head, head, head, (GROUP, GROUP), head, big,
            )
        ]
        + [
            pltpu.VMEM((16, 256), F32),
            pltpu.VMEM((8, 16, 256), F32),
            pltpu.VMEM((GROUP, 128), F32),
            pltpu.VMEM((GROUP, 128), F32),
        ],
        compiler_params=pltpu.CompilerParams(
            collective_id=0, has_side_effects=True, vmem_limit_bytes=62 << 20
        ),
        name="forward",
    )(*args)


def backward_kernel(
    cot_in, act_in, slope_in, feed_in, attend_in, x_in, q_in, k_in, v_in, prob_in, mixed_in, part_in,
    we_in, wa_in, wd_in, ws_in, vec, stats, cosine, sine,
    o_shrink, o_expand, o_attend, o_dense, r_out, r_in, o_vec,
    send_sems, recv_sems,
    rows_buf, we, norm_buf, act_buf, eg, wa, wd, q, k, v, prob, mixed, out_strips,
    g_shrink, g_expand, g_attend, g_dense, ag, tg, sums, vec_parts, *scratch,
):
    links = Links(send_sems, recv_sems)
    take = iter(scratch)

    def grab(n):
        return [next(take) for _ in range(n)]

    def load(*pairs):
        return [(links.move(a, b), b) for a, b in pairs]

    def ready(loads):
        for slot, ref in loads:
            links.arrive(ref, slot)

    first = load((act_in, act_buf), (cot_in, rows_buf.at[0]))
    second = load((slope_in, eg), (ws_in, norm_buf))
    third = load((wd_in, wd), (mixed_in, mixed))
    fourth = load((we_in, we), (wa_in, wa), (q_in, q), (k_in, k), (v_in, v), (prob_in, prob))
    links.greet(
        [(links.rep, links.peer(p)) for p in range(1, 8)]
        + [links.sibling, links.z_rep, links.y_plus, links.y_minus, links.y_far]
    )
    cot = rows_buf.at[0]
    jobs = {}
    for h in range(2):
        cols = pl.ds(h * 1024, 1024)
        jobs["S%d" % h] = grad_job(
            links, g_shrink.at[:, :, cols], o_shrink.at[:, cols], None, 64, *grab(4)
        )
    jobs["E0"] = grad_job(links, g_expand, o_expand, [(0, 0, FF_DEV, FF_DEV)], 16, *grab(4))
    for p in range(3):
        jobs["A%d" % p] = grad_job(
            links, g_attend.at[:, :, pl.ds(p * HD, HD)], o_attend.at[:, pl.ds(p * D, D)],
            [(0, 0, HD, HD)], 16, *grab(4)
        )
    jobs["D"] = grad_job(links, g_dense, o_dense, None, 16, *grab(4))
    jobs["out"] = token_scatter_job(links, part_in, out_strips, r_out, *grab(3))
    jobs["in"] = token_scatter_job(links, rows_buf, None, r_in, *grab(3))
    ones = jnp.ones((8, GROUP), BF)

    loads = {"first": first, "second": second, "third": third, "fourth": fourth}
    kept = {}

    def shrink_task(h):
        def run():
            if h == 0:
                ready(loads["first"])
            cols = pl.ds(h * 1024, 1024)

            def tile(i, rows):
                g_shrink[0, rows, cols] = dot(act_buf[:, rows], cot[:, cols], TN).astype(BF)

            tiles(FF_DEV, 256, tile)

        return run

    def slope_task(h):
        def run():
            if h == 0:
                ready(loads["second"])

            def tile(i, rows):
                grad = dot(cot[rows, :], norm_buf[...], NT)
                eg[rows, :] = (grad * eg[rows, :].astype(F32)).astype(BF)

            span(2 * h, 2 * h + 2, 256, tile)
            if h == 1:
                loads["feed"] = load((feed_in, norm_buf))

        return run

    def attended_task():
        ready(loads["third"])

        def tile(i, rows):
            ag[rows, :] = dot(cot[rows, :], wd[...], NT).astype(BF)

        tiles(GROUP, 256, tile)

    def dense_task():
        for half in range(2):
            cols = pl.ds(half * 1024, 1024)
            g_dense[0, :, cols] = dot(mixed[...], cot[:, cols], TN).astype(BF)
        sums[4:5, :] = dot(ones, cot[...], NN)[0:1]
        loads["x"] = load((x_in, cot))

    def expand_task():
        ready(loads["feed"])

        def tile(i, rows):
            g_expand[i] = dot(norm_buf[:, rows], eg[...], TN).astype(BF)

        tiles(D, 256, tile)
        loads["attend"] = load((attend_in, norm_buf))
        kept["expand"] = dot(ones, eg[...], NN)[0:1]

    def attention_task(h):
        def run():
            if h == 0:
                ready(loads["fourth"])

            def tile(i, rows):
                grad = dot(ag[rows, :], v[...], NT)
                weights = prob[rows, :].astype(F32)
                inner = jnp.sum(weights * grad, axis=1, keepdims=True)
                score_grad = (weights * (grad - inner)).astype(BF)
                act_buf[rows, :] = score_grad
                query_grad = dot(score_grad, k[...], NN) * INV_ROOT
                tg[rows, 0:HD] = turn(query_grad, cosine[rows, :], -sine[rows, :]).astype(BF)

            span(4 * h, 4 * h + 4, 128, tile)

        return run

    def key_task():
        def tile(i, rows):
            key_grad = dot(act_buf[:, rows], q[...], TN)
            tg[rows, HD : 2 * HD] = turn(key_grad, cosine[rows, :], -sine[rows, :]).astype(BF)
            tg[rows, 2 * HD :] = dot(prob[:, rows], ag[...], TN).astype(BF)

        tiles(GROUP, 256, tile)

    def attend_task(p):
        def run():
            if p == 0:
                ready(loads["attend"])
            cols = pl.ds(p * HD, HD)

            def tile(i, rows):
                s = i * 2
                both = dot(norm_buf[:, rows], tg[:, cols], TN).astype(BF)
                g_attend[s, :, cols] = both[:256]
                g_attend[s + 1, :, cols] = both[256:]

            tiles(D, 512, tile)
            if p == 2:
                kept["attend"] = dot(ones, tg[...], NN)[0:1]

        return run

    def input_task(h):
        def run():
            if h == 0:
                ready(loads["x"])
                sums[0:4, :] = jnp.zeros((4, D), F32)

            def tile(i, carry):
                rows = pl.ds(pl.multiple_of(i // 4 * 256, 256), 256)
                cols = pl.ds(pl.multiple_of(lax.rem(i, 4) * 512, 512), 512)
                normed = (cot[rows, cols].astype(F32) - stats[rows, 0:1]) * stats[rows, 1:2]
                grad = dot(tg[rows, :], wa[cols, :], NT)
                sums[0:1, cols] += jnp.sum(grad * normed, axis=0, keepdims=True)
                sums[1:2, cols] += jnp.sum(grad, axis=0, keepdims=True)
                combined = grad * vec[0:1, cols]
                grad = dot(eg[rows, :], we[cols, :], NT)
                sums[2:3, cols] += jnp.sum(grad * normed, axis=0, keepdims=True)
                sums[3:4, cols] += jnp.sum(grad, axis=0, keepdims=True)
                cot[rows, cols] = (combined + grad * vec[2:3, cols]).astype(BF)
                return carry

            lax.fori_loop(h * 4, h * 4 + 4, tile, 0)

        return run

    def vector_task():
        own = links.shard
        for s in range(8):
            vec_parts[s] = jnp.zeros((16, 256), F32)
        for p in range(3):
            block = p * 8 + own
            vec_parts[lax.div(block, 3), pl.ds(lax.rem(block, 3), 1), :] = kept["attend"][:, p * HD : (p + 1) * HD]
        for p in range(4):
            vec_parts[own, 3 + p : 4 + p, :] = kept["expand"][:, p * 256 : (p + 1) * 256]
        for s in range(8):
            vec_parts[s, 7:11, :] = sums[0:4, s * 256 : (s + 1) * 256]
        vec_parts[own, 11:12, :] = sums[4:5, pl.ds(pl.multiple_of(own * 256, 256), 256)]

    jobs["vec"] = vector_job(links, vec_parts, o_vec, *grab(4))
    tasks = {
        "S0": shrink_task(0), "S1": shrink_task(1), "sl1": slope_task(0), "sl2": slope_task(1),
        "ag": attended_task, "D": dense_task, "E0": expand_task,
        "at1": attention_task(0), "at2": attention_task(1), "key": key_task,
        "A0": attend_task(0), "A1": attend_task(1), "A2": attend_task(2),
        "in1": input_task(0), "in2": input_task(1), "in3": input_task(2), "in4": input_task(3),
        "v": vector_task,
    }
    follow(BACKWARD_ORDER, tasks, jobs)
    links.close()


def grad_scratch(s, m, n):
    return [
        pltpu.VMEM((s, 8 * m, n), BF),
        pltpu.VMEM((2, s, 2, m, n), BF),
        pltpu.VMEM((2, s, m, n), BF),
        pltpu.VMEM((s, m, n), BF),
    ]


def token_scratch():
    return [
        pltpu.VMEM((2, 1, 2, ROWS, D), BF),
        pltpu.VMEM((2, 1, ROWS, D), BF),
        pltpu.VMEM((1, ROWS, D), BF),
    ]


def backward(*args):
    big, wide, head = (GROUP, D), (GROUP, FF_DEV), (GROUP, HD)
    return pl.pallas_call(
        backward_kernel,
        out_shape=(
            shape(FF_DEV, D), shape(256, 8 * FF_DEV), shape(256, 3 * D), shape(256, D),
            shape(1, ROWS, D), shape(1, ROWS, D), shape(16, 256, kind=F32),
        ),
        in_specs=[ANY] * 16 + [VMEM] * 4,
        out_specs=[ANY] * 6 + [VMEM],
        scratch_shapes=sems(N_SEMS)
        + [
            pltpu.VMEM(dims, BF)
            for dims in (
                (1, *big), (D, FF_DEV), big, wide, wide, (D, 3 * HD), (HD, D),
                head, head, head, (GROUP, GROUP), head, (4, 1, ROWS, D),
                (1, FF_DEV, D), (8, 256, FF_DEV), (8, 256, 3 * HD), (1, 256, D), head, (GROUP, 3 * HD),
            )
        ]
        + [pltpu.VMEM((8, D), F32), pltpu.VMEM((8, 16, 256), F32)]
        + grad_scratch(1, 64, 1024) * 2
        + grad_scratch(8, 16, FF_DEV)
        + grad_scratch(8, 16, HD) * 3
        + grad_scratch(1, 16, D)
        + token_scratch()
        + token_scratch()
        + [
            pltpu.VMEM((8, 16, 256), F32),
            pltpu.VMEM((3, 16, 256), F32),
            pltpu.VMEM((4, 16, 256), F32),
            pltpu.VMEM((2, 16, 256), F32),
        ],
        compiler_params=pltpu.CompilerParams(
            collective_id=1, has_side_effects=True, vmem_limit_bytes=64 << 20
        ),
        name="backward",
    )(*args)


def per_device(
    tokens,
    out_cotangent,
    attend_weight,
    attend_bias,
    dense_weight,
    dense_bias,
    expand_weight,
    expand_bias,
    shrink_weight,
    shrink_bias,
    attend_gain,
    attend_shift,
    feed_gain,
    feed_shift,
    lengths,
    slot_source,
):
    shard = lax.axis_index("shard")
    (
        x, we, wa, cot, attend_in, feed_in, act, slope, q, k, v, prob, mixed, part,
        stats, vec, cosine, sine,
    ) = forward(
        tokens, out_cotangent, expand_weight, attend_weight, dense_weight, shrink_weight,
        attend_gain, attend_shift, feed_gain, feed_shift, dense_bias, shrink_bias, attend_bias, expand_bias,
        slot_source, lengths,
    )
    we, wa = we.reshape(D, FF_DEV), wa.reshape(D, 3 * HD)
    (shrink_sum, expand_sum, attend_sum, dense_sum, branch_sum, own_combined, sums) = backward(
        cot, act, slope, feed_in, attend_in, x, q, k, v, prob, mixed, part.reshape(1, GROUP, D),
        we, wa, dense_weight, shrink_weight, vec, stats, cosine, sine,
    )
    layer_out = (tokens.astype(F32) + branch_sum.reshape(ROWS, D).astype(F32) + vec[4] + vec[5]).astype(BF)

    def own_rows(values):
        return lax.dynamic_slice_in_dim(values, shard * ROWS, ROWS)

    own_combined = own_combined.reshape(ROWS, D).astype(F32)
    own_stats = own_rows(stats)
    own_inv = own_stats[:, 1:2]
    own_normed = (tokens.astype(F32) - own_stats[:, 0:1]) * own_inv
    mean_c = jnp.mean(own_combined, axis=-1, keepdims=True)
    mean_cn = jnp.mean(own_combined * own_normed, axis=-1, keepdims=True)
    tokens_grad = (
        out_cotangent.astype(F32) + (own_combined - mean_c - own_normed * mean_cn) * own_inv
    )
    return (
        layer_out,
        tokens_grad,
        attend_sum.astype(F32),
        sums[:3].reshape(768),
        dense_sum.astype(F32),
        sums[11],
        expand_sum.astype(F32),
        sums[3:7].reshape(1024),
        shrink_sum.astype(F32),
        sums[11],
        sums[7],
        sums[8],
        sums[9],
        sums[10],
    )


def solution(mesh):
    rows, split, whole = P(("rep", "shard"), None), P("shard"), P("shard", None)
    return jax.shard_map(
        per_device,
        mesh=mesh,
        in_specs=(rows, rows)
        + (whole, split) * 4
        + (split,) * 4
        + (P("rep", None), P("rep", None)),
        out_specs=(rows, rows) + (whole, split) * 4 + (split,) * 4,
        check_vma=False,
    )
```

```python
import jax
import jax.numpy as jnp
from jax import lax
from jax.experimental import pallas as pl
from jax.experimental.pallas import tpu as pltpu
from jax.sharding import PartitionSpec as P

D = 2048
HD = 256
ROT = 64
FF_DEV = 1024
ROWS = 128
GROUP = 1024
EPSILON = 1e-05
NEG_FILL = -1e30
MESH = pl.DeviceIdType.MESH
BF = jnp.bfloat16
F32 = jnp.float32
NN = (((1,), (0,)), ((), ()))
NT = (((1,), (1,)), ((), ()))
TN = (((0,), (0,)), ((), ()))
INV_ROOT = HD ** (-0.5)


def dot(a, b, dims):
    return lax.dot_general(a, b, dims, preferred_element_type=F32)


def span(lo, hi, size, body):
    def step(i, carry):
        body(i, pl.ds(pl.multiple_of(i * size, size), size))
        return carry

    lax.fori_loop(lo, hi, step, 0)


def rows_at(start, count):
    return pl.ds(pl.multiple_of(start, 16), count)


def tiles(total, size, body):
    span(0, total // size, size, body)


def turn(values, cosine, sine):
    first = values[:, :128]
    lane = lax.broadcasted_iota(jnp.int32, first.shape, 1)
    swapped = jnp.where(lane < ROT // 2, pltpu.roll(first, 128 - ROT // 2, 1), pltpu.roll(first, ROT // 2, 1))
    return jnp.concatenate([first * cosine + swapped * sine, values[:, 128:]], axis=1)


class Links:
    def __init__(self, send_sems, recv_sems):
        self.rep, self.shard = lax.axis_index("rep"), lax.axis_index("shard")
        rep, shard = self.rep, self.shard
        self.y, self.zh, self.c = rep // 4, lax.rem(rep // 2, 2), lax.rem(rep, 2)
        self.x, self.zl = shard // 2, lax.rem(shard, 2)
        self.sibling = (self.y * 4 + self.zh * 2 + (1 - self.c), shard)
        self.z_rep = (self.y * 4 + (1 - self.zh) * 2 + self.c, shard)
        self.y_plus, self.y_minus, self.y_far = self.at_y(1), self.at_y(3), self.at_y(2)
        self.x_plus, self.x_minus = self.at_x(1), self.at_x(3)
        self.z_shard = (rep, self.x * 2 + (1 - self.zl))
        self.send_sems, self.recv_sems, self.used, self.open = send_sems, recv_sems, 0, []

    def at_y(self, step):
        return (lax.rem(self.y + step, 4) * 4 + self.zh * 2 + self.c, self.shard)

    def at_x(self, step):
        return (self.rep, lax.rem(self.x + step, 4) * 2 + self.zl)

    def peer(self, k):
        return lax.rem(self.shard + k, 8)

    def greet(self, devices):
        barrier = pltpu.get_barrier_semaphore()
        for device in devices:
            pl.semaphore_signal(barrier, inc=1, device_id=device, device_id_type=MESH)
        pl.semaphore_wait(barrier, len(devices))

    def send(self, src, dst, device):
        slot = self.used
        self.used += 1
        copy = pltpu.make_async_remote_copy(
            src_ref=src, dst_ref=dst, send_sem=self.send_sems.at[slot],
            recv_sem=self.recv_sems.at[slot], device_id=device, device_id_type=MESH,
        )
        copy.start()
        self.open.append(copy)
        return slot

    def move(self, src, dst):
        slot = self.used
        self.used += 1
        copy = pltpu.make_async_copy(src, dst, self.recv_sems.at[slot])
        copy.start()
        return slot

    def arrive(self, ref, slot):
        pltpu.make_async_copy(ref, ref, self.recv_sems.at[slot]).wait()

    def close(self):
        for copy in self.open:
            copy.wait_send()


def add_into(target, *others):
    count, total, width = target.shape
    size = 16
    while total % (2 * size) == 0 and 2 * size * width <= 65536:
        size *= 2

    def body(i, carry):
        rows = rows_at(lax.rem(i, total // size) * size, size)
        j = lax.div(i, total // size)
        value = target[j, rows, :].astype(F32)
        for other in others:
            value = value + other[j, rows, :].astype(F32)
        target[j, rows, :] = value.astype(BF)
        return carry

    lax.fori_loop(0, count * (total // size), body, 0)


def ring_steps(links, strip, local, near, far, pos, plus, minus):
    ahead, behind, across = lax.rem(pos + 1, 4), lax.rem(pos + 3, 4), lax.rem(pos + 2, 4)
    a = links.send(strip(across, 0), far.at[0], minus)
    b = links.send(strip(across, 1), far.at[1], plus)
    c0 = links.send(strip(behind, 1), near.at[0, :, 1], minus)
    c1 = links.send(strip(ahead, 0), near.at[1, :, 0], plus)
    yield
    links.arrive(far.at[0], a)
    below, above = local(behind, 0), local(ahead, 1)
    add_into(below, far.at[0])
    d0 = links.send(below, near.at[0, :, 0], minus)
    links.arrive(far.at[1], b)
    add_into(above, far.at[1])
    d1 = links.send(above, near.at[1, :, 1], plus)
    yield
    links.arrive(near.at[0, :, 1], c0)
    links.arrive(near.at[1, :, 0], c1)
    links.arrive(near.at[0, :, 0], d0)
    links.arrive(near.at[1, :, 1], d1)
    for h in range(2):
        add_into(local(pos, h), near.at[0, :, h], near.at[1, :, h])


def swap_steps(links, local, pos, other, index, partner):
    a = links.send(local(pos, 1 - index), other, partner)
    yield
    links.arrive(other, a)
    add_into(local(pos, index), other)


def token_scatter_job(links, source, mine, out, near, far, other):
    x, zl = links.x, links.zl

    def strip(p, h):
        return source.at[:, rows_at((p * 2 + h) * ROWS, ROWS)]

    local = strip
    if mine is not None:
        ahead, behind = lax.rem(x + 1, 4), lax.rem(x + 3, 4)
        places = [(behind, 0), (ahead, 1), (x, 0), (x, 1)]
        slots = [links.move(strip(*place), mine.at[i]) for i, place in enumerate(places)]

        def local(p, h):
            if p is x:
                return mine.at[2 + h]
            return mine.at[h]

    ring = ring_steps(links, strip, local, near, far, x, links.x_plus, links.x_minus)
    next(ring)
    yield
    if mine is not None:
        for i, slot in enumerate(slots):
            links.arrive(mine.at[i], slot)
    yield from ring
    yield from swap_steps(links, local, x, other, zl, links.z_shard)
    links.arrive(out, links.move(local(x, zl), out))


def token_gather_job(links, own, out):
    mine = links.shard * ROWS
    z, xp, xm = links.z_shard, links.x_plus, links.x_minus

    def part(shard, first, count):
        return out.at[rows_at(shard * ROWS + first, count)]

    def forward(shard, first, count, device):
        return links.send(part(shard, first, count), part(shard, first, count), device)

    def near(step, flip):
        zl = 1 - links.zl if flip else links.zl
        return lax.rem(links.x + step, 4) * 2 + zl

    behind, ahead, across = near(3, False), near(1, False), near(2, False)
    behind_z, ahead_z, across_z, own_z = near(3, True), near(1, True), near(2, True), near(0, True)
    low, high = pl.ds(0, 64), pl.ds(64, 64)
    z_low = links.send(own.at[low], part(links.shard, 0, 64), z)
    p_low = links.send(own.at[low], part(links.shard, 0, 64), xp)
    m_low = links.send(own.at[low], part(links.shard, 0, 64), xm)
    p_high = links.send(own.at[high], part(links.shard, 64, 64), xp)
    m_high = links.send(own.at[high], part(links.shard, 64, 64), xm)
    z_high = links.send(own.at[high], part(links.shard, 64, 64), z)
    kept = links.move(own, out.at[rows_at(mine, ROWS)])
    yield
    links.arrive(out.at[rows_at(mine, ROWS)], kept)
    links.arrive(part(own_z, 0, 64), z_low)
    p_z = forward(own_z, 0, 64, xp)
    m_z = forward(own_z, 0, 64, xm)
    links.arrive(part(behind, 0, 64), p_low)
    p_far0 = forward(behind, 0, 32, xp)
    links.arrive(part(ahead, 0, 64), m_low)
    m_far0 = forward(ahead, 32, 32, xm)
    yield
    links.arrive(part(own_z, 64, 64), z_high)
    links.arrive(part(behind, 64, 64), p_high)
    z_behind = forward(behind, 64, 64, z)
    p_far1 = forward(behind, 64, 32, xp)
    links.arrive(part(ahead, 64, 64), m_high)
    z_ahead = forward(ahead, 64, 64, z)
    m_far1 = forward(ahead, 96, 32, xm)
    yield
    links.arrive(part(behind_z, 0, 64), p_z)
    p_far2 = forward(behind_z, 0, 32, xp)
    links.arrive(part(ahead_z, 0, 64), m_z)
    m_far2 = forward(ahead_z, 32, 32, xm)
    links.arrive(part(across, 64, 32), p_far1)
    z_far0 = forward(across, 64, 32, z)
    links.arrive(part(across, 96, 32), m_far1)
    z_far1 = forward(across, 96, 32, z)
    links.arrive(part(behind_z, 64, 64), z_behind)
    links.arrive(part(ahead_z, 64, 64), z_ahead)
    yield
    links.arrive(part(across, 0, 32), p_far0)
    links.arrive(part(across, 32, 32), m_far0)
    links.arrive(part(across_z, 0, 32), p_far2)
    links.arrive(part(across_z, 32, 32), m_far2)
    links.arrive(part(across_z, 64, 32), z_far0)
    links.arrive(part(across_z, 96, 32), z_far1)


def weight_job(links, weight, out, spans):
    piece = rows_at((links.y * 2 + links.c) * 32, 32)
    arrivals = []
    for k in range(8):
        target = links.peer(k)
        for to, first, stride, width in spans:
            cols = pl.ds(pl.multiple_of(first + target * stride, 256), width)
            src, dst = weight.at[piece, cols], out.at[links.shard, piece, pl.ds(to, width)]
            slot = links.send(src, dst, (links.rep, target)) if k else links.move(src, dst)
            arrivals.append((slot, to, width))
    yield
    for slot, to, width in arrivals:
        links.arrive(out.at[0, piece, pl.ds(to, width)], slot)

    def strip(step, first, count):
        return out.at[:, rows_at((lax.rem(links.y + step, 4) * 2 + links.c) * 32 + first, count)]

    def forward(step, first, count, device):
        return links.send(strip(step, first, count), strip(step, first, count), device)

    plus = forward(0, 0, 32, links.y_plus)
    minus = forward(0, 0, 32, links.y_minus)
    given = [(forward(0, 0, 32, links.sibling), 32)]
    yield
    links.arrive(strip(3, 0, 32), plus)
    far0 = forward(3, 0, 16, links.y_plus)
    given.append((forward(3, 0, 32, links.sibling), 32))
    links.arrive(strip(1, 0, 32), minus)
    far1 = forward(1, 16, 16, links.y_minus)
    given.append((forward(1, 0, 32, links.sibling), 32))
    yield
    links.arrive(strip(2, 0, 16), far0)
    given.append((forward(2, 0, 16, links.sibling), 16))
    links.arrive(strip(2, 16, 16), far1)
    given.append((forward(2, 16, 16, links.sibling), 16))
    yield
    for slot, count in given:
        links.arrive(strip(0, 0, count), slot)


def exchange_columns(links, held, out, row, m, cols):
    waits = []
    for k in range(8):
        target = links.peer(k)
        for first, start, stride, width in cols:
            there = pl.ds(pl.multiple_of(start + links.shard * stride, 256), width)
            src = held.at[target, :, pl.ds(first, width)]
            dst = out.at[rows_at(row, m), there]
            slot = links.send(src, dst, (links.rep, target)) if k else links.move(src, dst)
            waits.append((slot, dst))
    return waits


def grad_job_z(links, grad, out, cols, m, got, near, far, other, origin=None):
    c, y, zh = links.c, links.y, links.zh
    count, _, width = grad.shape
    half, out_half = width // 2, out.shape[1] // 2

    def row(cc, yy, hh):
        return (cc * 8 + yy * 2 + hh) * m

    theirs = [lax.rem(y + step, 4) for step in (2, 1, 3, 0)]
    slots = [
        links.send((origin or grad).at[:, rows_at(row(1 - c, p, 0), 2 * m)], got.at[:, rows_at(p * 2 * m, 2 * m)], links.sibling)
        for p in theirs
    ]
    yield
    for p, slot in zip(theirs, slots):
        links.arrive(got.at[:, rows_at(p * 2 * m, 2 * m)], slot)
    add_into(grad.at[:, rows_at(c * 8 * m, 8 * m)], got)

    def held(p, h):
        return grad.at[:, rows_at(row(c, p, h), m)]

    slots = [links.send(held(p, 1 - zh), other.at[:, p], links.z_rep) for p in theirs]
    yield
    for p, slot in zip(theirs, slots):
        links.arrive(other.at[:, p], slot)
        add_into(held(p, zh), other.at[:, p])

    def side(p, h):
        return grad.at[:, rows_at(row(c, p, zh), m), pl.ds(h * half, half)]

    yield from ring_steps(links, side, side, near, far, y, links.y_plus, links.y_minus)

    def strip(yy, hh, n):
        return out.at[rows_at(row(c, yy, hh), n)]

    def forward(yy, hh, n, device):
        return links.send(strip(yy, hh, n), strip(yy, hh, n), device)

    def out_side(yy, h):
        return out.at[rows_at(row(c, yy, zh), m), pl.ds(h * out_half, out_half)]

    mine = strip(y, zh, m)
    if count == 1:
        links.arrive(mine, links.move(held(y, zh).at[0], mine))
    else:
        waits = exchange_columns(links, held(y, zh), out, row(c, y, zh), m, cols)
        yield
        for slot, dst in waits:
            links.arrive(dst, slot)
    e0 = forward(y, zh, m, links.y_plus)
    e1 = forward(y, zh, m, links.y_minus)
    za = forward(y, zh, m, links.z_rep)
    yield
    behind, ahead, across = lax.rem(y + 3, 4), lax.rem(y + 1, 4), lax.rem(y + 2, 4)
    links.arrive(strip(behind, zh, m), e0)
    f0 = links.send(out_side(behind, 0), out_side(behind, 0), links.y_plus)
    zb0 = forward(behind, zh, m, links.z_rep)
    links.arrive(strip(ahead, zh, m), e1)
    f1 = links.send(out_side(ahead, 1), out_side(ahead, 1), links.y_minus)
    zb1 = forward(ahead, zh, m, links.z_rep)
    yield
    links.arrive(out_side(across, 0), f0)
    links.arrive(out_side(across, 1), f1)
    zc = forward(across, zh, m, links.z_rep)
    links.arrive(strip(y, 1 - zh, m), za)
    given = [forward(y, 0, 2 * m, links.sibling)]
    yield
    links.arrive(strip(behind, 1 - zh, m), zb0)
    given.append(forward(behind, 0, 2 * m, links.sibling))
    links.arrive(strip(ahead, 1 - zh, m), zb1)
    given.append(forward(ahead, 0, 2 * m, links.sibling))
    yield
    links.arrive(strip(across, 1 - zh, m), zc)
    given.append(forward(across, 0, 2 * m, links.sibling))
    yield
    for slot in given:
        links.arrive(strip(y, 0, 2 * m), slot)


def grad_job(links, grad, out, cols, m, got, near, far, other, origin=None):
    c, y, zh = links.c, links.y, links.zh
    count = grad.shape[0]

    def row(cc, yy, hh):
        return (cc * 8 + yy * 2 + hh) * m

    theirs = [lax.rem(y + step, 4) for step in (2, 1, 3, 0)]
    slots = [
        links.send((origin or grad).at[:, rows_at(row(1 - c, p, 0), 2 * m)], got.at[:, rows_at(p * 2 * m, 2 * m)], links.sibling)
        for p in theirs
    ]
    yield
    for p, slot in zip(theirs, slots):
        links.arrive(got.at[:, rows_at(p * 2 * m, 2 * m)], slot)

    add_into(grad.at[:, rows_at(c * 8 * m, 8 * m)], got)
    def held(p, h):
        return grad.at[:, rows_at(row(c, p, h), m)]

    yield from ring_steps(links, held, held, near, far, y, links.y_plus, links.y_minus)
    yield from swap_steps(links, held, y, other, zh, links.z_rep)
    piece = held(y, zh)

    def strip(yy, hh, n):
        return out.at[rows_at(row(c, yy, hh), n)]

    def forward(yy, hh, n, device):
        return links.send(strip(yy, hh, n), strip(yy, hh, n), device)

    mine = strip(y, zh, m)
    if count == 1:
        links.arrive(mine, links.move(piece.at[0], mine))
    else:
        waits = exchange_columns(links, piece, out, row(c, y, zh), m, cols)
        yield
        for slot, dst in waits:
            links.arrive(dst, slot)
    a = forward(y, zh, m, links.z_rep)
    yield
    links.arrive(mine, a)
    e0 = forward(y, 0, 2 * m, links.y_plus)
    e1 = forward(y, 0, 2 * m, links.y_minus)
    given = [(forward(y, 0, 2 * m, links.sibling), 2 * m)]
    yield
    behind, ahead, across = lax.rem(y + 3, 4), lax.rem(y + 1, 4), lax.rem(y + 2, 4)
    links.arrive(strip(behind, 0, 2 * m), e0)
    f0 = forward(behind, 0, m, links.y_plus)
    given.append((forward(behind, 0, 2 * m, links.sibling), 2 * m))
    links.arrive(strip(ahead, 0, 2 * m), e1)
    f1 = forward(ahead, 1, m, links.y_minus)
    given.append((forward(ahead, 0, 2 * m, links.sibling), 2 * m))
    yield
    links.arrive(mine, f0)
    given.append((forward(across, 0, m, links.sibling), m))
    links.arrive(mine, f1)
    given.append((forward(across, 1, m, links.sibling), m))
    yield
    for slot, n in given:
        links.arrive(strip(y, 0, n), slot)


def vector_job(links, source, out, parts, acc, slots_y, other):
    a = links.move(source.at[links.shard], parts.at[links.shard])
    waits = [
        links.send(source.at[links.peer(k)], parts.at[links.shard], (links.rep, links.peer(k)))
        for k in range(1, 8)
    ]
    yield
    links.arrive(parts.at[0], a)
    for slot in waits:
        links.arrive(parts.at[0], slot)
    value = parts[0]
    for s in range(1, 8):
        value = value + parts[s]
    acc[0] = value
    a = links.send(acc.at[0], other.at[0], links.sibling)
    yield
    links.arrive(other.at[0], a)
    acc[1] = acc[0] + other[0]
    a = links.send(acc.at[1], other.at[1], links.z_rep)
    yield
    links.arrive(other.at[1], a)
    acc[2] = acc[1] + other[1]
    slots_y[links.y] = acc[2]
    there = slots_y.at[links.y]
    waits = [links.send(acc.at[2], there, d) for d in (links.y_plus, links.y_minus, links.y_far)]
    yield
    for slot in waits:
        links.arrive(there, slot)
    out[...] = (slots_y[0] + slots_y[1]) + (slots_y[2] + slots_y[3])


def step(*jobs):
    for job in jobs:
        next(job, None)


def run_jobs(*jobs):
    jobs = list(jobs)
    while jobs:
        jobs = [job for job in jobs if next(job, True) is None]


N_SEMS = 320
BACKWARD_ORDER = (
    "S0", "S1", "*lead", "out", "*sl1", "S0", "*sl2", "S1", "*ag", "*D", "D", "*E0", "E0", "out",
    "D", "S1", "*E1", "E1", "S0", "D", "E0", "*at1", "E1", "S0", "S1", "*at2", "D", "*key", "E1",
    "*A0", "A0", "*A1", "A1", "out", "A0", "E0", "E1", "A1", "S1", "D", "*A2", "A2", "A0", "*in1",
    "A1", "A2", "E0", "*in2", "in0", "A1", "A2", "A0", "out", "S0", "E1", "E0", "*in3", "A1", "in0",
    "A2", "A0", "S0", "S1", "*in4", "in1", "A2", "D", "S0", "*v", "vec", "E1", "E0", "A1", "S0",
    "S1", "S0", "D", "in0", "S0", "E1", "A0", "S1", "D", "in1", "A1", "S1", "D", "E0", "in0", "E1",
    "A0", "A2", "vec", "E0", "A1", "vec", "E1", "E0", "in1", "A2", "E1", "A0", "A1", "E0", "vec",
    "A1", "E0", "A2", "A0", "vec", "in1", "A0", "A2", "A2",
)
Z_FIRST = ("S0", "E0")
FORWARD_ORDER = (
    "V", "E", "X", "A", "*t1", "V", "*t2", "E", "X", "X", "*n0", "E", "A", "E", "E", "X", "*nm",
    "C", "*nq", "*e0", "A", "*eq", "X", "*n2", "*em", "A", "*e2", "C", "A", "*p", "C", "*a1", "*a2",
    "*o1", "*o2", "C", "*s0", "*sm", "*sq", "C", "*s2",
)


def follow(order, tasks, jobs):
    for name in order:
        if name[0] == "*":
            tasks[name[1:]]()
        else:
            next(jobs[name], None)
    run_jobs(*jobs.values())

ANY = pl.BlockSpec(memory_space=pl.ANY)
VMEM = pl.BlockSpec(memory_space=pltpu.VMEM)
SMEM = pl.BlockSpec(memory_space=pltpu.SMEM)


def sems(n):
    return [pltpu.SemaphoreType.DMA((n,)), pltpu.SemaphoreType.DMA((n,))]


def shape(*dims, kind=BF):
    return jax.ShapeDtypeStruct(dims, kind)


def small_job(links, small, out):
    slots = [links.send(small, out.at[links.shard], (links.rep, links.peer(k))) for k in range(1, 8)]
    slots.append(links.move(small, out.at[links.shard]))
    yield
    for slot in slots:
        links.arrive(out.at[0], slot)


def forward_kernel(
    tok, cot_own, we_own, wa_own, wd_in, ws_in, g_a, s_a, g_f, s_f, b_d, b_s, b_a, b_e, source, lengths,
    x_out, we_out, wa_out, cot_all, attend_out, feed_out, slope_out, q_out, k_out, v_out,
    prob_out, mixed_out, part_out, shrink_out, stats_out, vec_out, cosine, sine,
    send_sems, recv_sems, x, we3, wa3, wd, ws, attend_in, feed_in, act, slope, q, k, v, prob, mixed, part,
    cot, g_shrink, small, small_all, src, begin, total,
):
    links = Links(send_sems, recv_sems)
    own = links.shard
    small[...] = jnp.zeros((16, 256), F32)
    row = 0
    for ref in (g_a, s_a, g_f, s_f, b_d, b_s, b_a, b_e):
        for first in range(0, ref.shape[0], 256):
            small[row : row + 1, :] = ref[pl.ds(first, 256)].astype(F32).reshape(1, 256)
            row += 1
    links.greet(
        [(links.rep, links.peer(p)) for p in range(1, 8)]
        + [links.sibling, links.y_plus, links.y_minus]
    )
    expand = weight_job(links, we_own, we3, [(0, 0, FF_DEV, FF_DEV)])
    attend = weight_job(links, wa_own, wa3, [(p * HD, p * D, HD, HD) for p in range(3)])
    gather_x = token_gather_job(links, tok, x)
    gather_cot = token_gather_job(links, cot_own, cot)
    vectors = small_job(links, small, small_all)
    loads = []
    saves = []
    kept = {}

    def save(*pairs):
        for a, b in pairs:
            saves.append((links.move(a, b), b))

    def table_task(h):
        def run():
            if h == 0:
                loads.extend([links.move(wd_in, wd), links.move(ws_in, ws)])
                src[...] = jnp.broadcast_to(source[...].astype(F32), (128, GROUP)).T

            def tile(i, rows):
                here = src[rows, :]
                first = jnp.zeros_like(here)
                start = jnp.int32(0)
                for j in range(3):
                    start = start + lengths[0, j]
                    edge = start.astype(F32)
                    first = jnp.where(here >= edge, edge, first)
                begin[rows, :] = first
                lane = lax.broadcasted_iota(jnp.int32, here.shape, 1)
                pair = lax.rem(lane, ROT // 2).astype(F32)
                angle = (here - first) * jnp.exp(pair * (-2.0 * 9.210340371976184 / ROT))
                cosine[rows, :] = jnp.where(lane < ROT, jnp.cos(angle), 1.0)
                turned = jnp.sin(angle)
                sine[rows, :] = jnp.where(lane < ROT // 2, -turned, jnp.where(lane < ROT, turned, 0.0))

            span(2 * h, 2 * h + 2, 256, tile)

        return run

    def pair_rows(hop, first, count):
        return rows_at(lax.rem(links.x + hop, 4) * 256 + first, count)

    def norm_task(hop):
        def run():
            if hop == 0:
                for s in range(8):
                    vec_out[:, s * 256 : (s + 1) * 256] = small_all[s, 0:8, :]
                pieces = []
                for p in range(3):
                    block = p * 8 + own
                    pieces.append(small_all[lax.div(block, 3), pl.ds(6 + lax.rem(block, 3), 1), :])
                kept["attend"] = jnp.concatenate(pieces, axis=1)
                kept["expand"] = jnp.concatenate([small_all[own, 9 + p : 10 + p, :] for p in range(4)], axis=1)

            def tile(i, carry):
                rows = pair_rows(hop, i * 128, 128)
                values = x[rows, :].astype(F32)
                mean = jnp.mean(values, axis=1, keepdims=True)
                center = values - mean
                inv = lax.rsqrt(jnp.mean(center * center, axis=1, keepdims=True) + EPSILON)
                normed = center * inv
                attend_in[rows, :] = (normed * vec_out[0:1, :] + vec_out[1:2, :]).astype(BF)
                feed_in[rows, :] = (normed * vec_out[2:3, :] + vec_out[3:4, :]).astype(BF)
                lane = lax.broadcasted_iota(jnp.int32, (128, 128), 1)
                stats_out[rows, :] = jnp.where(lane == 0, mean, inv)
                return carry

            lax.fori_loop(0, 2, tile, 0)
            if hop == 2:
                save((x, x_out), (attend_in, attend_out), (feed_in, feed_out))

        return run

    we, wa = we3.reshape(D, FF_DEV), wa3.reshape(D, 3 * HD)

    def expand_task(hop):
        def run():
            if hop == 0:
                save((we3, we_out))
            rows = pair_rows(hop, 0, 256)
            pre = dot(feed_in[rows, :], we[...], NN) + kept["expand"]
            below = 0.5 * (1.0 + lax.erf(pre * (0.5 ** 0.5)))
            act[rows, :] = (pre * below).astype(BF)
            density = jnp.exp(-0.5 * pre * pre) * 0.3989422804014327
            slope[rows, :] = (below + pre * density).astype(BF)
            if hop == 2:
                save((slope, slope_out))

        return run

    def shrink_task(hop):
        def run():
            rows = pair_rows(hop, 0, 256)

            def tile(i, here):
                for half in range(2):
                    cols = pl.ds(half * 1024, 1024)
                    value = dot(act[rows, here], cot[rows, cols], TN)
                    if hop == 0:
                        total[here, cols] = value
                    elif hop == 2:
                        g_shrink[0, here, cols] = (total[here, cols] + value).astype(BF)
                    else:
                        total[here, cols] += value

            save((cot.at[rows], cot_all.at[rows]))
            if hop != 2:
                tiles(FF_DEV, 256, tile)
                return
            for i in range(FF_DEV // 256):
                here = pl.ds(i * 256, 256)
                tile(i, here)
                save((g_shrink.at[0, here], shrink_out.at[0, here]))

        return run

    def project_task():
        save((wa3, wa_out))

        def tile(i, rows):
            triple = dot(attend_in[rows, :], wa[...], NN) + kept["attend"]
            cos, sin = cosine[rows, :], sine[rows, :]
            q[rows, :] = (turn(triple[:, :HD], cos, sin) * INV_ROOT).astype(BF)
            k[rows, :] = turn(triple[:, HD : 2 * HD], cos, sin).astype(BF)
            v[rows, :] = triple[:, 2 * HD :].astype(BF)

        tiles(GROUP, 256, tile)
        save((q, q_out), (k, k_out), (v, v_out))

    def attention_task(h):
        def run():
            key_src = source[...].astype(F32)

            def tile(i, rows):
                scores = dot(q[rows, :], k[...], NT)
                visible = (key_src >= begin[rows, 0:1]) & (key_src <= src[rows, 0:1])
                scores = jnp.where(visible, scores, NEG_FILL)
                weights = jnp.exp(scores - jnp.max(scores, axis=1, keepdims=True))
                weights = (weights / jnp.sum(weights, axis=1, keepdims=True)).astype(BF)
                prob[rows, :] = weights
                mixed[rows, :] = dot(weights, v[...], NN).astype(BF)

            span(2 * h, 2 * h + 2, 256, tile)
            if h == 1:
                save((prob, prob_out), (mixed, mixed_out))

        return run

    def out_task(h):
        def run():
            if h == 0:
                links.arrive(wd, loads[0])
                links.arrive(ws, loads[1])

            def tile(i, rows):
                total = dot(act[rows, :], ws[...], NN) + dot(mixed[rows, :], wd[...], NN)
                part[rows, :] = total.astype(BF)

            span(2 * h, 2 * h + 2, 256, tile)
            if h == 1:
                save((part, part_out))

        return run

    tasks = {
        "t1": table_task(0), "t2": table_task(1), "p": project_task,
        "a1": attention_task(0), "a2": attention_task(1), "o1": out_task(0), "o2": out_task(1),
    }
    for hop, name in ((0, "0"), (3, "m"), (1, "q"), (2, "2")):
        tasks["n" + name] = norm_task(hop)
        tasks["e" + name] = expand_task(hop)
        tasks["s" + name] = shrink_task(hop)
    follow(FORWARD_ORDER, tasks, {"E": expand, "A": attend, "X": gather_x, "C": gather_cot, "V": vectors})
    for slot, ref in saves:
        links.arrive(ref, slot)
    links.close()


def forward(*args):
    big, wide, head = (GROUP, D), (GROUP, FF_DEV), (GROUP, HD)
    table = shape(GROUP, 128, kind=F32)
    return pl.pallas_call(
        forward_kernel,
        out_shape=(
            shape(*big), shape(8, 256, FF_DEV), shape(8, 256, 3 * HD), shape(*big),
            shape(*big), shape(*big), shape(*wide),
            shape(*head), shape(*head), shape(*head), shape(GROUP, GROUP), shape(*head), shape(*big),
            shape(1, FF_DEV, D), table, shape(8, D, kind=F32), table, table,
        ),
        in_specs=[ANY] * 6 + [VMEM] * 9 + [SMEM],
        out_specs=[ANY] * 14 + [VMEM] * 4,
        scratch_shapes=sems(N_SEMS)
        + [
            pltpu.VMEM(dims, BF)
            for dims in (
                big, (8, 256, FF_DEV), (8, 256, 3 * HD), (HD, D), (FF_DEV, D), big, big, wide, wide,
                head, head, head, (GROUP, GROUP), head, big, big, (1, FF_DEV, D),
            )
        ]
        + [
            pltpu.VMEM((16, 256), F32),
            pltpu.VMEM((8, 16, 256), F32),
            pltpu.VMEM((GROUP, 128), F32),
            pltpu.VMEM((GROUP, 128), F32),
            pltpu.VMEM((FF_DEV, D), F32),
        ],
        compiler_params=pltpu.CompilerParams(
            collective_id=0, has_side_effects=True, vmem_limit_bytes=62 << 20
        ),
        name="forward",
    )(*args)


def backward_kernel(
    cot_in, shrink_in, slope_in, feed_in, attend_in, x_in, q_in, k_in, v_in, prob_in, mixed_in, part_in,
    we_in, wa_in, wd_in, ws_in, vec, stats, cosine, sine,
    o_shrink, o_expand0, o_expand1, o_attend, o_dense, r_out, r_in, o_vec,
    send_sems, recv_sems,
    rows_buf, we, norm_buf, act_buf, eg, wa, wd, q, k, v, prob, mixed, out_strips,
    g_shrink, g_expand, g_attend, g_dense, ag, tg, sums, vec_parts, *scratch,
):
    links = Links(send_sems, recv_sems)
    take = iter(scratch)

    def grab(n):
        return [next(take) for _ in range(n)]

    def load(*pairs):
        return [(links.move(a, b), b) for a, b in pairs]

    def ready(loads):
        for slot, ref in loads:
            links.arrive(ref, slot)

    half = rows_at(links.c * 512, 512)
    loads = {"first": load((shrink_in.at[:, half], g_shrink.at[:, half]))}
    links.greet(
        [(links.rep, links.peer(p)) for p in range(1, 8)]
        + [links.sibling, links.z_rep, links.y_plus, links.y_minus, links.y_far]
    )
    cot = rows_buf.at[0]
    jobs = {}
    for h in range(2):
        cols = pl.ds(h * 1024, 1024)
        jobs["S%d" % h] = (grad_job, grad_job_z)["S%d" % h in Z_FIRST](
            links, g_shrink.at[:, :, cols], o_shrink.at[:, cols], None, 64, *grab(4),
            shrink_in.at[:, :, cols],
        )
    for h, out in ((0, o_expand0), (1, o_expand1)):
        jobs["E%d" % h] = (grad_job, grad_job_z)["E%d" % h in Z_FIRST](
            links, g_expand.at[:, :, pl.ds(h * 512, 512)], out, [(0, 0, 512, 512)], 16, *grab(4)
        )
    for p in range(3):
        jobs["A%d" % p] = grad_job(
            links, g_attend.at[:, :, pl.ds(p * HD, HD)], o_attend.at[:, pl.ds(p * D, D)],
            [(0, 0, HD, HD)], 16, *grab(4)
        )
    jobs["D"] = grad_job(links, g_dense, o_dense, None, 16, *grab(4))
    jobs["out"] = token_scatter_job(links, part_in, out_strips, r_out, *grab(3))
    for h in range(2):
        cols = pl.ds(h * 1024, 1024)
        jobs["in%d" % h] = token_scatter_job(
            links, rows_buf.at[:, :, cols], None, r_in.at[:, :, cols], *grab(3)
        )
    ones = jnp.ones((8, GROUP), BF)

    kept = {}

    def lead_task():
        ready(loads["first"])
        loads["second"] = load((cot_in, rows_buf.at[0]), (slope_in, eg), (ws_in, norm_buf))

    def slope_task(h):
        def run():
            if h == 0:
                ready(loads["second"])
                loads["third"] = load((wd_in, wd), (mixed_in, mixed))
                loads["fourth"] = load((q_in, q), (k_in, k), (v_in, v), (prob_in, prob))

            def tile(i, rows):
                grad = dot(cot[rows, :], norm_buf[...], NT)
                eg[rows, :] = (grad * eg[rows, :].astype(F32)).astype(BF)

            span(2 * h, 2 * h + 2, 256, tile)
            if h == 1:
                loads["feed"] = load((feed_in, norm_buf))

        return run

    def attended_task():
        ready(loads["third"])

        def tile(i, rows):
            ag[rows, :] = dot(cot[rows, :], wd[...], NT).astype(BF)

        tiles(GROUP, 256, tile)

    def dense_task():
        for half in range(2):
            cols = pl.ds(half * 1024, 1024)
            g_dense[0, :, cols] = dot(mixed[...], cot[:, cols], TN).astype(BF)
        sums[4:5, :] = dot(ones, cot[...], NN)[0:1]
        loads["x"] = load((x_in, cot), (we_in, we), (wa_in, wa))

    def expand_task(h):
        def run():
            if h == 0:
                ready(loads["feed"])
            cols = pl.ds(h * 512, 512)

            def tile(i, rows):
                s = i * 2
                both = dot(norm_buf[:, rows], eg[:, cols], TN).astype(BF)
                g_expand[s, :, cols] = both[:256]
                g_expand[s + 1, :, cols] = both[256:]

            tiles(D, 512, tile)
            if h == 1:
                loads["attend"] = load((attend_in, norm_buf))
                kept["expand"] = dot(ones, eg[...], NN)[0:1]

        return run

    def attention_task(h):
        def run():
            if h == 0:
                ready(loads["fourth"])

            def tile(i, rows):
                grad = dot(ag[rows, :], v[...], NT)
                weights = prob[rows, :].astype(F32)
                inner = jnp.sum(weights * grad, axis=1, keepdims=True)
                score_grad = (weights * (grad - inner)).astype(BF)
                act_buf[rows, :] = score_grad
                query_grad = dot(score_grad, k[...], NN) * INV_ROOT
                tg[rows, 0:HD] = turn(query_grad, cosine[rows, :], -sine[rows, :]).astype(BF)

            span(4 * h, 4 * h + 4, 128, tile)

        return run

    def key_task():
        def tile(i, rows):
            key_grad = dot(act_buf[:, rows], q[...], TN)
            tg[rows, HD : 2 * HD] = turn(key_grad, cosine[rows, :], -sine[rows, :]).astype(BF)
            tg[rows, 2 * HD :] = dot(prob[:, rows], ag[...], TN).astype(BF)

        tiles(GROUP, 256, tile)

    def attend_task(p):
        def run():
            if p == 0:
                ready(loads["attend"])
            cols = pl.ds(p * HD, HD)

            def tile(i, rows):
                s = i * 2
                both = dot(norm_buf[:, rows], tg[:, cols], TN).astype(BF)
                g_attend[s, :, cols] = both[:256]
                g_attend[s + 1, :, cols] = both[256:]

            tiles(D, 512, tile)
            if p == 2:
                kept["attend"] = dot(ones, tg[...], NN)[0:1]

        return run

    def input_task(h):
        def run():
            if h == 0:
                ready(loads["x"])
                sums[0:4, :] = jnp.zeros((4, D), F32)

            def tile(i, carry):
                rows = pl.ds(pl.multiple_of((h % 2 * 2 + i // 2) * 256, 256), 256)
                cols = pl.ds(pl.multiple_of((h // 2 * 2 + lax.rem(i, 2)) * 512, 512), 512)
                normed = (cot[rows, cols].astype(F32) - stats[rows, 0:1]) * stats[rows, 1:2]
                grad = dot(tg[rows, :], wa[cols, :], NT)
                sums[0:1, cols] += jnp.sum(grad * normed, axis=0, keepdims=True)
                sums[1:2, cols] += jnp.sum(grad, axis=0, keepdims=True)
                combined = grad * vec[0:1, cols]
                grad = dot(eg[rows, :], we[cols, :], NT)
                sums[2:3, cols] += jnp.sum(grad * normed, axis=0, keepdims=True)
                sums[3:4, cols] += jnp.sum(grad, axis=0, keepdims=True)
                cot[rows, cols] = (combined + grad * vec[2:3, cols]).astype(BF)
                return carry

            lax.fori_loop(0, 4, tile, 0)

        return run

    def vector_task():
        own = links.shard
        for s in range(8):
            vec_parts[s] = jnp.zeros((16, 256), F32)
        for p in range(3):
            block = p * 8 + own
            vec_parts[lax.div(block, 3), pl.ds(lax.rem(block, 3), 1), :] = kept["attend"][:, p * HD : (p + 1) * HD]
        for p in range(4):
            vec_parts[own, 3 + p : 4 + p, :] = kept["expand"][:, p * 256 : (p + 1) * 256]
        for s in range(8):
            vec_parts[s, 7:11, :] = sums[0:4, s * 256 : (s + 1) * 256]
        vec_parts[own, 11:12, :] = sums[4:5, pl.ds(pl.multiple_of(own * 256, 256), 256)]

    jobs["vec"] = vector_job(links, vec_parts, o_vec, *grab(4))
    tasks = {
        "lead": lead_task, "sl1": slope_task(0), "sl2": slope_task(1),
        "ag": attended_task, "D": dense_task, "E0": expand_task(0), "E1": expand_task(1),
        "at1": attention_task(0), "at2": attention_task(1), "key": key_task,
        "A0": attend_task(0), "A1": attend_task(1), "A2": attend_task(2),
        "in1": input_task(0), "in2": input_task(1), "in3": input_task(2), "in4": input_task(3),
        "v": vector_task,
    }
    follow(BACKWARD_ORDER, tasks, jobs)
    links.close()


def grad_scratch(s, m, n, name=""):
    dims = ((2, s, 2, m, n), (2, s, m, n), (s, m, n))
    if name in Z_FIRST:
        dims = ((2, s, 2, m, n // 2), (2, s, m, n // 2), (s, 4, m, n))
    return [pltpu.VMEM((s, 8 * m, n), BF)] + [pltpu.VMEM(d, BF) for d in dims]


def token_scratch(width):
    return [
        pltpu.VMEM((2, 1, 2, ROWS, width), BF),
        pltpu.VMEM((2, 1, ROWS, width), BF),
        pltpu.VMEM((1, ROWS, width), BF),
    ]


def backward(*args):
    big, wide, head = (GROUP, D), (GROUP, FF_DEV), (GROUP, HD)
    return pl.pallas_call(
        backward_kernel,
        out_shape=(
            shape(FF_DEV, D), shape(256, 8 * 512), shape(256, 8 * 512), shape(256, 3 * D), shape(256, D),
            shape(1, ROWS, D), shape(1, ROWS, D), shape(16, 256, kind=F32),
        ),
        in_specs=[ANY] * 16 + [VMEM] * 4,
        out_specs=[ANY] * 7 + [VMEM],
        scratch_shapes=sems(N_SEMS)
        + [
            pltpu.VMEM(dims, BF)
            for dims in (
                (1, *big), (D, FF_DEV), big, wide, wide, (D, 3 * HD), (HD, D),
                head, head, head, (GROUP, GROUP), head, (4, 1, ROWS, D),
                (1, FF_DEV, D), (8, 256, FF_DEV), (8, 256, 3 * HD), (1, 256, D), head, (GROUP, 3 * HD),
            )
        ]
        + [pltpu.VMEM((8, D), F32), pltpu.VMEM((8, 16, 256), F32)]
        + grad_scratch(1, 64, 1024, "S0")
        + grad_scratch(1, 64, 1024, "S1")
        + grad_scratch(8, 16, 512, "E0")
        + grad_scratch(8, 16, 512, "E1")
        + grad_scratch(8, 16, HD) * 3
        + grad_scratch(1, 16, D)
        + token_scratch(D)
        + token_scratch(1024) * 2
        + [
            pltpu.VMEM((8, 16, 256), F32),
            pltpu.VMEM((3, 16, 256), F32),
            pltpu.VMEM((4, 16, 256), F32),
            pltpu.VMEM((2, 16, 256), F32),
        ],
        compiler_params=pltpu.CompilerParams(
            collective_id=1, has_side_effects=True, vmem_limit_bytes=64 << 20
        ),
        name="backward",
    )(*args)


def finish_kernel(
    shrink, expand0, expand1, attend, dense, branch, combined, tok, cot, vec, sums,
    layer_out, tokens_grad, g_attend, b_attend, g_dense, b_dense, g_expand, b_expand, g_shrink, b_shrink,
    gain_a, shift_a, gain_f, shift_f,
):
    g_shrink[...] = shrink[...].astype(F32)
    for s in range(8):
        for h, half in enumerate((expand0, expand1)):
            g_expand[:, (2 * s + h) * 512 : (2 * s + h + 1) * 512] = half[:, s * 512 : (s + 1) * 512].astype(F32)
    g_attend[...] = attend[...].astype(F32)
    g_dense[...] = dense[...].astype(F32)
    values = tok[...].astype(F32)
    layer_out[...] = (values + branch[0].astype(F32) + vec[4:5, :] + vec[5:6, :]).astype(BF)
    center = values - jnp.mean(values, axis=1, keepdims=True)
    inv = lax.rsqrt(jnp.mean(center * center, axis=1, keepdims=True) + EPSILON)
    normed = center * inv
    grad = combined[0].astype(F32)
    mean = jnp.mean(grad, axis=1, keepdims=True)
    slant = jnp.mean(grad * normed, axis=1, keepdims=True)
    tokens_grad[...] = cot[...].astype(F32) + (grad - mean - normed * slant) * inv

    @pl.when(pl.program_id(0) == 0)
    def _():
        for ref, first in ((b_attend, 0), (b_expand, 3), (gain_a, 7), (shift_a, 8), (gain_f, 9), (shift_f, 10),
                           (b_dense, 11), (b_shrink, 11)):
            for i in range(ref.shape[0] // 256):
                ref[pl.ds(i * 256, 256)] = sums[first + i : first + i + 1, :].reshape(256)


def finish(*args):
    steps = 2

    def rows(n, width):
        return pl.BlockSpec((n // steps, width), lambda i: (i, 0))

    def part(n, width):
        return pl.BlockSpec((1, n // steps, width), lambda i: (0, i, 0))

    def whole(*dims):
        return pl.BlockSpec(dims, lambda i: (0,) * len(dims))

    weights = [rows(256, 3 * D), rows(256, D), rows(256, 8 * FF_DEV), rows(FF_DEV, D)]
    return pl.pallas_call(
        finish_kernel,
        grid=(steps,),
        out_shape=(
            shape(ROWS, D), shape(ROWS, D, kind=F32),
            shape(256, 3 * D, kind=F32), shape(768, kind=F32), shape(256, D, kind=F32), shape(256, kind=F32),
            shape(256, 8 * FF_DEV, kind=F32), shape(1024, kind=F32), shape(FF_DEV, D, kind=F32),
            *[shape(256, kind=F32)] * 5,
        ),
        in_specs=[weights[3], rows(256, 4096), rows(256, 4096), weights[0], weights[1], part(ROWS, D), part(ROWS, D)]
        + [rows(ROWS, D)] * 2
        + [whole(8, D), whole(16, 256)],
        out_specs=[
            rows(ROWS, D), rows(ROWS, D), weights[0], whole(768), weights[1], whole(256), weights[2],
            whole(1024), weights[3], *[whole(256)] * 5,
        ],
        compiler_params=pltpu.CompilerParams(vmem_limit_bytes=60 << 20),
        name="finish",
    )(*args)


def per_device(
    tokens,
    out_cotangent,
    attend_weight,
    attend_bias,
    dense_weight,
    dense_bias,
    expand_weight,
    expand_bias,
    shrink_weight,
    shrink_bias,
    attend_gain,
    attend_shift,
    feed_gain,
    feed_shift,
    lengths,
    slot_source,
):
    (
        x, we, wa, cot, attend_in, feed_in, slope, q, k, v, prob, mixed, part, shrink,
        stats, vec, cosine, sine,
    ) = forward(
        tokens, out_cotangent, expand_weight, attend_weight, dense_weight, shrink_weight,
        attend_gain, attend_shift, feed_gain, feed_shift, dense_bias, shrink_bias, attend_bias, expand_bias,
        slot_source, lengths,
    )
    we, wa = we.reshape(D, FF_DEV), wa.reshape(D, 3 * HD)
    (shrink_sum, expand0, expand1, attend_sum, dense_sum, branch_sum, own_combined, sums) = backward(
        cot, shrink, slope, feed_in, attend_in, x, q, k, v, prob, mixed, part.reshape(1, GROUP, D),
        we, wa, dense_weight, shrink_weight, vec, stats, cosine, sine,
    )
    return tuple(
        finish(
            shrink_sum, expand0, expand1, attend_sum, dense_sum, branch_sum, own_combined,
            tokens, out_cotangent, vec, sums,
        )
    )


def solution(mesh):
    rows, split, whole = P(("rep", "shard"), None), P("shard"), P("shard", None)
    return jax.shard_map(
        per_device,
        mesh=mesh,
        in_specs=(rows, rows)
        + (whole, split) * 4
        + (split,) * 4
        + (P("rep", None), P("rep", None)),
        out_specs=(rows, rows) + (whole, split) * 4 + (split,) * 4,
        check_vma=False,
    )
```

```python
import jax
import jax.numpy as jnp
from jax import lax
from jax.experimental import pallas as pl
from jax.experimental.pallas import tpu as pltpu
from jax.sharding import PartitionSpec as P

D = 2048
HD = 256
ROT = 64
FF_DEV = 1024
ROWS = 128
GROUP = 1024
EPSILON = 1e-05
NEG_FILL = -1e30
MESH = pl.DeviceIdType.MESH
BF = jnp.bfloat16
F32 = jnp.float32
NN = (((1,), (0,)), ((), ()))
NT = (((1,), (1,)), ((), ()))
TN = (((0,), (0,)), ((), ()))
INV_ROOT = HD ** (-0.5)


def dot(a, b, dims):
    return lax.dot_general(a, b, dims, preferred_element_type=F32)


def span(lo, hi, size, body):
    def step(i, carry):
        body(i, pl.ds(pl.multiple_of(i * size, size), size))
        return carry

    lax.fori_loop(lo, hi, step, 0)


def rows_at(start, count):
    return pl.ds(pl.multiple_of(start, 16), count)


def tiles(total, size, body):
    span(0, total // size, size, body)


def turn(values, cosine, sine):
    first = values[:, :128]
    lane = lax.broadcasted_iota(jnp.int32, first.shape, 1)
    swapped = jnp.where(lane < ROT // 2, pltpu.roll(first, 128 - ROT // 2, 1), pltpu.roll(first, ROT // 2, 1))
    return jnp.concatenate([first * cosine + swapped * sine, values[:, 128:]], axis=1)


class Links:
    def __init__(self, send_sems, recv_sems):
        self.rep, self.shard = lax.axis_index("rep"), lax.axis_index("shard")
        rep, shard = self.rep, self.shard
        self.y, self.zh, self.c = rep // 4, lax.rem(rep // 2, 2), lax.rem(rep, 2)
        self.x, self.zl = shard // 2, lax.rem(shard, 2)
        self.sibling = (self.y * 4 + self.zh * 2 + (1 - self.c), shard)
        self.z_rep = (self.y * 4 + (1 - self.zh) * 2 + self.c, shard)
        self.y_plus, self.y_minus, self.y_far = self.at_y(1), self.at_y(3), self.at_y(2)
        self.x_plus, self.x_minus = self.at_x(1), self.at_x(3)
        self.z_shard = (rep, self.x * 2 + (1 - self.zl))
        self.send_sems, self.recv_sems, self.used, self.open = send_sems, recv_sems, 0, []

    def at_y(self, step):
        return (lax.rem(self.y + step, 4) * 4 + self.zh * 2 + self.c, self.shard)

    def at_x(self, step):
        return (self.rep, lax.rem(self.x + step, 4) * 2 + self.zl)

    def peer(self, k):
        return lax.rem(self.shard + k, 8)

    def greet(self, devices):
        barrier = pltpu.get_barrier_semaphore()
        for device in devices:
            pl.semaphore_signal(barrier, inc=1, device_id=device, device_id_type=MESH)
        pl.semaphore_wait(barrier, len(devices))

    def send(self, src, dst, device):
        slot = self.used
        self.used += 1
        copy = pltpu.make_async_remote_copy(
            src_ref=src, dst_ref=dst, send_sem=self.send_sems.at[slot],
            recv_sem=self.recv_sems.at[slot], device_id=device, device_id_type=MESH,
        )
        copy.start()
        self.open.append(copy)
        return slot

    def move(self, src, dst):
        slot = self.used
        self.used += 1
        copy = pltpu.make_async_copy(src, dst, self.recv_sems.at[slot])
        copy.start()
        return slot

    def arrive(self, ref, slot):
        pltpu.make_async_copy(ref, ref, self.recv_sems.at[slot]).wait()

    def close(self):
        for copy in self.open:
            copy.wait_send()


def add_into(target, *others):
    count, total, width = target.shape
    size = 16
    while total % (2 * size) == 0 and 2 * size * width <= 65536:
        size *= 2

    def body(i, carry):
        rows = rows_at(lax.rem(i, total // size) * size, size)
        j = lax.div(i, total // size)
        value = target[j, rows, :].astype(F32)
        for other in others:
            value = value + other[j, rows, :].astype(F32)
        target[j, rows, :] = value.astype(BF)
        return carry

    lax.fori_loop(0, count * (total // size), body, 0)


def ring_steps(links, strip, local, near, far, pos, plus, minus):
    ahead, behind, across = lax.rem(pos + 1, 4), lax.rem(pos + 3, 4), lax.rem(pos + 2, 4)
    a = links.send(strip(across, 0), far.at[0], minus)
    b = links.send(strip(across, 1), far.at[1], plus)
    c0 = links.send(strip(behind, 1), near.at[0, :, 1], minus)
    c1 = links.send(strip(ahead, 0), near.at[1, :, 0], plus)
    yield
    links.arrive(far.at[0], a)
    below, above = local(behind, 0), local(ahead, 1)
    add_into(below, far.at[0])
    d0 = links.send(below, near.at[0, :, 0], minus)
    links.arrive(far.at[1], b)
    add_into(above, far.at[1])
    d1 = links.send(above, near.at[1, :, 1], plus)
    yield
    links.arrive(near.at[0, :, 1], c0)
    links.arrive(near.at[1, :, 0], c1)
    links.arrive(near.at[0, :, 0], d0)
    links.arrive(near.at[1, :, 1], d1)
    for h in range(2):
        add_into(local(pos, h), near.at[0, :, h], near.at[1, :, h])


def swap_steps(links, local, pos, other, index, partner):
    a = links.send(local(pos, 1 - index), other, partner)
    yield
    links.arrive(other, a)
    add_into(local(pos, index), other)


def token_scatter_job(links, source, mine, out, near, far, other):
    x, zl = links.x, links.zl

    def strip(p, h):
        return source.at[:, rows_at((p * 2 + h) * ROWS, ROWS)]

    local = strip
    if mine is not None:
        ahead, behind = lax.rem(x + 1, 4), lax.rem(x + 3, 4)
        places = [(behind, 0), (ahead, 1), (x, 0), (x, 1)]
        slots = [links.move(strip(*place), mine.at[i]) for i, place in enumerate(places)]

        def local(p, h):
            if p is x:
                return mine.at[2 + h]
            return mine.at[h]

    ring = ring_steps(links, strip, local, near, far, x, links.x_plus, links.x_minus)
    next(ring)
    yield
    if mine is not None:
        for i, slot in enumerate(slots):
            links.arrive(mine.at[i], slot)
    yield from ring
    yield from swap_steps(links, local, x, other, zl, links.z_shard)
    links.arrive(out, links.move(local(x, zl), out))


def token_gather_job(links, own, out, low_rows):
    mine = links.shard * ROWS
    nl, nh = low_rows, ROWS - low_rows
    z, xp, xm = links.z_shard, links.x_plus, links.x_minus

    def part(shard, first, count):
        return out.at[rows_at(shard * ROWS + first, count)]

    def forward(shard, first, count, device):
        return links.send(part(shard, first, count), part(shard, first, count), device)

    def near(step, flip):
        zl = 1 - links.zl if flip else links.zl
        return lax.rem(links.x + step, 4) * 2 + zl

    behind, ahead, across = near(3, False), near(1, False), near(2, False)
    behind_z, ahead_z, across_z, own_z = near(3, True), near(1, True), near(2, True), near(0, True)
    low, high = pl.ds(0, nl), pl.ds(nl, nh)
    z_low = links.send(own.at[low], part(links.shard, 0, nl), z)
    p_low = links.send(own.at[low], part(links.shard, 0, nl), xp)
    m_low = links.send(own.at[low], part(links.shard, 0, nl), xm)
    p_high = links.send(own.at[high], part(links.shard, nl, nh), xp)
    m_high = links.send(own.at[high], part(links.shard, nl, nh), xm)
    z_high = links.send(own.at[high], part(links.shard, nl, nh), z)
    kept = links.move(own, out.at[rows_at(mine, ROWS)])
    yield
    links.arrive(out.at[rows_at(mine, ROWS)], kept)
    links.arrive(part(own_z, 0, nl), z_low)
    p_z = forward(own_z, 0, nl, xp)
    m_z = forward(own_z, 0, nl, xm)
    links.arrive(part(behind, 0, nl), p_low)
    p_far0 = forward(behind, 0, nl // 2, xp)
    links.arrive(part(ahead, 0, nl), m_low)
    m_far0 = forward(ahead, nl // 2, nl // 2, xm)
    yield
    links.arrive(part(own_z, nl, nh), z_high)
    links.arrive(part(behind, nl, nh), p_high)
    z_behind = forward(behind, nl, nh, z)
    p_far1 = forward(behind, nl, nh // 2, xp)
    links.arrive(part(ahead, nl, nh), m_high)
    z_ahead = forward(ahead, nl, nh, z)
    m_far1 = forward(ahead, nl + nh // 2, nh // 2, xm)
    yield
    links.arrive(part(behind_z, 0, nl), p_z)
    p_far2 = forward(behind_z, 0, nl // 2, xp)
    links.arrive(part(ahead_z, 0, nl), m_z)
    m_far2 = forward(ahead_z, nl // 2, nl // 2, xm)
    links.arrive(part(across, nl, nh // 2), p_far1)
    z_far0 = forward(across, nl, nh // 2, z)
    links.arrive(part(across, nl + nh // 2, nh // 2), m_far1)
    z_far1 = forward(across, nl + nh // 2, nh // 2, z)
    links.arrive(part(behind_z, nl, nh), z_behind)
    links.arrive(part(ahead_z, nl, nh), z_ahead)
    yield
    links.arrive(part(across, 0, nl // 2), p_far0)
    links.arrive(part(across, nl // 2, nl // 2), m_far0)
    links.arrive(part(across_z, 0, nl // 2), p_far2)
    links.arrive(part(across_z, nl // 2, nl // 2), m_far2)
    links.arrive(part(across_z, nl, nh // 2), z_far0)
    links.arrive(part(across_z, nl + nh // 2, nh // 2), z_far1)


def weight_job(links, weight, out, spans):
    piece = rows_at((links.y * 2 + links.c) * 32, 32)
    arrivals = []
    for k in range(8):
        target = links.peer(k)
        for to, first, stride, width in spans:
            cols = pl.ds(pl.multiple_of(first + target * stride, 256), width)
            src, dst = weight.at[piece, cols], out.at[links.shard, piece, pl.ds(to, width)]
            slot = links.send(src, dst, (links.rep, target)) if k else links.move(src, dst)
            arrivals.append((slot, to, width))
    yield
    for slot, to, width in arrivals:
        links.arrive(out.at[0, piece, pl.ds(to, width)], slot)

    def strip(step, first, count):
        return out.at[:, rows_at((lax.rem(links.y + step, 4) * 2 + links.c) * 32 + first, count)]

    def forward(step, first, count, device):
        return links.send(strip(step, first, count), strip(step, first, count), device)

    plus = forward(0, 0, 32, links.y_plus)
    minus = forward(0, 0, 32, links.y_minus)
    given = [(forward(0, 0, 32, links.sibling), 32)]
    yield
    links.arrive(strip(3, 0, 32), plus)
    far0 = forward(3, 0, 16, links.y_plus)
    given.append((forward(3, 0, 32, links.sibling), 32))
    links.arrive(strip(1, 0, 32), minus)
    far1 = forward(1, 16, 16, links.y_minus)
    given.append((forward(1, 0, 32, links.sibling), 32))
    yield
    links.arrive(strip(2, 0, 16), far0)
    given.append((forward(2, 0, 16, links.sibling), 16))
    links.arrive(strip(2, 16, 16), far1)
    given.append((forward(2, 16, 16, links.sibling), 16))
    yield
    for slot, count in given:
        links.arrive(strip(0, 0, count), slot)


def exchange_columns(links, held, out, row, m, cols):
    waits = []
    for k in range(8):
        target = links.peer(k)
        for first, start, stride, width in cols:
            there = pl.ds(pl.multiple_of(start + links.shard * stride, 256), width)
            src = held.at[target, :, pl.ds(first, width)]
            dst = out.at[rows_at(row, m), there]
            slot = links.send(src, dst, (links.rep, target)) if k else links.move(src, dst)
            waits.append((slot, dst))
    return waits


def grad_job_z(links, grad, out, cols, m, got, near, far, other, ready=None):
    c, y, zh = links.c, links.y, links.zh
    count, _, width = grad.shape
    half, out_half = width // 2, out.shape[1] // 2

    def row(cc, yy, hh):
        return (cc * 8 + yy * 2 + hh) * m

    theirs = [lax.rem(y + step, 4) for step in (2, 1, 3, 0)]
    if ready is None:
        slots = [
            links.send(grad.at[:, rows_at(row(1 - c, p, 0), 2 * m)], got.at[:, rows_at(p * 2 * m, 2 * m)], links.sibling)
            for p in theirs
        ]
        yield
        for p, slot in zip(theirs, slots):
            links.arrive(got.at[:, rows_at(p * 2 * m, 2 * m)], slot)
    else:
        ready()
    add_into(grad.at[:, rows_at(c * 8 * m, 8 * m)], got)

    def held(p, h):
        return grad.at[:, rows_at(row(c, p, h), m)]

    slots = [links.send(held(p, 1 - zh), other.at[:, p], links.z_rep) for p in theirs]
    yield
    for p, slot in zip(theirs, slots):
        links.arrive(other.at[:, p], slot)
        add_into(held(p, zh), other.at[:, p])

    def side(p, h):
        return grad.at[:, rows_at(row(c, p, zh), m), pl.ds(h * half, half)]

    yield from ring_steps(links, side, side, near, far, y, links.y_plus, links.y_minus)

    def strip(yy, hh, n):
        return out.at[rows_at(row(c, yy, hh), n)]

    def forward(yy, hh, n, device):
        return links.send(strip(yy, hh, n), strip(yy, hh, n), device)

    def out_side(yy, h):
        return out.at[rows_at(row(c, yy, zh), m), pl.ds(h * out_half, out_half)]

    mine = strip(y, zh, m)
    if count == 1:
        links.arrive(mine, links.move(held(y, zh).at[0], mine))
    else:
        waits = exchange_columns(links, held(y, zh), out, row(c, y, zh), m, cols)
        yield
        for slot, dst in waits:
            links.arrive(dst, slot)
    e0 = forward(y, zh, m, links.y_plus)
    e1 = forward(y, zh, m, links.y_minus)
    za = forward(y, zh, m, links.z_rep)
    yield
    behind, ahead, across = lax.rem(y + 3, 4), lax.rem(y + 1, 4), lax.rem(y + 2, 4)
    links.arrive(strip(behind, zh, m), e0)
    f0 = links.send(out_side(behind, 0), out_side(behind, 0), links.y_plus)
    zb0 = forward(behind, zh, m, links.z_rep)
    links.arrive(strip(ahead, zh, m), e1)
    f1 = links.send(out_side(ahead, 1), out_side(ahead, 1), links.y_minus)
    zb1 = forward(ahead, zh, m, links.z_rep)
    yield
    links.arrive(out_side(across, 0), f0)
    links.arrive(out_side(across, 1), f1)
    zc = forward(across, zh, m, links.z_rep)
    links.arrive(strip(y, 1 - zh, m), za)
    given = [forward(y, 0, 2 * m, links.sibling)]
    yield
    links.arrive(strip(behind, 1 - zh, m), zb0)
    given.append(forward(behind, 0, 2 * m, links.sibling))
    links.arrive(strip(ahead, 1 - zh, m), zb1)
    given.append(forward(ahead, 0, 2 * m, links.sibling))
    yield
    links.arrive(strip(across, 1 - zh, m), zc)
    given.append(forward(across, 0, 2 * m, links.sibling))
    yield
    for slot in given:
        links.arrive(strip(y, 0, 2 * m), slot)


def grad_job(links, grad, out, cols, m, got, near, far, other, ready=None):
    c, y, zh = links.c, links.y, links.zh
    count = grad.shape[0]

    def row(cc, yy, hh):
        return (cc * 8 + yy * 2 + hh) * m

    theirs = [lax.rem(y + step, 4) for step in (2, 1, 3, 0)]
    if ready is None:
        slots = [
            links.send(grad.at[:, rows_at(row(1 - c, p, 0), 2 * m)], got.at[:, rows_at(p * 2 * m, 2 * m)], links.sibling)
            for p in theirs
        ]
        yield
        for p, slot in zip(theirs, slots):
            links.arrive(got.at[:, rows_at(p * 2 * m, 2 * m)], slot)
    else:
        ready()

    add_into(grad.at[:, rows_at(c * 8 * m, 8 * m)], got)
    def held(p, h):
        return grad.at[:, rows_at(row(c, p, h), m)]

    yield from ring_steps(links, held, held, near, far, y, links.y_plus, links.y_minus)
    yield from swap_steps(links, held, y, other, zh, links.z_rep)
    piece = held(y, zh)

    def strip(yy, hh, n):
        return out.at[rows_at(row(c, yy, hh), n)]

    def forward(yy, hh, n, device):
        return links.send(strip(yy, hh, n), strip(yy, hh, n), device)

    mine = strip(y, zh, m)
    if count == 1:
        links.arrive(mine, links.move(piece.at[0], mine))
    else:
        waits = exchange_columns(links, piece, out, row(c, y, zh), m, cols)
        yield
        for slot, dst in waits:
            links.arrive(dst, slot)
    a = forward(y, zh, m, links.z_rep)
    yield
    links.arrive(mine, a)
    e0 = forward(y, 0, 2 * m, links.y_plus)
    e1 = forward(y, 0, 2 * m, links.y_minus)
    given = [(forward(y, 0, 2 * m, links.sibling), 2 * m)]
    yield
    behind, ahead, across = lax.rem(y + 3, 4), lax.rem(y + 1, 4), lax.rem(y + 2, 4)
    links.arrive(strip(behind, 0, 2 * m), e0)
    f0 = forward(behind, 0, m, links.y_plus)
    given.append((forward(behind, 0, 2 * m, links.sibling), 2 * m))
    links.arrive(strip(ahead, 0, 2 * m), e1)
    f1 = forward(ahead, 1, m, links.y_minus)
    given.append((forward(ahead, 0, 2 * m, links.sibling), 2 * m))
    yield
    links.arrive(mine, f0)
    given.append((forward(across, 0, m, links.sibling), m))
    links.arrive(mine, f1)
    given.append((forward(across, 1, m, links.sibling), m))
    yield
    for slot, n in given:
        links.arrive(strip(y, 0, n), slot)


def vector_job(links, source, out, parts, acc, slots_y, other):
    a = links.move(source.at[links.shard], parts.at[links.shard])
    waits = [
        links.send(source.at[links.peer(k)], parts.at[links.shard], (links.rep, links.peer(k)))
        for k in range(1, 8)
    ]
    yield
    links.arrive(parts.at[0], a)
    for slot in waits:
        links.arrive(parts.at[0], slot)
    value = parts[0]
    for s in range(1, 8):
        value = value + parts[s]
    acc[0] = value
    a = links.send(acc.at[0], other.at[0], links.sibling)
    yield
    links.arrive(other.at[0], a)
    acc[1] = acc[0] + other[0]
    a = links.send(acc.at[1], other.at[1], links.z_rep)
    yield
    links.arrive(other.at[1], a)
    acc[2] = acc[1] + other[1]
    slots_y[links.y] = acc[2]
    there = slots_y.at[links.y]
    waits = [links.send(acc.at[2], there, d) for d in (links.y_plus, links.y_minus, links.y_far)]
    yield
    for slot in waits:
        links.arrive(there, slot)
    out[...] = (slots_y[0] + slots_y[1]) + (slots_y[2] + slots_y[3])


def step(*jobs):
    for job in jobs:
        next(job, None)


def run_jobs(*jobs):
    jobs = list(jobs)
    while jobs:
        jobs = [job for job in jobs if next(job, True) is None]


N_SEMS = 320
BACKWARD_ORDER = (
    "S0", "S1", "*lead", "out", "*sl1", "*sl2", "S1", "*ag", "*D", "D", "*E0", "E0", "D", "S0",
    "out", "S1", "*E1", "E1", "D", "E0", "S0", "*at1", "E1", "D", "S1", "*at2", "S0", "E1", "*key",
    "*A0", "A0", "E0", "D", "out", "A0", "E1", "*A1", "A1", "E0", "*A2", "A2", "A0", "A1", "*in1",
    "A2", "A0", "A1", "E0", "*in2", "in0", "A2", "D", "out", "A1", "*in3", "A2", "E1", "A0", "S0",
    "E0", "A1", "*in4", "in1", "A2", "in0", "S1", "S0", "*v", "vec", "E1", "D", "A0", "S0", "A1",
    "E0", "S1", "in1", "D", "E0", "S0", "D", "E1", "S1", "S0", "S1", "A0", "A2", "E1", "E0", "in0",
    "A1", "E0", "vec", "vec", "A2", "E1", "E0", "in1", "A0", "E1", "A1", "in0", "vec", "A2", "A0",
    "A0", "A1", "vec", "A1", "A2", "in1", "A2",
)
Z_FIRST = ("S0", "E0")
FORWARD_ORDER = (
    "E", "V", "X", "A", "*t1", "*t2", "E", "V", "X", "X", "*n0", "E", "A", "E", "E", "X", "C",
    "*e0", "A", "*nm", "*nq", "X", "*em", "*eq", "*n2", "A", "C", "A", "*e2", "*p", "C", "*a0",
    "*a1", "*a2", "C", "*s3", "C", "*s2",
)


def follow(order, tasks, jobs):
    for name in order:
        if name[0] == "*":
            tasks[name[1:]]()
        else:
            next(jobs[name], None)
    run_jobs(*jobs.values())

ANY = pl.BlockSpec(memory_space=pl.ANY)
VMEM = pl.BlockSpec(memory_space=pltpu.VMEM)
SMEM = pl.BlockSpec(memory_space=pltpu.SMEM)


def sems(n):
    return [pltpu.SemaphoreType.DMA((n,)), pltpu.SemaphoreType.DMA((n,))]


def shape(*dims, kind=BF):
    return jax.ShapeDtypeStruct(dims, kind)


def small_job(links, small, out):
    slots = [links.send(small, out.at[links.shard], (links.rep, links.peer(k))) for k in range(1, 8)]
    slots.append(links.move(small, out.at[links.shard]))
    yield
    for slot in slots:
        links.arrive(out.at[0], slot)


def forward_kernel(
    tok, cot_own, we_own, wa_own, wd_in, ws_in, g_a, s_a, g_f, s_f, b_d, b_s, b_a, b_e, source, lengths,
    x_out, we_out, wa_out, cot_all, attend_out, feed_out, slope_out, q_out, k_out, v_out,
    prob_out, mixed_out, part_out, shrink_out, shrink_got, stats_out, vec_out, cosine, sine,
    send_sems, recv_sems, x, we3, wa3, wd, ws, attend_in, feed_in, act, slope, q, k, v, prob, mixed, part,
    cot, g_shrink, small, small_all, src, begin, total,
):
    links = Links(send_sems, recv_sems)
    own = links.shard
    small[...] = jnp.zeros((16, 256), F32)
    row = 0
    for ref in (g_a, s_a, g_f, s_f, b_d, b_s, b_a, b_e):
        for first in range(0, ref.shape[0], 256):
            small[row : row + 1, :] = ref[pl.ds(first, 256)].astype(F32).reshape(1, 256)
            row += 1
    links.greet(
        [(links.rep, links.peer(p)) for p in range(1, 8)]
        + [links.sibling, links.y_plus, links.y_minus]
    )
    expand = weight_job(links, we_own, we3, [(0, 0, FF_DEV, FF_DEV)])
    attend = weight_job(links, wa_own, wa3, [(p * HD, p * D, HD, HD) for p in range(3)])
    gather_x = token_gather_job(links, tok, x, 64)
    gather_cot = token_gather_job(links, cot_own, cot, 96)
    vectors = small_job(links, small, small_all)
    loads = []
    saves = []
    kept = {}

    def save(*pairs):
        for a, b in pairs:
            saves.append((links.move(a, b), b))

    def table_task(h):
        def run():
            if h == 0:
                loads.extend([links.move(wd_in, wd), links.move(ws_in, ws)])
                src[...] = jnp.broadcast_to(source[...].astype(F32), (128, GROUP)).T

            def tile(i, rows):
                here = src[rows, :]
                first = jnp.zeros_like(here)
                start = jnp.int32(0)
                for j in range(3):
                    start = start + lengths[0, j]
                    edge = start.astype(F32)
                    first = jnp.where(here >= edge, edge, first)
                begin[rows, :] = first
                lane = lax.broadcasted_iota(jnp.int32, here.shape, 1)
                pair = lax.rem(lane, ROT // 2).astype(F32)
                angle = (here - first) * jnp.exp(pair * (-2.0 * 9.210340371976184 / ROT))
                cosine[rows, :] = jnp.where(lane < ROT, jnp.cos(angle), 1.0)
                turned = jnp.sin(angle)
                sine[rows, :] = jnp.where(lane < ROT // 2, -turned, jnp.where(lane < ROT, turned, 0.0))

            span(2 * h, 2 * h + 2, 256, tile)

        return run

    def pair_rows(hop, first, count):
        return rows_at(lax.rem(links.x + hop, 4) * 256 + first, count)

    def norm_task(hop):
        def run():
            if hop == 0:
                for s in range(8):
                    vec_out[:, s * 256 : (s + 1) * 256] = small_all[s, 0:8, :]
                pieces = []
                for p in range(3):
                    block = p * 8 + own
                    pieces.append(small_all[lax.div(block, 3), pl.ds(6 + lax.rem(block, 3), 1), :])
                kept["attend"] = jnp.concatenate(pieces, axis=1)
                kept["expand"] = jnp.concatenate([small_all[own, 9 + p : 10 + p, :] for p in range(4)], axis=1)

            def tile(i, carry):
                rows = pair_rows(hop, i * 128, 128)
                values = x[rows, :].astype(F32)
                mean = jnp.mean(values, axis=1, keepdims=True)
                center = values - mean
                inv = lax.rsqrt(jnp.mean(center * center, axis=1, keepdims=True) + EPSILON)
                normed = center * inv
                attend_in[rows, :] = (normed * vec_out[0:1, :] + vec_out[1:2, :]).astype(BF)
                feed_in[rows, :] = (normed * vec_out[2:3, :] + vec_out[3:4, :]).astype(BF)
                lane = lax.broadcasted_iota(jnp.int32, (128, 128), 1)
                stats_out[rows, :] = jnp.where(lane == 0, mean, inv)
                return carry

            lax.fori_loop(0, 2, tile, 0)
            if hop == 2:
                save((x, x_out), (attend_in, attend_out), (feed_in, feed_out))

        return run

    we, wa = we3.reshape(D, FF_DEV), wa3.reshape(D, 3 * HD)

    def expand_task(hop):
        def run():
            if hop == 0:
                save((we3, we_out))
            rows = pair_rows(hop, 0, 256)
            pre = dot(feed_in[rows, :], we[...], NN) + kept["expand"]
            below = 0.5 * (1.0 + lax.erf(pre * (0.5 ** 0.5)))
            act[rows, :] = (pre * below).astype(BF)
            density = jnp.exp(-0.5 * pre * pre) * 0.3989422804014327
            slope[rows, :] = (below + pre * density).astype(BF)
            if hop == 2:
                save((slope, slope_out))

        return run

    def shrink_task(hops):
        def run():
            pairs = [pair_rows(hop, 0, 256) for hop in hops]
            for rows in pairs:
                save((cot.at[rows], cot_all.at[rows]))

            def tile(i, here):
                for half in range(2):
                    cols = pl.ds(half * 1024, 1024)
                    value = dot(act[pairs[0], here], cot[pairs[0], cols], TN)
                    for rows in pairs[1:]:
                        value = value + dot(act[rows, here], cot[rows, cols], TN)
                    if len(pairs) > 1:
                        total[here, cols] = value
                    else:
                        g_shrink[0, here, cols] = (total[here, cols] + value).astype(BF)

            if len(pairs) > 1:
                tiles(FF_DEV, 256, tile)
                return
            for i in range(4):
                half = 1 - links.c if i < 2 else links.c
                here = pl.ds(pl.multiple_of(half * 512 + i % 2 * 256, 256), 256)
                tile(i, here)
                place = pl.ds(i % 2 * 256, 256)
                if i < 2:
                    slot = links.send(g_shrink.at[0, here], shrink_got.at[0, place], links.sibling)
                    saves.append((slot, shrink_got.at[0, place]))
                else:
                    save((g_shrink.at[0, here], shrink_out.at[0, place]))

        return run

    def project_task():
        save((wa3, wa_out))

        def tile(i, rows):
            triple = dot(attend_in[rows, :], wa[...], NN) + kept["attend"]
            cos, sin = cosine[rows, :], sine[rows, :]
            q[rows, :] = (turn(triple[:, :HD], cos, sin) * INV_ROOT).astype(BF)
            k[rows, :] = turn(triple[:, HD : 2 * HD], cos, sin).astype(BF)
            v[rows, :] = triple[:, 2 * HD :].astype(BF)

        tiles(GROUP, 256, tile)
        save((q, q_out), (k, k_out), (v, v_out))

    def attention_rows(rows):
        key_src = source[...].astype(F32)
        scores = dot(q[rows, :], k[...], NT)
        visible = (key_src >= begin[rows, 0:1]) & (key_src <= src[rows, 0:1])
        scores = jnp.where(visible, scores, NEG_FILL)
        weights = jnp.exp(scores - jnp.max(scores, axis=1, keepdims=True))
        return (weights * (1.0 / jnp.sum(weights, axis=1, keepdims=True))).astype(BF)

    def mix_rows(rows, weights):
        prob[rows, :] = weights
        mixed[rows, :] = dot(weights, v[...], NN).astype(BF)

    def out_rows(rows):
        total = dot(act[rows, :], ws[...], NN) + dot(mixed[rows, :], wd[...], NN)
        part[rows, :] = total.astype(BF)

    def attention_first():
        links.arrive(wd, loads[0])
        links.arrive(ws, loads[1])
        rows = pl.ds(0, 256)
        mix_rows(rows, attention_rows(rows))

    def attention_next():
        def tile(i, rows):
            weights = attention_rows(rows)
            out_rows(pl.ds(pl.multiple_of(i * 256 - 256, 256), 256))
            mix_rows(rows, weights)

        span(1, 4, 256, tile)
        save((prob, prob_out), (mixed, mixed_out))

    def out_last():
        out_rows(pl.ds(768, 256))
        save((part, part_out))

    tasks = {
        "t1": table_task(0), "t2": table_task(1), "p": project_task,
        "a0": attention_first, "a1": attention_next, "a2": out_last,
    }
    tasks["s3"] = shrink_task((0, 3, 1))
    tasks["s2"] = shrink_task((2,))
    for hop, name in ((0, "0"), (3, "m"), (1, "q"), (2, "2")):
        tasks["n" + name] = norm_task(hop)
        tasks["e" + name] = expand_task(hop)
    follow(FORWARD_ORDER, tasks, {"E": expand, "A": attend, "X": gather_x, "C": gather_cot, "V": vectors})
    for slot, ref in saves:
        links.arrive(ref, slot)
    links.close()


def forward(*args):
    big, wide, head = (GROUP, D), (GROUP, FF_DEV), (GROUP, HD)
    table = shape(GROUP, 128, kind=F32)
    return pl.pallas_call(
        forward_kernel,
        out_shape=(
            shape(*big), shape(8, 256, FF_DEV), shape(8, 256, 3 * HD), shape(*big),
            shape(*big), shape(*big), shape(*wide),
            shape(*head), shape(*head), shape(*head), shape(GROUP, GROUP), shape(*head), shape(*big),
            shape(1, 512, D), shape(1, 512, D), table, shape(8, D, kind=F32), table, table,
        ),
        in_specs=[ANY] * 6 + [VMEM] * 9 + [SMEM],
        out_specs=[ANY] * 15 + [VMEM] * 4,
        scratch_shapes=sems(N_SEMS)
        + [
            pltpu.VMEM(dims, BF)
            for dims in (
                big, (8, 256, FF_DEV), (8, 256, 3 * HD), (HD, D), (FF_DEV, D), big, big, wide, wide,
                head, head, head, (GROUP, GROUP), head, big, big, (1, FF_DEV, D),
            )
        ]
        + [
            pltpu.VMEM((16, 256), F32),
            pltpu.VMEM((8, 16, 256), F32),
            pltpu.VMEM((GROUP, 128), F32),
            pltpu.VMEM((GROUP, 128), F32),
            pltpu.VMEM((FF_DEV, D), F32),
        ],
        compiler_params=pltpu.CompilerParams(
            collective_id=0, has_side_effects=True, vmem_limit_bytes=62 << 20
        ),
        name="forward",
    )(*args)


def backward_kernel(
    cot_in, shrink_in, shrink_got, slope_in, feed_in, attend_in, x_in, q_in, k_in, v_in, prob_in, mixed_in, part_in,
    we_in, wa_in, wd_in, ws_in, vec, stats, cosine, sine,
    o_shrink, o_expand0, o_expand1, o_attend, o_dense, r_out, r_in, o_vec,
    send_sems, recv_sems,
    rows_buf, we, norm_buf, act_buf, eg, wa, wd, q, k, v, prob, mixed, out_strips,
    g_shrink, g_expand, g_attend, g_dense, ag, tg, sums, vec_parts, *scratch,
):
    links = Links(send_sems, recv_sems)
    take = iter(scratch)

    def grab(n):
        return [next(take) for _ in range(n)]

    def load(*pairs):
        return [(links.move(a, b), b) for a, b in pairs]

    def ready(loads):
        for slot, ref in loads:
            links.arrive(ref, slot)

    half = rows_at(links.c * 512, 512)
    shrink_scratch = [grab(4), grab(4)]
    loads = {}
    for h in range(2):
        cols = pl.ds(h * 1024, 1024)
        loads["S%d" % h] = load(
            (shrink_in.at[:, :, cols], g_shrink.at[:, half, cols]), (shrink_got.at[:, :, cols], shrink_scratch[h][0])
        )
    links.greet(
        [(links.rep, links.peer(p)) for p in range(1, 8)]
        + [links.sibling, links.z_rep, links.y_plus, links.y_minus, links.y_far]
    )
    cot = rows_buf.at[0]
    jobs = {}
    for h in range(2):
        cols = pl.ds(h * 1024, 1024)
        jobs["S%d" % h] = (grad_job, grad_job_z)["S%d" % h in Z_FIRST](
            links, g_shrink.at[:, :, cols], o_shrink.at[:, cols], None, 64, *shrink_scratch[h],
            lambda h=h: ready(loads["S%d" % h]),
        )
    for h, out in ((0, o_expand0), (1, o_expand1)):
        jobs["E%d" % h] = (grad_job, grad_job_z)["E%d" % h in Z_FIRST](
            links, g_expand.at[:, :, pl.ds(h * 512, 512)], out, [(0, 0, 512, 512)], 16, *grab(4)
        )
    for p in range(3):
        jobs["A%d" % p] = grad_job(
            links, g_attend.at[:, :, pl.ds(p * HD, HD)], o_attend.at[:, pl.ds(p * D, D)],
            [(0, 0, HD, HD)], 16, *grab(4)
        )
    jobs["D"] = grad_job(links, g_dense, o_dense, None, 16, *grab(4))
    jobs["out"] = token_scatter_job(links, part_in, out_strips, r_out, *grab(3))
    for h in range(2):
        cols = pl.ds(h * 1024, 1024)
        jobs["in%d" % h] = token_scatter_job(
            links, rows_buf.at[:, :, cols], None, r_in.at[:, :, cols], *grab(3)
        )
    ones = jnp.ones((8, GROUP), BF)

    kept = {}

    def lead_task():
        loads["second"] = load((cot_in, rows_buf.at[0]), (slope_in, eg), (ws_in, norm_buf))

    def slope_task(h):
        def run():
            if h == 0:
                ready(loads["second"])
                loads["third"] = load((wd_in, wd), (mixed_in, mixed))
                loads["fourth"] = load((q_in, q), (k_in, k), (v_in, v), (prob_in, prob))

            def tile(i, rows):
                grad = dot(cot[rows, :], norm_buf[...], NT)
                eg[rows, :] = (grad * eg[rows, :].astype(F32)).astype(BF)

            span(2 * h, 2 * h + 2, 256, tile)
            if h == 1:
                loads["feed"] = load((feed_in, norm_buf))

        return run

    def attended_task():
        ready(loads["third"])

        def tile(i, rows):
            ag[rows, :] = dot(cot[rows, :], wd[...], NT).astype(BF)

        tiles(GROUP, 256, tile)

    def dense_task():
        for half in range(2):
            cols = pl.ds(half * 1024, 1024)
            g_dense[0, :, cols] = dot(mixed[...], cot[:, cols], TN).astype(BF)
        sums[4:5, :] = dot(ones, cot[...], NN)[0:1]
        loads["x"] = load((x_in, cot), (we_in, we), (wa_in, wa))

    def expand_task(h):
        def run():
            if h == 0:
                ready(loads["feed"])
            cols = pl.ds(h * 512, 512)

            def tile(i, rows):
                s = i * 2
                both = dot(norm_buf[:, rows], eg[:, cols], TN).astype(BF)
                g_expand[s, :, cols] = both[:256]
                g_expand[s + 1, :, cols] = both[256:]

            tiles(D, 512, tile)
            if h == 1:
                loads["attend"] = load((attend_in, norm_buf))
                kept["expand"] = dot(ones, eg[...], NN)[0:1]

        return run

    def attention_task(h):
        def run():
            if h == 0:
                ready(loads["fourth"])

            def tile(i, rows):
                grad = dot(ag[rows, :], v[...], NT)
                weights = prob[rows, :].astype(F32)
                inner = jnp.sum(weights * grad, axis=1, keepdims=True)
                score_grad = (weights * (grad - inner)).astype(BF)
                act_buf[rows, :] = score_grad
                query_grad = dot(score_grad, k[...], NN) * INV_ROOT
                tg[rows, 0:HD] = turn(query_grad, cosine[rows, :], -sine[rows, :]).astype(BF)

            span(4 * h, 4 * h + 4, 128, tile)

        return run

    def key_task():
        def tile(i, rows):
            key_grad = dot(act_buf[:, rows], q[...], TN)
            tg[rows, HD : 2 * HD] = turn(key_grad, cosine[rows, :], -sine[rows, :]).astype(BF)
            tg[rows, 2 * HD :] = dot(prob[:, rows], ag[...], TN).astype(BF)

        tiles(GROUP, 256, tile)

    def attend_task(p):
        def run():
            if p == 0:
                ready(loads["attend"])
            cols = pl.ds(p * HD, HD)

            def tile(i, rows):
                s = i * 2
                both = dot(norm_buf[:, rows], tg[:, cols], TN).astype(BF)
                g_attend[s, :, cols] = both[:256]
                g_attend[s + 1, :, cols] = both[256:]

            tiles(D, 512, tile)
            if p == 2:
                kept["attend"] = dot(ones, tg[...], NN)[0:1]

        return run

    def input_task(h):
        def run():
            if h == 0:
                ready(loads["x"])
                sums[0:4, :] = jnp.zeros((4, D), F32)

            def tile(i, carry):
                rows = pl.ds(pl.multiple_of((h % 2 * 2 + i // 2) * 256, 256), 256)
                cols = pl.ds(pl.multiple_of((h // 2 * 2 + lax.rem(i, 2)) * 512, 512), 512)
                normed = (cot[rows, cols].astype(F32) - stats[rows, 0:1]) * stats[rows, 1:2]
                grad = dot(tg[rows, :], wa[cols, :], NT)
                sums[0:1, cols] += jnp.sum(grad * normed, axis=0, keepdims=True)
                sums[1:2, cols] += jnp.sum(grad, axis=0, keepdims=True)
                combined = grad * vec[0:1, cols]
                grad = dot(eg[rows, :], we[cols, :], NT)
                sums[2:3, cols] += jnp.sum(grad * normed, axis=0, keepdims=True)
                sums[3:4, cols] += jnp.sum(grad, axis=0, keepdims=True)
                cot[rows, cols] = (combined + grad * vec[2:3, cols]).astype(BF)
                return carry

            lax.fori_loop(0, 4, tile, 0)

        return run

    def vector_task():
        own = links.shard
        for s in range(8):
            vec_parts[s] = jnp.zeros((16, 256), F32)
        for p in range(3):
            block = p * 8 + own
            vec_parts[lax.div(block, 3), pl.ds(lax.rem(block, 3), 1), :] = kept["attend"][:, p * HD : (p + 1) * HD]
        for p in range(4):
            vec_parts[own, 3 + p : 4 + p, :] = kept["expand"][:, p * 256 : (p + 1) * 256]
        for s in range(8):
            vec_parts[s, 7:11, :] = sums[0:4, s * 256 : (s + 1) * 256]
        vec_parts[own, 11:12, :] = sums[4:5, pl.ds(pl.multiple_of(own * 256, 256), 256)]

    jobs["vec"] = vector_job(links, vec_parts, o_vec, *grab(4))
    tasks = {
        "lead": lead_task, "sl1": slope_task(0), "sl2": slope_task(1),
        "ag": attended_task, "D": dense_task, "E0": expand_task(0), "E1": expand_task(1),
        "at1": attention_task(0), "at2": attention_task(1), "key": key_task,
        "A0": attend_task(0), "A1": attend_task(1), "A2": attend_task(2),
        "in1": input_task(0), "in2": input_task(1), "in3": input_task(2), "in4": input_task(3),
        "v": vector_task,
    }
    follow(BACKWARD_ORDER, tasks, jobs)
    links.close()


def grad_scratch(s, m, n, name=""):
    dims = ((2, s, 2, m, n), (2, s, m, n), (s, m, n))
    if name in Z_FIRST:
        dims = ((2, s, 2, m, n // 2), (2, s, m, n // 2), (s, 4, m, n))
    return [pltpu.VMEM((s, 8 * m, n), BF)] + [pltpu.VMEM(d, BF) for d in dims]


def token_scratch(width):
    return [
        pltpu.VMEM((2, 1, 2, ROWS, width), BF),
        pltpu.VMEM((2, 1, ROWS, width), BF),
        pltpu.VMEM((1, ROWS, width), BF),
    ]


def backward(*args):
    big, wide, head = (GROUP, D), (GROUP, FF_DEV), (GROUP, HD)
    return pl.pallas_call(
        backward_kernel,
        out_shape=(
            shape(FF_DEV, D), shape(256, 8 * 512), shape(256, 8 * 512), shape(256, 3 * D), shape(256, D),
            shape(1, ROWS, D), shape(1, ROWS, D), shape(16, 256, kind=F32),
        ),
        in_specs=[ANY] * 17 + [VMEM] * 4,
        out_specs=[ANY] * 7 + [VMEM],
        scratch_shapes=sems(N_SEMS)
        + [
            pltpu.VMEM(dims, BF)
            for dims in (
                (1, *big), (D, FF_DEV), big, wide, wide, (D, 3 * HD), (HD, D),
                head, head, head, (GROUP, GROUP), head, (4, 1, ROWS, D),
                (1, FF_DEV, D), (8, 256, FF_DEV), (8, 256, 3 * HD), (1, 256, D), head, (GROUP, 3 * HD),
            )
        ]
        + [pltpu.VMEM((8, D), F32), pltpu.VMEM((8, 16, 256), F32)]
        + grad_scratch(1, 64, 1024, "S0")
        + grad_scratch(1, 64, 1024, "S1")
        + grad_scratch(8, 16, 512, "E0")
        + grad_scratch(8, 16, 512, "E1")
        + grad_scratch(8, 16, HD) * 3
        + grad_scratch(1, 16, D)
        + token_scratch(D)
        + token_scratch(1024) * 2
        + [
            pltpu.VMEM((8, 16, 256), F32),
            pltpu.VMEM((3, 16, 256), F32),
            pltpu.VMEM((4, 16, 256), F32),
            pltpu.VMEM((2, 16, 256), F32),
        ],
        compiler_params=pltpu.CompilerParams(
            collective_id=1, has_side_effects=True, vmem_limit_bytes=64 << 20
        ),
        name="backward",
    )(*args)


def finish_kernel(
    shrink, expand0, expand1, attend, dense, branch, combined, tok, cot, vec, sums,
    layer_out, tokens_grad, g_attend, b_attend, g_dense, b_dense, g_expand, b_expand, g_shrink, b_shrink,
    gain_a, shift_a, gain_f, shift_f,
):
    g_shrink[...] = shrink[...].astype(F32)
    for s in range(8):
        for h, half in enumerate((expand0, expand1)):
            g_expand[:, (2 * s + h) * 512 : (2 * s + h + 1) * 512] = half[:, s * 512 : (s + 1) * 512].astype(F32)
    g_attend[...] = attend[...].astype(F32)
    g_dense[...] = dense[...].astype(F32)
    values = tok[...].astype(F32)
    layer_out[...] = (values + branch[0].astype(F32) + vec[4:5, :] + vec[5:6, :]).astype(BF)
    center = values - jnp.mean(values, axis=1, keepdims=True)
    inv = lax.rsqrt(jnp.mean(center * center, axis=1, keepdims=True) + EPSILON)
    normed = center * inv
    grad = combined[0].astype(F32)
    mean = jnp.mean(grad, axis=1, keepdims=True)
    slant = jnp.mean(grad * normed, axis=1, keepdims=True)
    tokens_grad[...] = cot[...].astype(F32) + (grad - mean - normed * slant) * inv

    @pl.when(pl.program_id(0) == 0)
    def _():
        for ref, first in ((b_attend, 0), (b_expand, 3), (gain_a, 7), (shift_a, 8), (gain_f, 9), (shift_f, 10),
                           (b_dense, 11), (b_shrink, 11)):
            for i in range(ref.shape[0] // 256):
                ref[pl.ds(i * 256, 256)] = sums[first + i : first + i + 1, :].reshape(256)


def finish(*args):
    steps = 2

    def rows(n, width):
        return pl.BlockSpec((n // steps, width), lambda i: (i, 0))

    def part(n, width):
        return pl.BlockSpec((1, n // steps, width), lambda i: (0, i, 0))

    def whole(*dims):
        return pl.BlockSpec(dims, lambda i: (0,) * len(dims))

    weights = [rows(256, 3 * D), rows(256, D), rows(256, 8 * FF_DEV), rows(FF_DEV, D)]
    return pl.pallas_call(
        finish_kernel,
        grid=(steps,),
        out_shape=(
            shape(ROWS, D), shape(ROWS, D, kind=F32),
            shape(256, 3 * D, kind=F32), shape(768, kind=F32), shape(256, D, kind=F32), shape(256, kind=F32),
            shape(256, 8 * FF_DEV, kind=F32), shape(1024, kind=F32), shape(FF_DEV, D, kind=F32),
            *[shape(256, kind=F32)] * 5,
        ),
        in_specs=[weights[3], rows(256, 4096), rows(256, 4096), weights[0], weights[1], part(ROWS, D), part(ROWS, D)]
        + [rows(ROWS, D)] * 2
        + [whole(8, D), whole(16, 256)],
        out_specs=[
            rows(ROWS, D), rows(ROWS, D), weights[0], whole(768), weights[1], whole(256), weights[2],
            whole(1024), weights[3], *[whole(256)] * 5,
        ],
        compiler_params=pltpu.CompilerParams(vmem_limit_bytes=60 << 20),
        name="finish",
    )(*args)


def per_device(
    tokens,
    out_cotangent,
    attend_weight,
    attend_bias,
    dense_weight,
    dense_bias,
    expand_weight,
    expand_bias,
    shrink_weight,
    shrink_bias,
    attend_gain,
    attend_shift,
    feed_gain,
    feed_shift,
    lengths,
    slot_source,
):
    (
        x, we, wa, cot, attend_in, feed_in, slope, q, k, v, prob, mixed, part, shrink, shrink_got,
        stats, vec, cosine, sine,
    ) = forward(
        tokens, out_cotangent, expand_weight, attend_weight, dense_weight, shrink_weight,
        attend_gain, attend_shift, feed_gain, feed_shift, dense_bias, shrink_bias, attend_bias, expand_bias,
        slot_source, lengths,
    )
    we, wa = we.reshape(D, FF_DEV), wa.reshape(D, 3 * HD)
    (shrink_sum, expand0, expand1, attend_sum, dense_sum, branch_sum, own_combined, sums) = backward(
        cot, shrink, shrink_got, slope, feed_in, attend_in, x, q, k, v, prob, mixed, part.reshape(1, GROUP, D),
        we, wa, dense_weight, shrink_weight, vec, stats, cosine, sine,
    )
    return tuple(
        finish(
            shrink_sum, expand0, expand1, attend_sum, dense_sum, branch_sum, own_combined,
            tokens, out_cotangent, vec, sums,
        )
    )


def solution(mesh):
    rows, split, whole = P(("rep", "shard"), None), P("shard"), P("shard", None)
    return jax.shard_map(
        per_device,
        mesh=mesh,
        in_specs=(rows, rows)
        + (whole, split) * 4
        + (split,) * 4
        + (P("rep", None), P("rep", None)),
        out_specs=(rows, rows) + (whole, split) * 4 + (split,) * 4,
        check_vma=False,
    )
```

```python
import jax
import jax.numpy as jnp
from jax import lax
from jax.experimental import pallas as pl
from jax.experimental.pallas import tpu as pltpu
from jax.sharding import PartitionSpec as P

D = 2048
HD = 256
ROT = 64
FF_DEV = 1024
ROWS = 128
GROUP = 1024
EPSILON = 1e-05
NEG_FILL = -1e30
MESH = pl.DeviceIdType.MESH
BF = jnp.bfloat16
F32 = jnp.float32
NN = (((1,), (0,)), ((), ()))
NT = (((1,), (1,)), ((), ()))
TN = (((0,), (0,)), ((), ()))
INV_ROOT = HD ** (-0.5)


def dot(a, b, dims):
    return lax.dot_general(a, b, dims, preferred_element_type=F32)


def span(lo, hi, size, body):
    def step(i, carry):
        body(i, pl.ds(pl.multiple_of(i * size, size), size))
        return carry

    lax.fori_loop(lo, hi, step, 0)


def rows_at(start, count):
    return pl.ds(pl.multiple_of(start, 16), count)


def tiles(total, size, body):
    span(0, total // size, size, body)


def turn(values, cosine, sine):
    first = values[:, :128]
    lane = lax.broadcasted_iota(jnp.int32, first.shape, 1)
    swapped = jnp.where(lane < ROT // 2, pltpu.roll(first, 128 - ROT // 2, 1), pltpu.roll(first, ROT // 2, 1))
    return jnp.concatenate([first * cosine + swapped * sine, values[:, 128:]], axis=1)


class Links:
    def __init__(self, send_sems, recv_sems):
        self.rep, self.shard = lax.axis_index("rep"), lax.axis_index("shard")
        rep, shard = self.rep, self.shard
        self.y, self.zh, self.c = rep // 4, lax.rem(rep // 2, 2), lax.rem(rep, 2)
        self.x, self.zl = shard // 2, lax.rem(shard, 2)
        self.sibling = (self.y * 4 + self.zh * 2 + (1 - self.c), shard)
        self.z_rep = (self.y * 4 + (1 - self.zh) * 2 + self.c, shard)
        self.y_plus, self.y_minus, self.y_far = self.at_y(1), self.at_y(3), self.at_y(2)
        self.x_plus, self.x_minus = self.at_x(1), self.at_x(3)
        self.z_shard = (rep, self.x * 2 + (1 - self.zl))
        self.send_sems, self.recv_sems, self.used, self.open = send_sems, recv_sems, 0, []

    def at_y(self, step):
        return (lax.rem(self.y + step, 4) * 4 + self.zh * 2 + self.c, self.shard)

    def at_x(self, step):
        return (self.rep, lax.rem(self.x + step, 4) * 2 + self.zl)

    def peer(self, k):
        return lax.rem(self.shard + k, 8)

    def greet(self, devices, meanwhile=None):
        barrier = pltpu.get_barrier_semaphore()
        for device in devices:
            pl.semaphore_signal(barrier, inc=1, device_id=device, device_id_type=MESH)
        if meanwhile is not None:
            meanwhile()
        pl.semaphore_wait(barrier, len(devices))

    def send(self, src, dst, device):
        slot = self.used
        self.used += 1
        copy = pltpu.make_async_remote_copy(
            src_ref=src, dst_ref=dst, send_sem=self.send_sems.at[slot],
            recv_sem=self.recv_sems.at[slot], device_id=device, device_id_type=MESH,
        )
        copy.start()
        self.open.append(copy)
        return slot

    def move(self, src, dst):
        slot = self.used
        self.used += 1
        copy = pltpu.make_async_copy(src, dst, self.recv_sems.at[slot])
        copy.start()
        return slot

    def arrive(self, ref, slot):
        pltpu.make_async_copy(ref, ref, self.recv_sems.at[slot]).wait()

    def close(self):
        for copy in self.open:
            copy.wait_send()


def add_into(target, *others):
    count, total, width = target.shape
    size = 16
    while total % (2 * size) == 0 and 2 * size * width <= 65536:
        size *= 2

    def body(i, carry):
        rows = rows_at(lax.rem(i, total // size) * size, size)
        j = lax.div(i, total // size)
        value = target[j, rows, :].astype(F32)
        for other in others:
            value = value + other[j, rows, :].astype(F32)
        target[j, rows, :] = value.astype(BF)
        return carry

    lax.fori_loop(0, count * (total // size), body, 0)


def ring_steps(links, strip, local, near, far, pos, plus, minus):
    ahead, behind, across = lax.rem(pos + 1, 4), lax.rem(pos + 3, 4), lax.rem(pos + 2, 4)
    a = links.send(strip(across, 0), far.at[0], minus)
    b = links.send(strip(across, 1), far.at[1], plus)
    c0 = links.send(strip(behind, 1), near.at[0, :, 1], minus)
    c1 = links.send(strip(ahead, 0), near.at[1, :, 0], plus)
    yield
    links.arrive(far.at[0], a)
    below, above = local(behind, 0), local(ahead, 1)
    add_into(below, far.at[0])
    d0 = links.send(below, near.at[0, :, 0], minus)
    links.arrive(far.at[1], b)
    add_into(above, far.at[1])
    d1 = links.send(above, near.at[1, :, 1], plus)
    yield
    links.arrive(near.at[0, :, 1], c0)
    links.arrive(near.at[1, :, 0], c1)
    links.arrive(near.at[0, :, 0], d0)
    links.arrive(near.at[1, :, 1], d1)
    for h in range(2):
        add_into(local(pos, h), near.at[0, :, h], near.at[1, :, h])


def swap_steps(links, local, pos, other, index, partner):
    a = links.send(local(pos, 1 - index), other, partner)
    yield
    links.arrive(other, a)
    add_into(local(pos, index), other)


def token_scatter_job(links, source, mine, out, near, far, other):
    x, zl = links.x, links.zl

    def strip(p, h):
        return source.at[:, rows_at((p * 2 + h) * ROWS, ROWS)]

    local = strip
    if mine is not None:
        ahead, behind = lax.rem(x + 1, 4), lax.rem(x + 3, 4)
        places = [(behind, 0), (ahead, 1), (x, 0), (x, 1)]
        slots = [links.move(strip(*place), mine.at[i]) for i, place in enumerate(places)]

        def local(p, h):
            if p is x:
                return mine.at[2 + h]
            return mine.at[h]

    ring = ring_steps(links, strip, local, near, far, x, links.x_plus, links.x_minus)
    next(ring)
    yield
    if mine is not None:
        for i, slot in enumerate(slots):
            links.arrive(mine.at[i], slot)
    yield from ring
    yield from swap_steps(links, local, x, other, zl, links.z_shard)
    links.arrive(out, links.move(local(x, zl), out))


def token_gather_job(links, own, out, low_rows):
    mine = links.shard * ROWS
    nl, nh = low_rows, ROWS - low_rows
    z, xp, xm = links.z_shard, links.x_plus, links.x_minus

    def part(shard, first, count):
        return out.at[rows_at(shard * ROWS + first, count)]

    def forward(shard, first, count, device):
        return links.send(part(shard, first, count), part(shard, first, count), device)

    def near(step, flip):
        zl = 1 - links.zl if flip else links.zl
        return lax.rem(links.x + step, 4) * 2 + zl

    behind, ahead, across = near(3, False), near(1, False), near(2, False)
    behind_z, ahead_z, across_z, own_z = near(3, True), near(1, True), near(2, True), near(0, True)
    low, high = pl.ds(0, nl), pl.ds(nl, nh)
    z_low = links.send(own.at[low], part(links.shard, 0, nl), z)
    p_low = links.send(own.at[low], part(links.shard, 0, nl), xp)
    m_low = links.send(own.at[low], part(links.shard, 0, nl), xm)
    p_high = links.send(own.at[high], part(links.shard, nl, nh), xp)
    m_high = links.send(own.at[high], part(links.shard, nl, nh), xm)
    z_high = links.send(own.at[high], part(links.shard, nl, nh), z)
    kept = links.move(own, out.at[rows_at(mine, ROWS)])
    yield
    links.arrive(out.at[rows_at(mine, ROWS)], kept)
    links.arrive(part(own_z, 0, nl), z_low)
    p_z = forward(own_z, 0, nl, xp)
    m_z = forward(own_z, 0, nl, xm)
    links.arrive(part(behind, 0, nl), p_low)
    p_far0 = forward(behind, 0, nl // 2, xp)
    links.arrive(part(ahead, 0, nl), m_low)
    m_far0 = forward(ahead, nl // 2, nl // 2, xm)
    yield
    links.arrive(part(own_z, nl, nh), z_high)
    links.arrive(part(behind, nl, nh), p_high)
    z_behind = forward(behind, nl, nh, z)
    p_far1 = forward(behind, nl, nh // 2, xp)
    links.arrive(part(ahead, nl, nh), m_high)
    z_ahead = forward(ahead, nl, nh, z)
    m_far1 = forward(ahead, nl + nh // 2, nh // 2, xm)
    yield
    links.arrive(part(behind_z, 0, nl), p_z)
    p_far2 = forward(behind_z, 0, nl // 2, xp)
    links.arrive(part(ahead_z, 0, nl), m_z)
    m_far2 = forward(ahead_z, nl // 2, nl // 2, xm)
    links.arrive(part(across, nl, nh // 2), p_far1)
    z_far0 = forward(across, nl, nh // 2, z)
    links.arrive(part(across, nl + nh // 2, nh // 2), m_far1)
    z_far1 = forward(across, nl + nh // 2, nh // 2, z)
    links.arrive(part(behind_z, nl, nh), z_behind)
    links.arrive(part(ahead_z, nl, nh), z_ahead)
    yield
    links.arrive(part(across, 0, nl // 2), p_far0)
    links.arrive(part(across, nl // 2, nl // 2), m_far0)
    links.arrive(part(across_z, 0, nl // 2), p_far2)
    links.arrive(part(across_z, nl // 2, nl // 2), m_far2)
    links.arrive(part(across_z, nl, nh // 2), z_far0)
    links.arrive(part(across_z, nl + nh // 2, nh // 2), z_far1)


def weight_job(links, weight, out, spans):
    piece = rows_at((links.y * 2 + links.c) * 32, 32)
    arrivals = []
    for k in range(8):
        target = links.peer(k)
        for to, first, stride, width in spans:
            cols = pl.ds(pl.multiple_of(first + target * stride, 256), width)
            src, dst = weight.at[piece, cols], out.at[links.shard, piece, pl.ds(to, width)]
            slot = links.send(src, dst, (links.rep, target)) if k else links.move(src, dst)
            arrivals.append((slot, to, width))
    yield
    for slot, to, width in arrivals:
        links.arrive(out.at[0, piece, pl.ds(to, width)], slot)

    def strip(step, first, count):
        return out.at[:, rows_at((lax.rem(links.y + step, 4) * 2 + links.c) * 32 + first, count)]

    def forward(step, first, count, device):
        return links.send(strip(step, first, count), strip(step, first, count), device)

    plus = forward(0, 0, 32, links.y_plus)
    minus = forward(0, 0, 32, links.y_minus)
    given = [(forward(0, 0, 32, links.sibling), 32)]
    yield
    links.arrive(strip(3, 0, 32), plus)
    far0 = forward(3, 0, 16, links.y_plus)
    given.append((forward(3, 0, 32, links.sibling), 32))
    links.arrive(strip(1, 0, 32), minus)
    far1 = forward(1, 16, 16, links.y_minus)
    given.append((forward(1, 0, 32, links.sibling), 32))
    yield
    links.arrive(strip(2, 0, 16), far0)
    given.append((forward(2, 0, 16, links.sibling), 16))
    links.arrive(strip(2, 16, 16), far1)
    given.append((forward(2, 16, 16, links.sibling), 16))
    yield
    for slot, count in given:
        links.arrive(strip(0, 0, count), slot)


def exchange_columns(links, held, out, row, m, cols):
    waits = []
    for k in range(8):
        target = links.peer(k)
        for first, start, stride, width in cols:
            there = pl.ds(pl.multiple_of(start + links.shard * stride, 256), width)
            src = held.at[target, :, pl.ds(first, width)]
            dst = out.at[rows_at(row, m), there]
            slot = links.send(src, dst, (links.rep, target)) if k else links.move(src, dst)
            waits.append((slot, dst))
    return waits


def grad_job_z(links, grad, out, cols, m, got, near, far, other, ready=None):
    c, y, zh = links.c, links.y, links.zh
    count, _, width = grad.shape
    half, out_half = width // 2, out.shape[1] // 2

    def row(cc, yy, hh):
        return (cc * 8 + yy * 2 + hh) * m

    theirs = [lax.rem(y + step, 4) for step in (2, 1, 3, 0)]
    if ready is None:
        slots = [
            links.send(grad.at[:, rows_at(row(1 - c, p, 0), 2 * m)], got.at[:, rows_at(p * 2 * m, 2 * m)], links.sibling)
            for p in theirs
        ]
        yield
        for p, slot in zip(theirs, slots):
            links.arrive(got.at[:, rows_at(p * 2 * m, 2 * m)], slot)
    else:
        ready()
    add_into(grad.at[:, rows_at(c * 8 * m, 8 * m)], got)

    def held(p, h):
        return grad.at[:, rows_at(row(c, p, h), m)]

    slots = [links.send(held(p, 1 - zh), other.at[:, p], links.z_rep) for p in theirs]
    yield
    for p, slot in zip(theirs, slots):
        links.arrive(other.at[:, p], slot)
        add_into(held(p, zh), other.at[:, p])

    def side(p, h):
        return grad.at[:, rows_at(row(c, p, zh), m), pl.ds(h * half, half)]

    yield from ring_steps(links, side, side, near, far, y, links.y_plus, links.y_minus)

    def strip(yy, hh, n):
        return out.at[rows_at(row(c, yy, hh), n)]

    def forward(yy, hh, n, device):
        return links.send(strip(yy, hh, n), strip(yy, hh, n), device)

    def out_side(yy, h):
        return out.at[rows_at(row(c, yy, zh), m), pl.ds(h * out_half, out_half)]

    mine = strip(y, zh, m)
    if count == 1:
        links.arrive(mine, links.move(held(y, zh).at[0], mine))
    else:
        waits = exchange_columns(links, held(y, zh), out, row(c, y, zh), m, cols)
        yield
        for slot, dst in waits:
            links.arrive(dst, slot)
    e0 = forward(y, zh, m, links.y_plus)
    e1 = forward(y, zh, m, links.y_minus)
    za = forward(y, zh, m, links.z_rep)
    yield
    behind, ahead, across = lax.rem(y + 3, 4), lax.rem(y + 1, 4), lax.rem(y + 2, 4)
    links.arrive(strip(behind, zh, m), e0)
    f0 = links.send(out_side(behind, 0), out_side(behind, 0), links.y_plus)
    zb0 = forward(behind, zh, m, links.z_rep)
    links.arrive(strip(ahead, zh, m), e1)
    f1 = links.send(out_side(ahead, 1), out_side(ahead, 1), links.y_minus)
    zb1 = forward(ahead, zh, m, links.z_rep)
    yield
    links.arrive(out_side(across, 0), f0)
    links.arrive(out_side(across, 1), f1)
    zc = forward(across, zh, m, links.z_rep)
    links.arrive(strip(y, 1 - zh, m), za)
    given = [forward(y, 0, 2 * m, links.sibling)]
    yield
    links.arrive(strip(behind, 1 - zh, m), zb0)
    given.append(forward(behind, 0, 2 * m, links.sibling))
    links.arrive(strip(ahead, 1 - zh, m), zb1)
    given.append(forward(ahead, 0, 2 * m, links.sibling))
    yield
    links.arrive(strip(across, 1 - zh, m), zc)
    given.append(forward(across, 0, 2 * m, links.sibling))
    yield
    for slot in given:
        links.arrive(strip(y, 0, 2 * m), slot)


def grad_job(links, grad, out, cols, m, got, near, far, other, ready=None):
    c, y, zh = links.c, links.y, links.zh
    count = grad.shape[0]

    def row(cc, yy, hh):
        return (cc * 8 + yy * 2 + hh) * m

    theirs = [lax.rem(y + step, 4) for step in (2, 1, 3, 0)]
    if ready is None:
        slots = [
            links.send(grad.at[:, rows_at(row(1 - c, p, 0), 2 * m)], got.at[:, rows_at(p * 2 * m, 2 * m)], links.sibling)
            for p in theirs
        ]
        yield
        for p, slot in zip(theirs, slots):
            links.arrive(got.at[:, rows_at(p * 2 * m, 2 * m)], slot)
    else:
        ready()

    add_into(grad.at[:, rows_at(c * 8 * m, 8 * m)], got)
    def held(p, h):
        return grad.at[:, rows_at(row(c, p, h), m)]

    yield from ring_steps(links, held, held, near, far, y, links.y_plus, links.y_minus)
    yield from swap_steps(links, held, y, other, zh, links.z_rep)
    piece = held(y, zh)

    def strip(yy, hh, n):
        return out.at[rows_at(row(c, yy, hh), n)]

    def forward(yy, hh, n, device):
        return links.send(strip(yy, hh, n), strip(yy, hh, n), device)

    mine = strip(y, zh, m)
    if count == 1:
        links.arrive(mine, links.move(piece.at[0], mine))
    else:
        waits = exchange_columns(links, piece, out, row(c, y, zh), m, cols)
        yield
        for slot, dst in waits:
            links.arrive(dst, slot)
    a = forward(y, zh, m, links.z_rep)
    yield
    links.arrive(mine, a)
    e0 = forward(y, 0, 2 * m, links.y_plus)
    e1 = forward(y, 0, 2 * m, links.y_minus)
    given = [(forward(y, 0, 2 * m, links.sibling), 2 * m)]
    yield
    behind, ahead, across = lax.rem(y + 3, 4), lax.rem(y + 1, 4), lax.rem(y + 2, 4)
    links.arrive(strip(behind, 0, 2 * m), e0)
    f0 = forward(behind, 0, m, links.y_plus)
    given.append((forward(behind, 0, 2 * m, links.sibling), 2 * m))
    links.arrive(strip(ahead, 0, 2 * m), e1)
    f1 = forward(ahead, 1, m, links.y_minus)
    given.append((forward(ahead, 0, 2 * m, links.sibling), 2 * m))
    yield
    links.arrive(mine, f0)
    given.append((forward(across, 0, m, links.sibling), m))
    links.arrive(mine, f1)
    given.append((forward(across, 1, m, links.sibling), m))
    yield
    for slot, n in given:
        links.arrive(strip(y, 0, n), slot)


def vector_job(links, source, out, parts, acc, slots_y, other):
    a = links.move(source.at[links.shard], parts.at[links.shard])
    waits = [
        links.send(source.at[links.peer(k)], parts.at[links.shard], (links.rep, links.peer(k)))
        for k in range(1, 8)
    ]
    yield
    links.arrive(parts.at[0], a)
    for slot in waits:
        links.arrive(parts.at[0], slot)
    value = parts[0]
    for s in range(1, 8):
        value = value + parts[s]
    acc[0] = value
    a = links.send(acc.at[0], other.at[0], links.sibling)
    yield
    links.arrive(other.at[0], a)
    acc[1] = acc[0] + other[0]
    a = links.send(acc.at[1], other.at[1], links.z_rep)
    yield
    links.arrive(other.at[1], a)
    acc[2] = acc[1] + other[1]
    slots_y[links.y] = acc[2]
    there = slots_y.at[links.y]
    waits = [links.send(acc.at[2], there, d) for d in (links.y_plus, links.y_minus, links.y_far)]
    yield
    for slot in waits:
        links.arrive(there, slot)
    out[...] = (slots_y[0] + slots_y[1]) + (slots_y[2] + slots_y[3])


def step(*jobs):
    for job in jobs:
        next(job, None)


def run_jobs(*jobs):
    jobs = list(jobs)
    while jobs:
        jobs = [job for job in jobs if next(job, True) is None]


N_SEMS = 320
BACKWARD_ORDER = (
    "S0", "S1", "*lead", "out", "*sl1", "S0", "*sl2", "*ag", "S1", "*D", "D", "*E0", "E0", "D",
    "out", "S0", "*E1", "E1", "E0", "D", "S1", "*at1", "E1", "D", "S0", "*at2", "*key", "E1", "*A0",
    "A0", "E0", "*A1", "A1", "A0", "S1", "E1", "A1", "E0", "out", "D", "A0", "*A2", "A2", "S1",
    "A1", "*in1", "A2", "A0", "E0", "E1", "*in2", "in0", "S1", "*in3", "A2", "A1", "E0", "out", "D",
    "A0", "in0", "A2", "A1", "E1", "S0", "S1", "*in4", "in1", "A2", "E0", "S1", "*v", "vec", "A0",
    "D", "E1", "in0", "A1", "E0", "D", "E0", "S0", "D", "A0", "in1", "E1", "in0", "A1", "S0", "A2",
    "A0", "E0", "S0", "vec", "vec", "E0", "E1", "A2", "E1", "A1", "vec", "in1", "A0", "A0", "A2",
    "A1", "vec", "A1", "A2", "in1", "A2",
)
Z_FIRST = ("E0",)
FORWARD_ORDER = (
    "E", "V", "X", "A", "*t1", "*t2", "E", "V", "X", "X", "*n0", "E", "A", "E", "E", "X", "C",
    "*e0", "A", "*nm", "*nq", "X", "*em", "*eq", "*n2", "A", "C", "A", "*e2", "*p", "C", "*a0",
    "*a1", "*a2", "C", "*s3", "C", "*s2",
)


def follow(order, tasks, jobs):
    for name in order:
        if name[0] == "*":
            tasks[name[1:]]()
        else:
            next(jobs[name], None)
    run_jobs(*jobs.values())

ANY = pl.BlockSpec(memory_space=pl.ANY)
VMEM = pl.BlockSpec(memory_space=pltpu.VMEM)
SMEM = pl.BlockSpec(memory_space=pltpu.SMEM)


def sems(n):
    return [pltpu.SemaphoreType.DMA((n,)), pltpu.SemaphoreType.DMA((n,))]


def shape(*dims, kind=BF):
    return jax.ShapeDtypeStruct(dims, kind)


def small_job(links, small, out):
    slots = [links.send(small, out.at[links.shard], (links.rep, links.peer(k))) for k in range(1, 8)]
    slots.append(links.move(small, out.at[links.shard]))
    yield
    for slot in slots:
        links.arrive(out.at[0], slot)


def forward_kernel(
    tok, cot_own, we_own, wa_own, wd_in, ws_in, g_a, s_a, g_f, s_f, b_d, b_s, b_a, b_e, source, lengths,
    x_out, we_out, wa_out, cot_all, attend_out, feed_out, slope_out, q_out, k_out, v_out,
    prob_out, mixed_out, part_out, shrink_out, shrink_got, stats_keep, vec_keep, cosine_keep, sine_keep,
    send_sems, recv_sems, x, we3, wa3, wd, ws, attend_in, feed_in, act, slope, q, k, v, prob, mixed, part,
    cot, g_shrink, small, small_all, src, begin, total, stats_out, vec_out, cosine, sine,
):
    links = Links(send_sems, recv_sems)
    own = links.shard
    def pack():
        small[...] = jnp.zeros((16, 256), F32)
        row = 0
        for ref in (g_a, s_a, g_f, s_f, b_d, b_s, b_a, b_e):
            for first in range(0, ref.shape[0], 256):
                small[row : row + 1, :] = ref[pl.ds(first, 256)].astype(F32).reshape(1, 256)
                row += 1

    links.greet(
        [(links.rep, links.peer(p)) for p in range(1, 8)]
        + [links.sibling, links.y_plus, links.y_minus],
        pack,
    )
    expand = weight_job(links, we_own, we3, [(0, 0, FF_DEV, FF_DEV)])
    attend = weight_job(links, wa_own, wa3, [(p * HD, p * D, HD, HD) for p in range(3)])
    gather_x = token_gather_job(links, tok, x, 64)
    gather_cot = token_gather_job(links, cot_own, cot, 96)
    vectors = small_job(links, small, small_all)
    loads = []
    saves = []
    kept = {}

    def save(*pairs):
        for a, b in pairs:
            saves.append((links.move(a, b), b))

    def table_task(h):
        def run():
            if h == 0:
                loads.extend([links.move(wd_in, wd), links.move(ws_in, ws)])
                src[...] = jnp.broadcast_to(source[...].astype(F32), (128, GROUP)).T

            def tile(i, rows):
                here = src[rows, :]
                first = jnp.zeros_like(here)
                start = jnp.int32(0)
                for j in range(3):
                    start = start + lengths[0, j]
                    edge = start.astype(F32)
                    first = jnp.where(here >= edge, edge, first)
                begin[rows, :] = first
                lane = lax.broadcasted_iota(jnp.int32, here.shape, 1)
                pair = lax.rem(lane, ROT // 2).astype(F32)
                angle = (here - first) * jnp.exp(pair * (-2.0 * 9.210340371976184 / ROT))
                cosine[rows, :] = jnp.where(lane < ROT, jnp.cos(angle), 1.0)
                turned = jnp.sin(angle)
                sine[rows, :] = jnp.where(lane < ROT // 2, -turned, jnp.where(lane < ROT, turned, 0.0))

            span(2 * h, 2 * h + 2, 256, tile)
            if h == 1:
                save((cosine, cosine_keep), (sine, sine_keep))

        return run

    def pair_rows(hop, first, count):
        return rows_at(lax.rem(links.x + hop, 4) * 256 + first, count)

    def norm_task(hop):
        def run():
            if hop == 0:
                for s in range(8):
                    vec_out[:, s * 256 : (s + 1) * 256] = small_all[s, 0:8, :]
                pieces = []
                for p in range(3):
                    block = p * 8 + own
                    pieces.append(small_all[lax.div(block, 3), pl.ds(6 + lax.rem(block, 3), 1), :])
                kept["attend"] = jnp.concatenate(pieces, axis=1)
                kept["expand"] = jnp.concatenate([small_all[own, 9 + p : 10 + p, :] for p in range(4)], axis=1)

            def tile(i, carry):
                rows = pair_rows(hop, i * 128, 128)
                values = x[rows, :].astype(F32)
                mean = jnp.mean(values, axis=1, keepdims=True)
                center = values - mean
                inv = lax.rsqrt(jnp.mean(center * center, axis=1, keepdims=True) + EPSILON)
                normed = center * inv
                attend_in[rows, :] = (normed * vec_out[0:1, :] + vec_out[1:2, :]).astype(BF)
                feed_in[rows, :] = (normed * vec_out[2:3, :] + vec_out[3:4, :]).astype(BF)
                lane = lax.broadcasted_iota(jnp.int32, (128, 128), 1)
                stats_out[rows, :] = jnp.where(lane == 0, mean, inv)
                return carry

            lax.fori_loop(0, 2, tile, 0)
            if hop == 2:
                save((x, x_out), (attend_in, attend_out), (feed_in, feed_out), (stats_out, stats_keep), (vec_out, vec_keep))

        return run

    we, wa = we3.reshape(D, FF_DEV), wa3.reshape(D, 3 * HD)

    def expand_task(hop):
        def run():
            if hop == 0:
                save((we3, we_out))
            rows = pair_rows(hop, 0, 256)
            pre = dot(feed_in[rows, :], we[...], NN) + kept["expand"]
            below = 0.5 * (1.0 + lax.erf(pre * (0.5 ** 0.5)))
            act[rows, :] = (pre * below).astype(BF)
            density = jnp.exp(-0.5 * pre * pre) * 0.3989422804014327
            slope[rows, :] = (below + pre * density).astype(BF)
            if hop == 2:
                save((slope, slope_out))

        return run

    def shrink_task(hops):
        def run():
            pairs = [pair_rows(hop, 0, 256) for hop in hops]
            for rows in pairs:
                save((cot.at[rows], cot_all.at[rows]))

            def tile(i, here):
                for half in range(2):
                    cols = pl.ds(half * 1024, 1024)
                    value = dot(act[pairs[0], here], cot[pairs[0], cols], TN)
                    for rows in pairs[1:]:
                        value = value + dot(act[rows, here], cot[rows, cols], TN)
                    if len(pairs) > 1:
                        total[here, cols] = value
                    else:
                        g_shrink[0, here, cols] = (total[here, cols] + value).astype(BF)

            if len(pairs) > 1:
                tiles(FF_DEV, 256, tile)
                return
            for i in range(4):
                half = 1 - links.c if i < 2 else links.c
                here = pl.ds(pl.multiple_of(half * 512 + i % 2 * 256, 256), 256)
                tile(i, here)
                place = pl.ds(i % 2 * 256, 256)
                if i < 2:
                    slot = links.send(g_shrink.at[0, here], shrink_got.at[0, place], links.sibling)
                    saves.append((slot, shrink_got.at[0, place]))
                else:
                    save((g_shrink.at[0, here], shrink_out.at[0, place]))

        return run

    def project_task():
        save((wa3, wa_out))

        def tile(i, rows):
            triple = dot(attend_in[rows, :], wa[...], NN) + kept["attend"]
            cos, sin = cosine[rows, :], sine[rows, :]
            q[rows, :] = (turn(triple[:, :HD], cos, sin) * INV_ROOT).astype(BF)
            k[rows, :] = turn(triple[:, HD : 2 * HD], cos, sin).astype(BF)
            v[rows, :] = triple[:, 2 * HD :].astype(BF)

        tiles(GROUP, 256, tile)
        save((q, q_out), (k, k_out), (v, v_out))

    def attention_rows(rows):
        key_src = source[...].astype(F32)
        scores = dot(q[rows, :], k[...], NT)
        visible = (key_src >= begin[rows, 0:1]) & (key_src <= src[rows, 0:1])
        scores = jnp.where(visible, scores, NEG_FILL)
        weights = jnp.exp(scores - jnp.max(scores, axis=1, keepdims=True))
        return (weights * (1.0 / jnp.sum(weights, axis=1, keepdims=True))).astype(BF)

    def mix_rows(rows, weights):
        prob[rows, :] = weights
        mixed[rows, :] = dot(weights, v[...], NN).astype(BF)

    def out_rows(rows):
        total = dot(act[rows, :], ws[...], NN) + dot(mixed[rows, :], wd[...], NN)
        part[rows, :] = total.astype(BF)

    def attention_first():
        links.arrive(wd, loads[0])
        links.arrive(ws, loads[1])
        rows = pl.ds(0, 256)
        mix_rows(rows, attention_rows(rows))

    def attention_next():
        def tile(i, rows):
            weights = attention_rows(rows)
            out_rows(pl.ds(pl.multiple_of(i * 256 - 256, 256), 256))
            mix_rows(rows, weights)

        span(1, 4, 256, tile)
        save((prob, prob_out), (mixed, mixed_out))

    def out_last():
        out_rows(pl.ds(768, 256))
        save((part, part_out))

    tasks = {
        "t1": table_task(0), "t2": table_task(1), "p": project_task,
        "a0": attention_first, "a1": attention_next, "a2": out_last,
    }
    tasks["s3"] = shrink_task((0, 3, 1))
    tasks["s2"] = shrink_task((2,))
    for hop, name in ((0, "0"), (3, "m"), (1, "q"), (2, "2")):
        tasks["n" + name] = norm_task(hop)
        tasks["e" + name] = expand_task(hop)
    follow(FORWARD_ORDER, tasks, {"E": expand, "A": attend, "X": gather_x, "C": gather_cot, "V": vectors})
    for slot, ref in saves:
        links.arrive(ref, slot)
    links.close()


def forward(*args):
    big, wide, head = (GROUP, D), (GROUP, FF_DEV), (GROUP, HD)
    table = shape(GROUP, 128, kind=F32)
    return pl.pallas_call(
        forward_kernel,
        out_shape=(
            shape(*big), shape(8, 256, FF_DEV), shape(8, 256, 3 * HD), shape(*big),
            shape(*big), shape(*big), shape(*wide),
            shape(*head), shape(*head), shape(*head), shape(GROUP, GROUP), shape(*head), shape(*big),
            shape(1, 512, D), shape(1, 512, D), table, shape(8, D, kind=F32), table, table,
        ),
        in_specs=[ANY] * 6 + [VMEM] * 9 + [SMEM],
        out_specs=[ANY] * 19,
        scratch_shapes=sems(N_SEMS)
        + [
            pltpu.VMEM(dims, BF)
            for dims in (
                big, (8, 256, FF_DEV), (8, 256, 3 * HD), (HD, D), (FF_DEV, D), big, big, wide, wide,
                head, head, head, (GROUP, GROUP), head, big, big, (1, FF_DEV, D),
            )
        ]
        + [
            pltpu.VMEM((16, 256), F32),
            pltpu.VMEM((8, 16, 256), F32),
            pltpu.VMEM((GROUP, 128), F32),
            pltpu.VMEM((GROUP, 128), F32),
            pltpu.VMEM((FF_DEV, D), F32),
            pltpu.VMEM((GROUP, 128), F32),
            pltpu.VMEM((8, D), F32),
            pltpu.VMEM((GROUP, 128), F32),
            pltpu.VMEM((GROUP, 128), F32),
        ],
        compiler_params=pltpu.CompilerParams(
            collective_id=0, has_side_effects=True, vmem_limit_bytes=62 << 20
        ),
        name="forward",
    )(*args)


def backward_kernel(
    cot_in, shrink_in, shrink_got, slope_in, feed_in, attend_in, x_in, q_in, k_in, v_in, prob_in, mixed_in, part_in,
    we_in, wa_in, wd_in, ws_in, vec_in, stats_in, cosine_in, sine_in,
    o_shrink, o_expand0, o_expand1, o_attend, o_dense, r_out, r_in, o_vec,
    send_sems, recv_sems,
    rows_buf, we, norm_buf, act_buf, eg, wa, wd, q, k, v, prob, mixed, out_strips,
    g_shrink, g_expand, g_attend, g_dense, ag, tg, sums, vec_parts, vec, stats, cosine, sine, *scratch,
):
    links = Links(send_sems, recv_sems)
    take = iter(scratch)

    def grab(n):
        return [next(take) for _ in range(n)]

    def load(*pairs):
        return [(links.move(a, b), b) for a, b in pairs]

    def ready(loads):
        for slot, ref in loads:
            links.arrive(ref, slot)

    half = rows_at(links.c * 512, 512)
    shrink_scratch = [grab(4), grab(4)]
    loads = {}
    for h in range(2):
        cols = pl.ds(h * 1024, 1024)
        loads["S%d" % h] = load(
            (shrink_in.at[:, :, cols], g_shrink.at[:, half, cols]), (shrink_got.at[:, :, cols], shrink_scratch[h][0])
        )
    links.greet(
        [(links.rep, links.peer(p)) for p in range(1, 8)]
        + [links.sibling, links.z_rep, links.y_plus, links.y_minus, links.y_far]
    )
    cot = rows_buf.at[0]
    jobs = {}
    for h in range(2):
        cols = pl.ds(h * 1024, 1024)
        jobs["S%d" % h] = (grad_job, grad_job_z)["S%d" % h in Z_FIRST](
            links, g_shrink.at[:, :, cols], o_shrink.at[:, cols], None, 64, *shrink_scratch[h],
            lambda h=h: ready(loads["S%d" % h]),
        )
    for h, out in ((0, o_expand0), (1, o_expand1)):
        jobs["E%d" % h] = (grad_job, grad_job_z)["E%d" % h in Z_FIRST](
            links, g_expand.at[:, :, pl.ds(h * 512, 512)], out, [(0, 0, 512, 512)], 16, *grab(4)
        )
    for p in range(3):
        jobs["A%d" % p] = grad_job(
            links, g_attend.at[:, :, pl.ds(p * HD, HD)], o_attend.at[:, pl.ds(p * D, D)],
            [(0, 0, HD, HD)], 16, *grab(4)
        )
    jobs["D"] = grad_job(links, g_dense, o_dense, None, 16, *grab(4))
    jobs["out"] = token_scatter_job(links, part_in, out_strips, r_out, *grab(3))
    for h in range(2):
        cols = pl.ds(h * 1024, 1024)
        jobs["in%d" % h] = token_scatter_job(
            links, rows_buf.at[:, :, cols], None, r_in.at[:, :, cols], *grab(3)
        )
    ones = jnp.ones((8, GROUP), BF)

    kept = {}

    def lead_task():
        loads["second"] = load((cot_in, rows_buf.at[0]), (slope_in, eg), (ws_in, norm_buf))
        loads["tables"] = load((vec_in, vec), (stats_in, stats), (cosine_in, cosine), (sine_in, sine))

    def slope_task(h):
        def run():
            if h == 0:
                ready(loads["second"])
                loads["third"] = load((wd_in, wd), (mixed_in, mixed))
                loads["fourth"] = load((q_in, q), (k_in, k), (v_in, v), (prob_in, prob))

            def tile(i, rows):
                grad = dot(cot[rows, :], norm_buf[...], NT)
                eg[rows, :] = (grad * eg[rows, :].astype(F32)).astype(BF)

            span(2 * h, 2 * h + 2, 256, tile)
            if h == 1:
                loads["feed"] = load((feed_in, norm_buf))

        return run

    def attended_task():
        ready(loads["third"])

        def tile(i, rows):
            ag[rows, :] = dot(cot[rows, :], wd[...], NT).astype(BF)

        tiles(GROUP, 256, tile)

    def dense_task():
        for half in range(2):
            cols = pl.ds(half * 1024, 1024)
            g_dense[0, :, cols] = dot(mixed[...], cot[:, cols], TN).astype(BF)
        sums[4:5, :] = dot(ones, cot[...], NN)[0:1]
        loads["x"] = load((x_in, cot), (we_in, we), (wa_in, wa))

    def expand_task(h):
        def run():
            if h == 0:
                ready(loads["feed"])
            cols = pl.ds(h * 512, 512)

            def tile(i, rows):
                s = i * 2
                both = dot(norm_buf[:, rows], eg[:, cols], TN).astype(BF)
                g_expand[s, :, cols] = both[:256]
                g_expand[s + 1, :, cols] = both[256:]

            tiles(D, 512, tile)
            if h == 1:
                loads["attend"] = load((attend_in, norm_buf))
                kept["expand"] = dot(ones, eg[...], NN)[0:1]

        return run

    def attention_task(h):
        def run():
            if h == 0:
                ready(loads["fourth"] + loads["tables"])

            def tile(i, rows):
                grad = dot(ag[rows, :], v[...], NT)
                weights = prob[rows, :].astype(F32)
                inner = jnp.sum(weights * grad, axis=1, keepdims=True)
                score_grad = (weights * (grad - inner)).astype(BF)
                act_buf[rows, :] = score_grad
                query_grad = dot(score_grad, k[...], NN) * INV_ROOT
                tg[rows, 0:HD] = turn(query_grad, cosine[rows, :], -sine[rows, :]).astype(BF)

            span(4 * h, 4 * h + 4, 128, tile)

        return run

    def key_task():
        def tile(i, rows):
            key_grad = dot(act_buf[:, rows], q[...], TN)
            tg[rows, HD : 2 * HD] = turn(key_grad, cosine[rows, :], -sine[rows, :]).astype(BF)
            tg[rows, 2 * HD :] = dot(prob[:, rows], ag[...], TN).astype(BF)

        tiles(GROUP, 256, tile)

    def attend_task(p):
        def run():
            if p == 0:
                ready(loads["attend"])
            cols = pl.ds(p * HD, HD)

            def tile(i, rows):
                s = i * 2
                both = dot(norm_buf[:, rows], tg[:, cols], TN).astype(BF)
                g_attend[s, :, cols] = both[:256]
                g_attend[s + 1, :, cols] = both[256:]

            tiles(D, 512, tile)
            if p == 2:
                kept["attend"] = dot(ones, tg[...], NN)[0:1]

        return run

    def input_task(h):
        def run():
            if h == 0:
                ready(loads["x"])
                sums[0:4, :] = jnp.zeros((4, D), F32)

            def tile(i, carry):
                rows = pl.ds(pl.multiple_of((h % 2 * 2 + i // 2) * 256, 256), 256)
                cols = pl.ds(pl.multiple_of((h // 2 * 2 + lax.rem(i, 2)) * 512, 512), 512)
                normed = (cot[rows, cols].astype(F32) - stats[rows, 0:1]) * stats[rows, 1:2]
                grad = dot(tg[rows, :], wa[cols, :], NT)
                sums[0:1, cols] += jnp.sum(grad * normed, axis=0, keepdims=True)
                sums[1:2, cols] += jnp.sum(grad, axis=0, keepdims=True)
                combined = grad * vec[0:1, cols]
                grad = dot(eg[rows, :], we[cols, :], NT)
                sums[2:3, cols] += jnp.sum(grad * normed, axis=0, keepdims=True)
                sums[3:4, cols] += jnp.sum(grad, axis=0, keepdims=True)
                cot[rows, cols] = (combined + grad * vec[2:3, cols]).astype(BF)
                return carry

            lax.fori_loop(0, 4, tile, 0)

        return run

    def vector_task():
        own = links.shard
        for s in range(8):
            vec_parts[s] = jnp.zeros((16, 256), F32)
        for p in range(3):
            block = p * 8 + own
            vec_parts[lax.div(block, 3), pl.ds(lax.rem(block, 3), 1), :] = kept["attend"][:, p * HD : (p + 1) * HD]
        for p in range(4):
            vec_parts[own, 3 + p : 4 + p, :] = kept["expand"][:, p * 256 : (p + 1) * 256]
        for s in range(8):
            vec_parts[s, 7:11, :] = sums[0:4, s * 256 : (s + 1) * 256]
        vec_parts[own, 11:12, :] = sums[4:5, pl.ds(pl.multiple_of(own * 256, 256), 256)]

    jobs["vec"] = vector_job(links, vec_parts, o_vec, *grab(4))
    tasks = {
        "lead": lead_task, "sl1": slope_task(0), "sl2": slope_task(1),
        "ag": attended_task, "D": dense_task, "E0": expand_task(0), "E1": expand_task(1),
        "at1": attention_task(0), "at2": attention_task(1), "key": key_task,
        "A0": attend_task(0), "A1": attend_task(1), "A2": attend_task(2),
        "in1": input_task(0), "in2": input_task(1), "in3": input_task(2), "in4": input_task(3),
        "v": vector_task,
    }
    follow(BACKWARD_ORDER, tasks, jobs)
    links.close()


def grad_scratch(s, m, n, name=""):
    dims = ((2, s, 2, m, n), (2, s, m, n), (s, m, n))
    if name in Z_FIRST:
        dims = ((2, s, 2, m, n // 2), (2, s, m, n // 2), (s, 4, m, n))
    return [pltpu.VMEM((s, 8 * m, n), BF)] + [pltpu.VMEM(d, BF) for d in dims]


def token_scratch(width):
    return [
        pltpu.VMEM((2, 1, 2, ROWS, width), BF),
        pltpu.VMEM((2, 1, ROWS, width), BF),
        pltpu.VMEM((1, ROWS, width), BF),
    ]


def backward(*args):
    big, wide, head = (GROUP, D), (GROUP, FF_DEV), (GROUP, HD)
    return pl.pallas_call(
        backward_kernel,
        out_shape=(
            shape(FF_DEV, D), shape(256, 8 * 512), shape(256, 8 * 512), shape(256, 3 * D), shape(256, D),
            shape(1, ROWS, D), shape(1, ROWS, D), shape(16, 256, kind=F32),
        ),
        in_specs=[ANY] * 21,
        out_specs=[ANY] * 7 + [VMEM],
        scratch_shapes=sems(N_SEMS)
        + [
            pltpu.VMEM(dims, BF)
            for dims in (
                (1, *big), (D, FF_DEV), big, wide, wide, (D, 3 * HD), (HD, D),
                head, head, head, (GROUP, GROUP), head, (4, 1, ROWS, D),
                (1, FF_DEV, D), (8, 256, FF_DEV), (8, 256, 3 * HD), (1, 256, D), head, (GROUP, 3 * HD),
            )
        ]
        + [pltpu.VMEM((8, D), F32), pltpu.VMEM((8, 16, 256), F32), pltpu.VMEM((8, D), F32)]
        + [pltpu.VMEM((GROUP, 128), F32)] * 3
        + grad_scratch(1, 64, 1024, "S0")
        + grad_scratch(1, 64, 1024, "S1")
        + grad_scratch(8, 16, 512, "E0")
        + grad_scratch(8, 16, 512, "E1")
        + grad_scratch(8, 16, HD) * 3
        + grad_scratch(1, 16, D)
        + token_scratch(D)
        + token_scratch(1024) * 2
        + [
            pltpu.VMEM((8, 16, 256), F32),
            pltpu.VMEM((3, 16, 256), F32),
            pltpu.VMEM((4, 16, 256), F32),
            pltpu.VMEM((2, 16, 256), F32),
        ],
        compiler_params=pltpu.CompilerParams(
            collective_id=1, has_side_effects=True, vmem_limit_bytes=64 << 20
        ),
        name="backward",
    )(*args)


def finish_kernel(
    shrink, expand0, expand1, attend, dense, branch, combined, tok, cot, vec, sums,
    layer_out, tokens_grad, g_attend, b_attend, g_dense, b_dense, g_expand, b_expand, g_shrink, b_shrink,
    gain_a, shift_a, gain_f, shift_f,
):
    g_shrink[...] = shrink[...].astype(F32)
    for s in range(8):
        for h, half in enumerate((expand0, expand1)):
            g_expand[:, (2 * s + h) * 512 : (2 * s + h + 1) * 512] = half[:, s * 512 : (s + 1) * 512].astype(F32)
    g_attend[...] = attend[...].astype(F32)
    g_dense[...] = dense[...].astype(F32)
    values = tok[...].astype(F32)
    layer_out[...] = (values + branch[0].astype(F32) + vec[4:5, :] + vec[5:6, :]).astype(BF)
    center = values - jnp.mean(values, axis=1, keepdims=True)
    inv = lax.rsqrt(jnp.mean(center * center, axis=1, keepdims=True) + EPSILON)
    normed = center * inv
    grad = combined[0].astype(F32)
    mean = jnp.mean(grad, axis=1, keepdims=True)
    slant = jnp.mean(grad * normed, axis=1, keepdims=True)
    tokens_grad[...] = cot[...].astype(F32) + (grad - mean - normed * slant) * inv

    @pl.when(pl.program_id(0) == 0)
    def _():
        for ref, first in ((b_attend, 0), (b_expand, 3), (gain_a, 7), (shift_a, 8), (gain_f, 9), (shift_f, 10),
                           (b_dense, 11), (b_shrink, 11)):
            for i in range(ref.shape[0] // 256):
                ref[pl.ds(i * 256, 256)] = sums[first + i : first + i + 1, :].reshape(256)


def finish(*args):
    steps = 2

    def rows(n, width):
        return pl.BlockSpec((n // steps, width), lambda i: (i, 0))

    def part(n, width):
        return pl.BlockSpec((1, n // steps, width), lambda i: (0, i, 0))

    def whole(*dims):
        return pl.BlockSpec(dims, lambda i: (0,) * len(dims))

    weights = [rows(256, 3 * D), rows(256, D), rows(256, 8 * FF_DEV), rows(FF_DEV, D)]
    return pl.pallas_call(
        finish_kernel,
        grid=(steps,),
        out_shape=(
            shape(ROWS, D), shape(ROWS, D, kind=F32),
            shape(256, 3 * D, kind=F32), shape(768, kind=F32), shape(256, D, kind=F32), shape(256, kind=F32),
            shape(256, 8 * FF_DEV, kind=F32), shape(1024, kind=F32), shape(FF_DEV, D, kind=F32),
            *[shape(256, kind=F32)] * 5,
        ),
        in_specs=[weights[3], rows(256, 4096), rows(256, 4096), weights[0], weights[1], part(ROWS, D), part(ROWS, D)]
        + [rows(ROWS, D)] * 2
        + [whole(8, D), whole(16, 256)],
        out_specs=[
            rows(ROWS, D), rows(ROWS, D), weights[0], whole(768), weights[1], whole(256), weights[2],
            whole(1024), weights[3], *[whole(256)] * 5,
        ],
        compiler_params=pltpu.CompilerParams(vmem_limit_bytes=60 << 20),
        name="finish",
    )(*args)


def per_device(
    tokens,
    out_cotangent,
    attend_weight,
    attend_bias,
    dense_weight,
    dense_bias,
    expand_weight,
    expand_bias,
    shrink_weight,
    shrink_bias,
    attend_gain,
    attend_shift,
    feed_gain,
    feed_shift,
    lengths,
    slot_source,
):
    (
        x, we, wa, cot, attend_in, feed_in, slope, q, k, v, prob, mixed, part, shrink, shrink_got,
        stats, vec, cosine, sine,
    ) = forward(
        tokens, out_cotangent, expand_weight, attend_weight, dense_weight, shrink_weight,
        attend_gain, attend_shift, feed_gain, feed_shift, dense_bias, shrink_bias, attend_bias, expand_bias,
        slot_source, lengths,
    )
    we, wa = we.reshape(D, FF_DEV), wa.reshape(D, 3 * HD)
    (shrink_sum, expand0, expand1, attend_sum, dense_sum, branch_sum, own_combined, sums) = backward(
        cot, shrink, shrink_got, slope, feed_in, attend_in, x, q, k, v, prob, mixed, part.reshape(1, GROUP, D),
        we, wa, dense_weight, shrink_weight, vec, stats, cosine, sine,
    )
    return tuple(
        finish(
            shrink_sum, expand0, expand1, attend_sum, dense_sum, branch_sum, own_combined,
            tokens, out_cotangent, vec, sums,
        )
    )


def solution(mesh):
    rows, split, whole = P(("rep", "shard"), None), P("shard"), P("shard", None)
    return jax.shard_map(
        per_device,
        mesh=mesh,
        in_specs=(rows, rows)
        + (whole, split) * 4
        + (split,) * 4
        + (P("rep", None), P("rep", None)),
        out_specs=(rows, rows) + (whole, split) * 4 + (split,) * 4,
        check_vma=False,
    )
```

```python
import jax
import jax.numpy as jnp
from jax import lax
from jax.experimental import pallas as pl
from jax.experimental.pallas import tpu as pltpu
from jax.sharding import PartitionSpec as P

D = 2048
HD = 256
ROT = 64
FF_DEV = 1024
ROWS = 128
GROUP = 1024
EPSILON = 1e-05
NEG_FILL = -1e30
MESH = pl.DeviceIdType.MESH
BF = jnp.bfloat16
F32 = jnp.float32
NN = (((1,), (0,)), ((), ()))
NT = (((1,), (1,)), ((), ()))
TN = (((0,), (0,)), ((), ()))
INV_ROOT = HD ** (-0.5)


def dot(a, b, dims):
    return lax.dot_general(a, b, dims, preferred_element_type=F32)


def span(lo, hi, size, body):
    def step(i, carry):
        body(i, pl.ds(pl.multiple_of(i * size, size), size))
        return carry

    lax.fori_loop(lo, hi, step, 0)


def rows_at(start, count):
    return pl.ds(pl.multiple_of(start, 16), count)


def tiles(total, size, body):
    span(0, total // size, size, body)


def turn(values, cosine, sine):
    first = values[:, :128]
    lane = lax.broadcasted_iota(jnp.int32, first.shape, 1)
    swapped = jnp.where(lane < ROT // 2, pltpu.roll(first, 128 - ROT // 2, 1), pltpu.roll(first, ROT // 2, 1))
    return jnp.concatenate([first * cosine + swapped * sine, values[:, 128:]], axis=1)


class Links:
    def __init__(self, send_sems, recv_sems):
        self.rep, self.shard = lax.axis_index("rep"), lax.axis_index("shard")
        rep, shard = self.rep, self.shard
        self.y, self.zh, self.c = rep // 4, lax.rem(rep // 2, 2), lax.rem(rep, 2)
        self.x, self.zl = shard // 2, lax.rem(shard, 2)
        self.sibling = (self.y * 4 + self.zh * 2 + (1 - self.c), shard)
        self.z_rep = (self.y * 4 + (1 - self.zh) * 2 + self.c, shard)
        self.y_plus, self.y_minus, self.y_far = self.at_y(1), self.at_y(3), self.at_y(2)
        self.x_plus, self.x_minus = self.at_x(1), self.at_x(3)
        self.z_shard = (rep, self.x * 2 + (1 - self.zl))
        self.send_sems, self.recv_sems, self.used, self.open = send_sems, recv_sems, 0, []

    def at_y(self, step):
        return (lax.rem(self.y + step, 4) * 4 + self.zh * 2 + self.c, self.shard)

    def at_x(self, step):
        return (self.rep, lax.rem(self.x + step, 4) * 2 + self.zl)

    def peer(self, k):
        return lax.rem(self.shard + k, 8)

    def greet(self, devices, meanwhile=None):
        barrier = pltpu.get_barrier_semaphore()
        for device in devices:
            pl.semaphore_signal(barrier, inc=1, device_id=device, device_id_type=MESH)
        if meanwhile is not None:
            meanwhile()
        pl.semaphore_wait(barrier, len(devices))

    def send(self, src, dst, device):
        slot = self.used
        self.used += 1
        copy = pltpu.make_async_remote_copy(
            src_ref=src, dst_ref=dst, send_sem=self.send_sems.at[slot],
            recv_sem=self.recv_sems.at[slot], device_id=device, device_id_type=MESH,
        )
        copy.start()
        self.open.append(copy)
        return slot

    def move(self, src, dst):
        slot = self.used
        self.used += 1
        copy = pltpu.make_async_copy(src, dst, self.recv_sems.at[slot])
        copy.start()
        return slot

    def arrive(self, ref, slot):
        pltpu.make_async_copy(ref, ref, self.recv_sems.at[slot]).wait()

    def close(self):
        for copy in self.open:
            copy.wait_send()


def add_into(target, *others):
    count, total, width = target.shape
    size = 16
    while total % (2 * size) == 0 and 2 * size * width <= 65536:
        size *= 2

    def body(i, carry):
        rows = rows_at(lax.rem(i, total // size) * size, size)
        j = lax.div(i, total // size)
        value = target[j, rows, :].astype(F32)
        for other in others:
            value = value + other[j, rows, :].astype(F32)
        target[j, rows, :] = value.astype(BF)
        return carry

    lax.fori_loop(0, count * (total // size), body, 0)


def ring_steps(links, strip, local, near, far, pos, plus, minus):
    ahead, behind, across = lax.rem(pos + 1, 4), lax.rem(pos + 3, 4), lax.rem(pos + 2, 4)
    a = links.send(strip(across, 0), far.at[0], minus)
    b = links.send(strip(across, 1), far.at[1], plus)
    c0 = links.send(strip(behind, 1), near.at[0, :, 1], minus)
    c1 = links.send(strip(ahead, 0), near.at[1, :, 0], plus)
    yield
    links.arrive(far.at[0], a)
    below, above = local(behind, 0), local(ahead, 1)
    add_into(below, far.at[0])
    d0 = links.send(below, near.at[0, :, 0], minus)
    links.arrive(far.at[1], b)
    add_into(above, far.at[1])
    d1 = links.send(above, near.at[1, :, 1], plus)
    yield
    links.arrive(near.at[0, :, 1], c0)
    links.arrive(near.at[1, :, 0], c1)
    links.arrive(near.at[0, :, 0], d0)
    links.arrive(near.at[1, :, 1], d1)
    for h in range(2):
        add_into(local(pos, h), near.at[0, :, h], near.at[1, :, h])


def swap_steps(links, local, pos, other, index, partner):
    a = links.send(local(pos, 1 - index), other, partner)
    yield
    links.arrive(other, a)
    add_into(local(pos, index), other)


def token_scatter_job(links, source, mine, out, near, far, other):
    x, zl = links.x, links.zl

    def strip(p, h):
        return source.at[:, rows_at((p * 2 + h) * ROWS, ROWS)]

    local = strip
    if mine is not None:
        ahead, behind = lax.rem(x + 1, 4), lax.rem(x + 3, 4)
        places = [(behind, 0), (ahead, 1), (x, 0), (x, 1)]
        slots = [links.move(strip(*place), mine.at[i]) for i, place in enumerate(places)]

        def local(p, h):
            if p is x:
                return mine.at[2 + h]
            return mine.at[h]

    ring = ring_steps(links, strip, local, near, far, x, links.x_plus, links.x_minus)
    next(ring)
    yield
    if mine is not None:
        for i, slot in enumerate(slots):
            links.arrive(mine.at[i], slot)
    yield from ring
    yield from swap_steps(links, local, x, other, zl, links.z_shard)
    links.arrive(out, links.move(local(x, zl), out))


def token_gather_job(links, own, out, low_rows):
    mine = links.shard * ROWS
    nl, nh = low_rows, ROWS - low_rows
    z, xp, xm = links.z_shard, links.x_plus, links.x_minus

    def part(shard, first, count):
        return out.at[rows_at(shard * ROWS + first, count)]

    def forward(shard, first, count, device):
        return links.send(part(shard, first, count), part(shard, first, count), device)

    def near(step, flip):
        zl = 1 - links.zl if flip else links.zl
        return lax.rem(links.x + step, 4) * 2 + zl

    behind, ahead, across = near(3, False), near(1, False), near(2, False)
    behind_z, ahead_z, across_z, own_z = near(3, True), near(1, True), near(2, True), near(0, True)
    low, high = pl.ds(0, nl), pl.ds(nl, nh)
    z_low = links.send(own.at[low], part(links.shard, 0, nl), z)
    p_low = links.send(own.at[low], part(links.shard, 0, nl), xp)
    m_low = links.send(own.at[low], part(links.shard, 0, nl), xm)
    p_high = links.send(own.at[high], part(links.shard, nl, nh), xp)
    m_high = links.send(own.at[high], part(links.shard, nl, nh), xm)
    z_high = links.send(own.at[high], part(links.shard, nl, nh), z)
    kept = links.move(own, out.at[rows_at(mine, ROWS)])
    yield
    links.arrive(out.at[rows_at(mine, ROWS)], kept)
    links.arrive(part(own_z, 0, nl), z_low)
    p_z = forward(own_z, 0, nl, xp)
    m_z = forward(own_z, 0, nl, xm)
    links.arrive(part(behind, 0, nl), p_low)
    p_far0 = forward(behind, 0, nl // 2, xp)
    links.arrive(part(ahead, 0, nl), m_low)
    m_far0 = forward(ahead, nl // 2, nl // 2, xm)
    yield
    links.arrive(part(own_z, nl, nh), z_high)
    links.arrive(part(behind, nl, nh), p_high)
    z_behind = forward(behind, nl, nh, z)
    p_far1 = forward(behind, nl, nh // 2, xp)
    links.arrive(part(ahead, nl, nh), m_high)
    z_ahead = forward(ahead, nl, nh, z)
    m_far1 = forward(ahead, nl + nh // 2, nh // 2, xm)
    yield
    links.arrive(part(behind_z, 0, nl), p_z)
    p_far2 = forward(behind_z, 0, nl // 2, xp)
    links.arrive(part(ahead_z, 0, nl), m_z)
    m_far2 = forward(ahead_z, nl // 2, nl // 2, xm)
    links.arrive(part(across, nl, nh // 2), p_far1)
    z_far0 = forward(across, nl, nh // 2, z)
    links.arrive(part(across, nl + nh // 2, nh // 2), m_far1)
    z_far1 = forward(across, nl + nh // 2, nh // 2, z)
    links.arrive(part(behind_z, nl, nh), z_behind)
    links.arrive(part(ahead_z, nl, nh), z_ahead)
    yield
    links.arrive(part(across, 0, nl // 2), p_far0)
    links.arrive(part(across, nl // 2, nl // 2), m_far0)
    links.arrive(part(across_z, 0, nl // 2), p_far2)
    links.arrive(part(across_z, nl // 2, nl // 2), m_far2)
    links.arrive(part(across_z, nl, nh // 2), z_far0)
    links.arrive(part(across_z, nl + nh // 2, nh // 2), z_far1)


def weight_job(links, weight, out, spans):
    piece = rows_at((links.y * 2 + links.c) * 32, 32)
    arrivals = []
    for k in range(8):
        target = links.peer(k)
        for to, first, stride, width in spans:
            cols = pl.ds(pl.multiple_of(first + target * stride, 256), width)
            src, dst = weight.at[piece, cols], out.at[links.shard, piece, pl.ds(to, width)]
            slot = links.send(src, dst, (links.rep, target)) if k else links.move(src, dst)
            arrivals.append((slot, to, width))
    yield
    for slot, to, width in arrivals:
        links.arrive(out.at[0, piece, pl.ds(to, width)], slot)

    def strip(step, first, count):
        return out.at[:, rows_at((lax.rem(links.y + step, 4) * 2 + links.c) * 32 + first, count)]

    def forward(step, first, count, device):
        return links.send(strip(step, first, count), strip(step, first, count), device)

    plus = forward(0, 0, 32, links.y_plus)
    minus = forward(0, 0, 32, links.y_minus)
    given = [(forward(0, 0, 32, links.sibling), 32)]
    yield
    links.arrive(strip(3, 0, 32), plus)
    far0 = forward(3, 0, 16, links.y_plus)
    given.append((forward(3, 0, 32, links.sibling), 32))
    links.arrive(strip(1, 0, 32), minus)
    far1 = forward(1, 16, 16, links.y_minus)
    given.append((forward(1, 0, 32, links.sibling), 32))
    yield
    links.arrive(strip(2, 0, 16), far0)
    given.append((forward(2, 0, 16, links.sibling), 16))
    links.arrive(strip(2, 16, 16), far1)
    given.append((forward(2, 16, 16, links.sibling), 16))
    yield
    for slot, count in given:
        links.arrive(strip(0, 0, count), slot)


def exchange_columns(links, held, out, row, m, cols):
    waits = []
    for k in range(8):
        target = links.peer(k)
        for first, start, stride, width in cols:
            there = pl.ds(pl.multiple_of(start + links.shard * stride, 256), width)
            src = held.at[target, :, pl.ds(first, width)]
            dst = out.at[rows_at(row, m), there]
            slot = links.send(src, dst, (links.rep, target)) if k else links.move(src, dst)
            waits.append((slot, dst))
    return waits


def grad_job_z(links, grad, out, cols, m, got, near, far, other, ready=None):
    c, y, zh = links.c, links.y, links.zh
    count, _, width = grad.shape
    half, out_half = width // 2, out.shape[1] // 2

    def row(cc, yy, hh):
        return (cc * 8 + yy * 2 + hh) * m

    theirs = [lax.rem(y + step, 4) for step in (2, 1, 3, 0)]
    if ready is None:
        slots = [
            links.send(grad.at[:, rows_at(row(1 - c, p, 0), 2 * m)], got.at[:, rows_at(p * 2 * m, 2 * m)], links.sibling)
            for p in theirs
        ]
        yield
        for p, slot in zip(theirs, slots):
            links.arrive(got.at[:, rows_at(p * 2 * m, 2 * m)], slot)
    else:
        ready()
    add_into(grad.at[:, rows_at(c * 8 * m, 8 * m)], got)

    def held(p, h):
        return grad.at[:, rows_at(row(c, p, h), m)]

    slots = [links.send(held(p, 1 - zh), other.at[:, p], links.z_rep) for p in theirs]
    yield
    for p, slot in zip(theirs, slots):
        links.arrive(other.at[:, p], slot)
        add_into(held(p, zh), other.at[:, p])

    def side(p, h):
        return grad.at[:, rows_at(row(c, p, zh), m), pl.ds(h * half, half)]

    yield from ring_steps(links, side, side, near, far, y, links.y_plus, links.y_minus)

    def strip(yy, hh, n):
        return out.at[rows_at(row(c, yy, hh), n)]

    def forward(yy, hh, n, device):
        return links.send(strip(yy, hh, n), strip(yy, hh, n), device)

    def out_side(yy, h):
        return out.at[rows_at(row(c, yy, zh), m), pl.ds(h * out_half, out_half)]

    mine = strip(y, zh, m)
    if count == 1:
        links.arrive(mine, links.move(held(y, zh).at[0], mine))
    else:
        waits = exchange_columns(links, held(y, zh), out, row(c, y, zh), m, cols)
        yield
        for slot, dst in waits:
            links.arrive(dst, slot)
    e0 = forward(y, zh, m, links.y_plus)
    e1 = forward(y, zh, m, links.y_minus)
    za = forward(y, zh, m, links.z_rep)
    yield
    behind, ahead, across = lax.rem(y + 3, 4), lax.rem(y + 1, 4), lax.rem(y + 2, 4)
    links.arrive(strip(behind, zh, m), e0)
    f0 = links.send(out_side(behind, 0), out_side(behind, 0), links.y_plus)
    zb0 = forward(behind, zh, m, links.z_rep)
    links.arrive(strip(ahead, zh, m), e1)
    f1 = links.send(out_side(ahead, 1), out_side(ahead, 1), links.y_minus)
    zb1 = forward(ahead, zh, m, links.z_rep)
    yield
    links.arrive(out_side(across, 0), f0)
    links.arrive(out_side(across, 1), f1)
    zc = forward(across, zh, m, links.z_rep)
    links.arrive(strip(y, 1 - zh, m), za)
    given = [forward(y, 0, 2 * m, links.sibling)]
    yield
    links.arrive(strip(behind, 1 - zh, m), zb0)
    given.append(forward(behind, 0, 2 * m, links.sibling))
    links.arrive(strip(ahead, 1 - zh, m), zb1)
    given.append(forward(ahead, 0, 2 * m, links.sibling))
    yield
    links.arrive(strip(across, 1 - zh, m), zc)
    given.append(forward(across, 0, 2 * m, links.sibling))
    yield
    for slot in given:
        links.arrive(strip(y, 0, 2 * m), slot)


def grad_job(links, grad, out, cols, m, got, near, far, other, ready=None):
    c, y, zh = links.c, links.y, links.zh
    count = grad.shape[0]

    def row(cc, yy, hh):
        return (cc * 8 + yy * 2 + hh) * m

    theirs = [lax.rem(y + step, 4) for step in (2, 1, 3, 0)]
    if ready is None:
        slots = [
            links.send(grad.at[:, rows_at(row(1 - c, p, 0), 2 * m)], got.at[:, rows_at(p * 2 * m, 2 * m)], links.sibling)
            for p in theirs
        ]
        yield
        for p, slot in zip(theirs, slots):
            links.arrive(got.at[:, rows_at(p * 2 * m, 2 * m)], slot)
    else:
        ready()

    add_into(grad.at[:, rows_at(c * 8 * m, 8 * m)], got)
    def held(p, h):
        return grad.at[:, rows_at(row(c, p, h), m)]

    yield from ring_steps(links, held, held, near, far, y, links.y_plus, links.y_minus)
    yield from swap_steps(links, held, y, other, zh, links.z_rep)
    piece = held(y, zh)

    def strip(yy, hh, n):
        return out.at[rows_at(row(c, yy, hh), n)]

    def forward(yy, hh, n, device):
        return links.send(strip(yy, hh, n), strip(yy, hh, n), device)

    mine = strip(y, zh, m)
    if count == 1:
        links.arrive(mine, links.move(piece.at[0], mine))
    else:
        waits = exchange_columns(links, piece, out, row(c, y, zh), m, cols)
        yield
        for slot, dst in waits:
            links.arrive(dst, slot)
    a = forward(y, zh, m, links.z_rep)
    yield
    links.arrive(mine, a)
    e0 = forward(y, 0, 2 * m, links.y_plus)
    e1 = forward(y, 0, 2 * m, links.y_minus)
    given = [(forward(y, 0, 2 * m, links.sibling), 2 * m)]
    yield
    behind, ahead, across = lax.rem(y + 3, 4), lax.rem(y + 1, 4), lax.rem(y + 2, 4)
    links.arrive(strip(behind, 0, 2 * m), e0)
    f0 = forward(behind, 0, m, links.y_plus)
    given.append((forward(behind, 0, 2 * m, links.sibling), 2 * m))
    links.arrive(strip(ahead, 0, 2 * m), e1)
    f1 = forward(ahead, 1, m, links.y_minus)
    given.append((forward(ahead, 0, 2 * m, links.sibling), 2 * m))
    yield
    links.arrive(mine, f0)
    given.append((forward(across, 0, m, links.sibling), m))
    links.arrive(mine, f1)
    given.append((forward(across, 1, m, links.sibling), m))
    yield
    for slot, n in given:
        links.arrive(strip(y, 0, n), slot)


def vector_job(links, source, out, parts, acc, slots_y, other):
    a = links.move(source.at[links.shard], parts.at[links.shard])
    waits = [
        links.send(source.at[links.peer(k)], parts.at[links.shard], (links.rep, links.peer(k)))
        for k in range(1, 8)
    ]
    yield
    links.arrive(parts.at[0], a)
    for slot in waits:
        links.arrive(parts.at[0], slot)
    value = parts[0]
    for s in range(1, 8):
        value = value + parts[s]
    acc[0] = value
    a = links.send(acc.at[0], other.at[0], links.sibling)
    yield
    links.arrive(other.at[0], a)
    acc[1] = acc[0] + other[0]
    a = links.send(acc.at[1], other.at[1], links.z_rep)
    yield
    links.arrive(other.at[1], a)
    acc[2] = acc[1] + other[1]
    slots_y[links.y] = acc[2]
    there = slots_y.at[links.y]
    waits = [links.send(acc.at[2], there, d) for d in (links.y_plus, links.y_minus, links.y_far)]
    yield
    for slot in waits:
        links.arrive(there, slot)
    parts[0] = (slots_y[0] + slots_y[1]) + (slots_y[2] + slots_y[3])
    links.arrive(out, links.move(parts.at[0], out))


def step(*jobs):
    for job in jobs:
        next(job, None)


def run_jobs(*jobs):
    jobs = list(jobs)
    while jobs:
        jobs = [job for job in jobs if next(job, True) is None]


N_SEMS = 320
BACKWARD_ORDER = (
    "S0", "S1", "*lead", "out", "*sl1", "S0", "*sl2", "*ag", "S1", "*D", "D", "*E0", "E0", "D",
    "out", "S0", "*E1", "E1", "E0", "D", "S1", "*at1", "E1", "D", "S0", "*at2", "*key", "E1", "*A0",
    "A0", "E0", "*A1", "A1", "A0", "S1", "E1", "A1", "E0", "out", "D", "A0", "*A2", "A2", "S1",
    "A1", "*in1", "A2", "A0", "E0", "E1", "*in2", "in0", "S1", "*in3", "A2", "A1", "E0", "out", "D",
    "A0", "in0", "A2", "A1", "E1", "S0", "S1", "*in4", "in1", "A2", "E0", "S1", "*v", "vec", "A0",
    "D", "E1", "in0", "A1", "E0", "D", "E0", "S0", "D", "A0", "in1", "E1", "in0", "A1", "S0", "A2",
    "A0", "E0", "S0", "vec", "vec", "E0", "E1", "A2", "E1", "A1", "vec", "in1", "A0", "A0", "A2",
    "A1", "vec", "A1", "A2", "in1", "A2",
)
Z_FIRST = ("E0",)
FORWARD_ORDER = (
    "E", "V", "X", "A", "*t1", "*t2", "E", "V", "X", "X", "*n0", "E", "A", "E", "E", "X", "C",
    "*e0", "A", "*nm", "*nq", "X", "*em", "*eq", "*n2", "A", "C", "A", "*e2", "*p", "C", "*a0",
    "*a1", "C", "*a2", "*s3", "C", "*s2",
)


def follow(order, tasks, jobs):
    for name in order:
        if name[0] == "*":
            tasks[name[1:]]()
        else:
            next(jobs[name], None)
    run_jobs(*jobs.values())

ANY = pl.BlockSpec(memory_space=pl.ANY)
VMEM = pl.BlockSpec(memory_space=pltpu.VMEM)
SMEM = pl.BlockSpec(memory_space=pltpu.SMEM)


def sems(n):
    return [pltpu.SemaphoreType.DMA((n,)), pltpu.SemaphoreType.DMA((n,))]


def shape(*dims, kind=BF):
    return jax.ShapeDtypeStruct(dims, kind)


def small_job(links, small, out):
    slots = [links.send(small, out.at[links.shard], (links.rep, links.peer(k))) for k in range(1, 8)]
    slots.append(links.move(small, out.at[links.shard]))
    yield
    for slot in slots:
        links.arrive(out.at[0], slot)


def forward_kernel(
    tok, cot_own, we_own, wa_own, wd_in, ws_in, g_a, s_a, g_f, s_f, b_d, b_s, b_a, b_e, source, lengths,
    x_out, we_out, wa_out, cot_all, attend_out, feed_out, slope_out, q_out, k_out, v_out,
    prob_out, mixed_out, part_out, shrink_out, shrink_got, stats_keep, vec_keep, cosine_keep, sine_keep,
    send_sems, recv_sems, x, we3, wa3, wd, ws, attend_in, feed_in, act, slope, q, k, v, prob, mixed, part,
    cot, g_shrink, small, small_all, src, begin, total, stats_out, vec_out, cosine, sine,
):
    links = Links(send_sems, recv_sems)
    own = links.shard
    def pack():
        small[...] = jnp.zeros((16, 256), F32)
        row = 0
        for ref in (g_a, s_a, g_f, s_f, b_d, b_s, b_a, b_e):
            for first in range(0, ref.shape[0], 256):
                small[row : row + 1, :] = ref[pl.ds(first, 256)].astype(F32).reshape(1, 256)
                row += 1

    links.greet(
        [(links.rep, links.peer(p)) for p in range(1, 8)]
        + [links.sibling, links.y_plus, links.y_minus],
        pack,
    )
    expand = weight_job(links, we_own, we3, [(0, 0, FF_DEV, FF_DEV)])
    attend = weight_job(links, wa_own, wa3, [(p * HD, p * D, HD, HD) for p in range(3)])
    gather_x = token_gather_job(links, tok, x, 64)
    gather_cot = token_gather_job(links, cot_own, cot, 96)
    vectors = small_job(links, small, small_all)
    loads = []
    saves = []
    kept = {}

    def save(*pairs):
        for a, b in pairs:
            saves.append((links.move(a, b), b))

    def table_task(h):
        def run():
            if h == 0:
                loads.extend([links.move(wd_in, wd), links.move(ws_in, ws)])
                src[...] = jnp.broadcast_to(source[...].astype(F32), (128, GROUP)).T

            def tile(i, rows):
                here = src[rows, :]
                first = jnp.zeros_like(here)
                start = jnp.int32(0)
                for j in range(3):
                    start = start + lengths[0, j]
                    edge = start.astype(F32)
                    first = jnp.where(here >= edge, edge, first)
                begin[rows, :] = first
                lane = lax.broadcasted_iota(jnp.int32, here.shape, 1)
                pair = lax.rem(lane, ROT // 2).astype(F32)
                angle = (here - first) * jnp.exp(pair * (-2.0 * 9.210340371976184 / ROT))
                cosine[rows, :] = jnp.where(lane < ROT, jnp.cos(angle), 1.0)
                turned = jnp.sin(angle)
                sine[rows, :] = jnp.where(lane < ROT // 2, -turned, jnp.where(lane < ROT, turned, 0.0))

            span(2 * h, 2 * h + 2, 256, tile)
            if h == 1:
                save((cosine, cosine_keep), (sine, sine_keep))

        return run

    def pair_rows(hop, first, count):
        return rows_at(lax.rem(links.x + hop, 4) * 256 + first, count)

    def norm_task(hop):
        def run():
            if hop == 0:
                for s in range(8):
                    vec_out[:, s * 256 : (s + 1) * 256] = small_all[s, 0:8, :]
                pieces = []
                for p in range(3):
                    block = p * 8 + own
                    pieces.append(small_all[lax.div(block, 3), pl.ds(6 + lax.rem(block, 3), 1), :])
                kept["attend"] = jnp.concatenate(pieces, axis=1)
                kept["expand"] = jnp.concatenate([small_all[own, 9 + p : 10 + p, :] for p in range(4)], axis=1)

            def tile(i, carry):
                rows = pair_rows(hop, i * 128, 128)
                values = x[rows, :].astype(F32)
                mean = jnp.mean(values, axis=1, keepdims=True)
                center = values - mean
                inv = lax.rsqrt(jnp.mean(center * center, axis=1, keepdims=True) + EPSILON)
                normed = center * inv
                attend_in[rows, :] = (normed * vec_out[0:1, :] + vec_out[1:2, :]).astype(BF)
                feed_in[rows, :] = (normed * vec_out[2:3, :] + vec_out[3:4, :]).astype(BF)
                lane = lax.broadcasted_iota(jnp.int32, (128, 128), 1)
                stats_out[rows, :] = jnp.where(lane == 0, mean, inv)
                return carry

            lax.fori_loop(0, 2, tile, 0)
            if hop == 2:
                save((x, x_out), (attend_in, attend_out), (feed_in, feed_out), (stats_out, stats_keep), (vec_out, vec_keep))

        return run

    we, wa = we3.reshape(D, FF_DEV), wa3.reshape(D, 3 * HD)

    def expand_task(hop):
        def run():
            if hop == 0:
                save((we3, we_out))
            rows = pair_rows(hop, 0, 256)
            pre = dot(feed_in[rows, :], we[...], NN) + kept["expand"]
            below = 0.5 * (1.0 + lax.erf(pre * (0.5 ** 0.5)))
            act[rows, :] = (pre * below).astype(BF)
            density = jnp.exp(-0.5 * pre * pre) * 0.3989422804014327
            slope[rows, :] = (below + pre * density).astype(BF)
            if hop == 2:
                save((slope, slope_out))

        return run

    def shrink_task(hops):
        def run():
            pairs = [pair_rows(hop, 0, 256) for hop in hops]
            for rows in pairs:
                save((cot.at[rows], cot_all.at[rows]))

            def tile(i, here):
                for half in range(2):
                    cols = pl.ds(half * 1024, 1024)
                    value = dot(act[pairs[0], here], cot[pairs[0], cols], TN)
                    for rows in pairs[1:]:
                        value = value + dot(act[rows, here], cot[rows, cols], TN)
                    if len(pairs) > 1:
                        total[here, cols] = value
                    else:
                        g_shrink[0, here, cols] = (total[here, cols] + value).astype(BF)

            if len(pairs) > 1:
                tiles(FF_DEV, 256, tile)
                return
            for i in range(4):
                half = 1 - links.c if i < 2 else links.c
                here = pl.ds(pl.multiple_of(half * 512 + i % 2 * 256, 256), 256)
                tile(i, here)
                place = pl.ds(i % 2 * 256, 256)
                if i < 2:
                    slot = links.send(g_shrink.at[0, here], shrink_got.at[0, place], links.sibling)
                    saves.append((slot, shrink_got.at[0, place]))
                else:
                    save((g_shrink.at[0, here], shrink_out.at[0, place]))

        return run

    def project_task():
        save((wa3, wa_out))

        def tile(i, rows):
            triple = dot(attend_in[rows, :], wa[...], NN) + kept["attend"]
            cos, sin = cosine[rows, :], sine[rows, :]
            q[rows, :] = (turn(triple[:, :HD], cos, sin) * INV_ROOT).astype(BF)
            k[rows, :] = turn(triple[:, HD : 2 * HD], cos, sin).astype(BF)
            v[rows, :] = triple[:, 2 * HD :].astype(BF)

        tiles(GROUP, 256, tile)
        save((q, q_out), (k, k_out), (v, v_out))

    def attention_rows(rows):
        key_src = source[...].astype(F32)
        scores = dot(q[rows, :], k[...], NT)
        visible = (key_src >= begin[rows, 0:1]) & (key_src <= src[rows, 0:1])
        scores = jnp.where(visible, scores, NEG_FILL)
        weights = jnp.exp(scores - jnp.max(scores, axis=1, keepdims=True))
        return (weights * (1.0 / jnp.sum(weights, axis=1, keepdims=True))).astype(BF)

    def mix_rows(rows, weights):
        prob[rows, :] = weights
        mixed[rows, :] = dot(weights, v[...], NN).astype(BF)

    def out_rows(rows):
        total = dot(act[rows, :], ws[...], NN) + dot(mixed[rows, :], wd[...], NN)
        part[rows, :] = total.astype(BF)

    def attention_first():
        links.arrive(wd, loads[0])
        links.arrive(ws, loads[1])
        rows = pl.ds(0, 256)
        mix_rows(rows, attention_rows(rows))

    def attention_next():
        def tile(i, rows):
            weights = attention_rows(rows)
            out_rows(pl.ds(pl.multiple_of(i * 256 - 256, 256), 256))
            mix_rows(rows, weights)

        span(1, 4, 256, tile)
        save((prob, prob_out), (mixed, mixed_out))

    def out_last():
        out_rows(pl.ds(768, 256))
        save((part, part_out))

    tasks = {
        "t1": table_task(0), "t2": table_task(1), "p": project_task,
        "a0": attention_first, "a1": attention_next, "a2": out_last,
    }
    tasks["s3"] = shrink_task((0, 3, 1))
    tasks["s2"] = shrink_task((2,))
    for hop, name in ((0, "0"), (3, "m"), (1, "q"), (2, "2")):
        tasks["n" + name] = norm_task(hop)
        tasks["e" + name] = expand_task(hop)
    follow(FORWARD_ORDER, tasks, {"E": expand, "A": attend, "X": gather_x, "C": gather_cot, "V": vectors})
    for slot, ref in saves:
        links.arrive(ref, slot)
    links.close()


def forward(*args):
    big, wide, head = (GROUP, D), (GROUP, FF_DEV), (GROUP, HD)
    table = shape(GROUP, 128, kind=F32)
    return pl.pallas_call(
        forward_kernel,
        out_shape=(
            shape(*big), shape(8, 256, FF_DEV), shape(8, 256, 3 * HD), shape(*big),
            shape(*big), shape(*big), shape(*wide),
            shape(*head), shape(*head), shape(*head), shape(GROUP, GROUP), shape(*head), shape(*big),
            shape(1, 512, D), shape(1, 512, D), table, shape(8, D, kind=F32), table, table,
        ),
        in_specs=[ANY] * 6 + [VMEM] * 9 + [SMEM],
        out_specs=[ANY] * 19,
        scratch_shapes=sems(N_SEMS)
        + [
            pltpu.VMEM(dims, BF)
            for dims in (
                big, (8, 256, FF_DEV), (8, 256, 3 * HD), (HD, D), (FF_DEV, D), big, big, wide, wide,
                head, head, head, (GROUP, GROUP), head, big, big, (1, FF_DEV, D),
            )
        ]
        + [
            pltpu.VMEM((16, 256), F32),
            pltpu.VMEM((8, 16, 256), F32),
            pltpu.VMEM((GROUP, 128), F32),
            pltpu.VMEM((GROUP, 128), F32),
            pltpu.VMEM((FF_DEV, D), F32),
            pltpu.VMEM((GROUP, 128), F32),
            pltpu.VMEM((8, D), F32),
            pltpu.VMEM((GROUP, 128), F32),
            pltpu.VMEM((GROUP, 128), F32),
        ],
        compiler_params=pltpu.CompilerParams(
            collective_id=0, has_side_effects=True, vmem_limit_bytes=62 << 20
        ),
        name="forward",
    )(*args)


def backward_kernel(
    cot_in, shrink_in, shrink_got, slope_in, feed_in, attend_in, x_in, q_in, k_in, v_in, prob_in, mixed_in, part_in,
    we_in, wa_in, wd_in, ws_in, vec_in, stats_in, cosine_in, sine_in,
    o_shrink, o_expand0, o_expand1, o_attend, o_dense, r_out, r_in, o_vec,
    send_sems, recv_sems,
    rows_buf, we, norm_buf, act_buf, eg, wa, wd, q, k, v, prob, mixed, out_strips,
    g_shrink, g_expand, g_attend, g_dense, ag, tg, sums, vec_parts, vec, stats, cosine, sine, *scratch,
):
    links = Links(send_sems, recv_sems)
    take = iter(scratch)

    def grab(n):
        return [next(take) for _ in range(n)]

    def load(*pairs):
        return [(links.move(a, b), b) for a, b in pairs]

    def ready(loads):
        for slot, ref in loads:
            links.arrive(ref, slot)

    half = rows_at(links.c * 512, 512)
    shrink_scratch = [grab(4), grab(4)]
    loads = {}
    for h in range(2):
        cols = pl.ds(h * 1024, 1024)
        loads["S%d" % h] = load(
            (shrink_in.at[:, :, cols], g_shrink.at[:, half, cols]), (shrink_got.at[:, :, cols], shrink_scratch[h][0])
        )
    links.greet(
        [(links.rep, links.peer(p)) for p in range(1, 8)]
        + [links.sibling, links.z_rep, links.y_plus, links.y_minus, links.y_far]
    )
    cot = rows_buf.at[0]
    jobs = {}
    for h in range(2):
        cols = pl.ds(h * 1024, 1024)
        jobs["S%d" % h] = (grad_job, grad_job_z)["S%d" % h in Z_FIRST](
            links, g_shrink.at[:, :, cols], o_shrink.at[:, cols], None, 64, *shrink_scratch[h],
            lambda h=h: ready(loads["S%d" % h]),
        )
    for h, out in ((0, o_expand0), (1, o_expand1)):
        jobs["E%d" % h] = (grad_job, grad_job_z)["E%d" % h in Z_FIRST](
            links, g_expand.at[:, :, pl.ds(h * 512, 512)], out, [(0, 0, 512, 512)], 16, *grab(4)
        )
    for p in range(3):
        jobs["A%d" % p] = grad_job(
            links, g_attend.at[:, :, pl.ds(p * HD, HD)], o_attend.at[:, pl.ds(p * D, D)],
            [(0, 0, HD, HD)], 16, *grab(4)
        )
    jobs["D"] = grad_job(links, g_dense, o_dense, None, 16, *grab(4))
    jobs["out"] = token_scatter_job(links, part_in, out_strips, r_out, *grab(3))
    for h in range(2):
        cols = pl.ds(h * 1024, 1024)
        jobs["in%d" % h] = token_scatter_job(
            links, rows_buf.at[:, :, cols], None, r_in.at[:, :, cols], *grab(3)
        )
    ones = jnp.ones((8, GROUP), BF)

    kept = {}

    def lead_task():
        loads["second"] = load((cot_in, rows_buf.at[0]), (slope_in, eg), (ws_in, norm_buf))
        loads["tables"] = load((vec_in, vec), (stats_in, stats), (cosine_in, cosine), (sine_in, sine))

    def slope_task(h):
        def run():
            if h == 0:
                ready(loads["second"])
                loads["third"] = load((wd_in, wd), (mixed_in, mixed))
                loads["fourth"] = load((q_in, q), (k_in, k), (v_in, v), (prob_in, prob))

            def tile(i, rows):
                grad = dot(cot[rows, :], norm_buf[...], NT)
                eg[rows, :] = (grad * eg[rows, :].astype(F32)).astype(BF)

            span(2 * h, 2 * h + 2, 256, tile)
            if h == 1:
                loads["feed"] = load((feed_in, norm_buf))

        return run

    def attended_task():
        ready(loads["third"])

        def tile(i, rows):
            ag[rows, :] = dot(cot[rows, :], wd[...], NT).astype(BF)

        tiles(GROUP, 256, tile)

    def dense_task():
        for half in range(2):
            cols = pl.ds(half * 1024, 1024)
            g_dense[0, :, cols] = dot(mixed[...], cot[:, cols], TN).astype(BF)
        sums[4:5, :] = dot(ones, cot[...], NN)[0:1]
        loads["x"] = load((x_in, cot), (we_in, we), (wa_in, wa))

    def expand_task(h):
        def run():
            if h == 0:
                ready(loads["feed"])
            cols = pl.ds(h * 512, 512)

            def tile(i, rows):
                s = i * 2
                both = dot(norm_buf[:, rows], eg[:, cols], TN).astype(BF)
                g_expand[s, :, cols] = both[:256]
                g_expand[s + 1, :, cols] = both[256:]

            tiles(D, 512, tile)
            if h == 1:
                loads["attend"] = load((attend_in, norm_buf))
                kept["expand"] = dot(ones, eg[...], NN)[0:1]

        return run

    def attention_task(h):
        def run():
            if h == 0:
                ready(loads["fourth"] + loads["tables"])

            def tile(i, rows):
                grad = dot(ag[rows, :], v[...], NT)
                weights = prob[rows, :].astype(F32)
                inner = jnp.sum(weights * grad, axis=1, keepdims=True)
                score_grad = (weights * (grad - inner)).astype(BF)
                act_buf[rows, :] = score_grad
                query_grad = dot(score_grad, k[...], NN) * INV_ROOT
                tg[rows, 0:HD] = turn(query_grad, cosine[rows, :], -sine[rows, :]).astype(BF)

            span(4 * h, 4 * h + 4, 128, tile)

        return run

    def key_task():
        def tile(i, rows):
            key_grad = dot(act_buf[:, rows], q[...], TN)
            tg[rows, HD : 2 * HD] = turn(key_grad, cosine[rows, :], -sine[rows, :]).astype(BF)
            tg[rows, 2 * HD :] = dot(prob[:, rows], ag[...], TN).astype(BF)

        tiles(GROUP, 256, tile)

    def attend_task(p):
        def run():
            if p == 0:
                ready(loads["attend"])
            cols = pl.ds(p * HD, HD)

            def tile(i, rows):
                s = i * 2
                both = dot(norm_buf[:, rows], tg[:, cols], TN).astype(BF)
                g_attend[s, :, cols] = both[:256]
                g_attend[s + 1, :, cols] = both[256:]

            tiles(D, 512, tile)
            if p == 2:
                kept["attend"] = dot(ones, tg[...], NN)[0:1]

        return run

    def input_task(h):
        def run():
            if h == 0:
                ready(loads["x"])
                sums[0:4, :] = jnp.zeros((4, D), F32)

            def tile(i, carry):
                rows = pl.ds(pl.multiple_of((h % 2 * 2 + i // 2) * 256, 256), 256)
                cols = pl.ds(pl.multiple_of((h // 2 * 2 + lax.rem(i, 2)) * 512, 512), 512)
                normed = (cot[rows, cols].astype(F32) - stats[rows, 0:1]) * stats[rows, 1:2]
                grad = dot(tg[rows, :], wa[cols, :], NT)
                sums[0:1, cols] += jnp.sum(grad * normed, axis=0, keepdims=True)
                sums[1:2, cols] += jnp.sum(grad, axis=0, keepdims=True)
                combined = grad * vec[0:1, cols]
                grad = dot(eg[rows, :], we[cols, :], NT)
                sums[2:3, cols] += jnp.sum(grad * normed, axis=0, keepdims=True)
                sums[3:4, cols] += jnp.sum(grad, axis=0, keepdims=True)
                cot[rows, cols] = (combined + grad * vec[2:3, cols]).astype(BF)
                return carry

            lax.fori_loop(0, 4, tile, 0)

        return run

    def vector_task():
        own = links.shard
        for s in range(8):
            vec_parts[s] = jnp.zeros((16, 256), F32)
        for p in range(3):
            block = p * 8 + own
            vec_parts[lax.div(block, 3), pl.ds(lax.rem(block, 3), 1), :] = kept["attend"][:, p * HD : (p + 1) * HD]
        for p in range(4):
            vec_parts[own, 3 + p : 4 + p, :] = kept["expand"][:, p * 256 : (p + 1) * 256]
        for s in range(8):
            vec_parts[s, 7:11, :] = sums[0:4, s * 256 : (s + 1) * 256]
        vec_parts[own, 11:12, :] = sums[4:5, pl.ds(pl.multiple_of(own * 256, 256), 256)]

    jobs["vec"] = vector_job(links, vec_parts, o_vec, *grab(4))
    tasks = {
        "lead": lead_task, "sl1": slope_task(0), "sl2": slope_task(1),
        "ag": attended_task, "D": dense_task, "E0": expand_task(0), "E1": expand_task(1),
        "at1": attention_task(0), "at2": attention_task(1), "key": key_task,
        "A0": attend_task(0), "A1": attend_task(1), "A2": attend_task(2),
        "in1": input_task(0), "in2": input_task(1), "in3": input_task(2), "in4": input_task(3),
        "v": vector_task,
    }
    follow(BACKWARD_ORDER, tasks, jobs)
    links.close()


def grad_scratch(s, m, n, name=""):
    dims = ((2, s, 2, m, n), (2, s, m, n), (s, m, n))
    if name in Z_FIRST:
        dims = ((2, s, 2, m, n // 2), (2, s, m, n // 2), (s, 4, m, n))
    return [pltpu.VMEM((s, 8 * m, n), BF)] + [pltpu.VMEM(d, BF) for d in dims]


def token_scratch(width):
    return [
        pltpu.VMEM((2, 1, 2, ROWS, width), BF),
        pltpu.VMEM((2, 1, ROWS, width), BF),
        pltpu.VMEM((1, ROWS, width), BF),
    ]


def backward(*args):
    big, wide, head = (GROUP, D), (GROUP, FF_DEV), (GROUP, HD)
    return pl.pallas_call(
        backward_kernel,
        out_shape=(
            shape(FF_DEV, D), shape(256, 8 * 512), shape(256, 8 * 512), shape(256, 3 * D), shape(256, D),
            shape(1, ROWS, D), shape(1, ROWS, D), shape(16, 256, kind=F32),
        ),
        in_specs=[ANY] * 21,
        out_specs=[ANY] * 8,
        scratch_shapes=sems(N_SEMS)
        + [
            pltpu.VMEM(dims, BF)
            for dims in (
                (1, *big), (D, FF_DEV), big, wide, wide, (D, 3 * HD), (HD, D),
                head, head, head, (GROUP, GROUP), head, (4, 1, ROWS, D),
                (1, FF_DEV, D), (8, 256, FF_DEV), (8, 256, 3 * HD), (1, 256, D), head, (GROUP, 3 * HD),
            )
        ]
        + [pltpu.VMEM((8, D), F32), pltpu.VMEM((8, 16, 256), F32), pltpu.VMEM((8, D), F32)]
        + [pltpu.VMEM((GROUP, 128), F32)] * 3
        + grad_scratch(1, 64, 1024, "S0")
        + grad_scratch(1, 64, 1024, "S1")
        + grad_scratch(8, 16, 512, "E0")
        + grad_scratch(8, 16, 512, "E1")
        + grad_scratch(8, 16, HD) * 3
        + grad_scratch(1, 16, D)
        + token_scratch(D)
        + token_scratch(1024) * 2
        + [
            pltpu.VMEM((8, 16, 256), F32),
            pltpu.VMEM((3, 16, 256), F32),
            pltpu.VMEM((4, 16, 256), F32),
            pltpu.VMEM((2, 16, 256), F32),
        ],
        compiler_params=pltpu.CompilerParams(
            collective_id=1, has_side_effects=True, vmem_limit_bytes=64 << 20
        ),
        name="backward",
    )(*args)


def finish_kernel(
    shrink, expand0, expand1, attend, dense, branch, combined, tok, cot, vec, sums,
    layer_out, tokens_grad, g_attend, b_attend, g_dense, b_dense, g_expand, b_expand, g_shrink, b_shrink,
    gain_a, shift_a, gain_f, shift_f,
):
    g_shrink[...] = shrink[...].astype(F32)
    for s in range(8):
        for h, half in enumerate((expand0, expand1)):
            g_expand[:, (2 * s + h) * 512 : (2 * s + h + 1) * 512] = half[:, s * 512 : (s + 1) * 512].astype(F32)
    g_attend[...] = attend[...].astype(F32)
    g_dense[...] = dense[...].astype(F32)
    values = tok[...].astype(F32)
    layer_out[...] = (values + branch[0].astype(F32) + vec[4:5, :] + vec[5:6, :]).astype(BF)
    center = values - jnp.mean(values, axis=1, keepdims=True)
    inv = lax.rsqrt(jnp.mean(center * center, axis=1, keepdims=True) + EPSILON)
    normed = center * inv
    grad = combined[0].astype(F32)
    mean = jnp.mean(grad, axis=1, keepdims=True)
    slant = jnp.mean(grad * normed, axis=1, keepdims=True)
    tokens_grad[...] = cot[...].astype(F32) + (grad - mean - normed * slant) * inv

    @pl.when(pl.program_id(0) == 0)
    def _():
        for ref, first in ((b_attend, 0), (b_expand, 3), (gain_a, 7), (shift_a, 8), (gain_f, 9), (shift_f, 10),
                           (b_dense, 11), (b_shrink, 11)):
            for i in range(ref.shape[0] // 256):
                ref[pl.ds(i * 256, 256)] = sums[first + i : first + i + 1, :].reshape(256)


def finish(*args):
    steps = 2

    def rows(n, width):
        return pl.BlockSpec((n // steps, width), lambda i: (i, 0))

    def part(n, width):
        return pl.BlockSpec((1, n // steps, width), lambda i: (0, i, 0))

    def whole(*dims):
        return pl.BlockSpec(dims, lambda i: (0,) * len(dims))

    weights = [rows(256, 3 * D), rows(256, D), rows(256, 8 * FF_DEV), rows(FF_DEV, D)]
    return pl.pallas_call(
        finish_kernel,
        grid=(steps,),
        out_shape=(
            shape(ROWS, D), shape(ROWS, D, kind=F32),
            shape(256, 3 * D, kind=F32), shape(768, kind=F32), shape(256, D, kind=F32), shape(256, kind=F32),
            shape(256, 8 * FF_DEV, kind=F32), shape(1024, kind=F32), shape(FF_DEV, D, kind=F32),
            *[shape(256, kind=F32)] * 5,
        ),
        in_specs=[weights[3], rows(256, 4096), rows(256, 4096), weights[0], weights[1], part(ROWS, D), part(ROWS, D)]
        + [rows(ROWS, D)] * 2
        + [whole(8, D), whole(16, 256)],
        out_specs=[
            rows(ROWS, D), rows(ROWS, D), weights[0], whole(768), weights[1], whole(256), weights[2],
            whole(1024), weights[3], *[whole(256)] * 5,
        ],
        compiler_params=pltpu.CompilerParams(vmem_limit_bytes=60 << 20),
        name="finish",
    )(*args)


def per_device(
    tokens,
    out_cotangent,
    attend_weight,
    attend_bias,
    dense_weight,
    dense_bias,
    expand_weight,
    expand_bias,
    shrink_weight,
    shrink_bias,
    attend_gain,
    attend_shift,
    feed_gain,
    feed_shift,
    lengths,
    slot_source,
):
    (
        x, we, wa, cot, attend_in, feed_in, slope, q, k, v, prob, mixed, part, shrink, shrink_got,
        stats, vec, cosine, sine,
    ) = forward(
        tokens, out_cotangent, expand_weight, attend_weight, dense_weight, shrink_weight,
        attend_gain, attend_shift, feed_gain, feed_shift, dense_bias, shrink_bias, attend_bias, expand_bias,
        slot_source, lengths,
    )
    we, wa = we.reshape(D, FF_DEV), wa.reshape(D, 3 * HD)
    (shrink_sum, expand0, expand1, attend_sum, dense_sum, branch_sum, own_combined, sums) = backward(
        cot, shrink, shrink_got, slope, feed_in, attend_in, x, q, k, v, prob, mixed, part.reshape(1, GROUP, D),
        we, wa, dense_weight, shrink_weight, vec, stats, cosine, sine,
    )
    return tuple(
        finish(
            shrink_sum, expand0, expand1, attend_sum, dense_sum, branch_sum, own_combined,
            tokens, out_cotangent, vec, sums,
        )
    )


def solution(mesh):
    rows, split, whole = P(("rep", "shard"), None), P("shard"), P("shard", None)
    return jax.shard_map(
        per_device,
        mesh=mesh,
        in_specs=(rows, rows)
        + (whole, split) * 4
        + (split,) * 4
        + (P("rep", None), P("rep", None)),
        out_specs=(rows, rows) + (whole, split) * 4 + (split,) * 4,
        check_vma=False,
    )
```
